256 devices in a mesh: dp: 64 (over z, x, core), proto: 4 (over y).
Axes of the slice: x: 4, y: 4, z: 8, core: 2. Of those that a mesh axis runs over, the one named last changes fastest.
Arguments:
- teacher_feats: bfloat16 [64, 256, 256], P('dp'), may hold values from -32 to 32
- student_feats: bfloat16 [64, 256, 256], P('dp'), may hold values from -48 to 48
- prototypes: bfloat16 [32768, 256], P('proto'), may hold values from -0.45 to 0.45
- patch_mask: int32 [64, 256], P('dp'), may hold values from 0 to 1, as said below
Outputs:
- loss: float32 [], replicated
- student_grad: float32 [64, 256, 256], P('dp')
- proto_grad: float32 [4, 8192, 256], P('proto', 'dp')
The draws below stay inside these ranges and needn't reach their ends.
Inputs may be any that keep to these rules, and one draw needn't show every extreme that they name: `patch_mask`: each image masks between 64 and 128 of its patches; at least one image masks exactly 128.
All inputs are finite; a program needn't handle non-finite values.
Results may differ from the reference program's by a relative error of at most 0.0065.
Values may be sent and summed in bfloat16 or wider, within the bound.
No kernel may reach another device: no remote copies, remote signals or barrier semaphores. Data moves between devices by JAX's collectives and lax.ppermute only.
A program may use at most 128 MiB of HBM per device.

```python
import jax
import jax.numpy as jnp
from jax import lax

K = 256
PROTO = 32768
PATCHES = 256
BALANCING_PASSES = 3
LOSS_SCALE = 16384
IMAGES = 64
N_PROTO = 4


def proto_table(key):
    values = jax.random.normal(jax.random.fold_in(key, 77), (PROTO, K), jnp.float32) * K ** (-0.5)
    return jnp.clip(values, -0.45, 0.45)


def image_ramp(top):
    steps = jnp.arange(IMAGES, dtype=jnp.float32) / (IMAGES - 1)
    return (1.0 + (top - 1.0) * steps)[:, None, None]


def draw_prototypes(key, part):
    return proto_table(key).astype(jnp.bfloat16)


def draw_teacher_feats(key, part):
    key = jax.random.fold_in(key, 11)
    return (jax.random.normal(key, (IMAGES, PATCHES, K), jnp.float32) * 0.2).astype(jnp.bfloat16)


def draw_student_feats(key, part):
    key = jax.random.fold_in(key, 21)
    return (jax.random.normal(key, (IMAGES, PATCHES, K), jnp.float32) * 0.3 * image_ramp(3.0)).astype(jnp.bfloat16)


def draw_patch_mask(key, part):
    key = jax.random.fold_in(key, 5)
    most_masked = PATCHES // 2
    least_masked = PATCHES // 4
    counts = jax.random.randint(jax.random.fold_in(key, 1), (IMAGES,), least_masked, most_masked + 1)
    full_draw = jax.random.randint(jax.random.fold_in(key, 2), (IMAGES,), 0, 4) == 0
    forced_image = jax.random.randint(jax.random.fold_in(key, 4), (), 0, IMAGES)
    full_image = full_draw | (jnp.arange(IMAGES, dtype=jnp.int32) == forced_image)
    counts = jnp.where(full_image, most_masked, counts)
    image_random_keys = jax.random.split(jax.random.fold_in(key, 3), IMAGES)

    def shuffle(sub_key):
        return jax.random.permutation(sub_key, PATCHES)
    ranks = jax.vmap(shuffle)(image_random_keys)
    return (ranks < counts[:, None]).astype(jnp.int32)


def setup_inputs(seed: int = 0) -> dict:
    key_of = jax.random.split(jax.random.key(seed), 5)
    teacher_feats = draw_teacher_feats(jax.random.fold_in(key_of[4], 71), 0)
    student_feats = draw_student_feats(jax.random.fold_in(key_of[4], 71), 0)
    prototypes = draw_prototypes(jax.random.fold_in(key_of[4], 71), 0)
    patch_mask = draw_patch_mask(jax.random.fold_in(key_of[4], 71), 0)
    return {"teacher_feats": teacher_feats, "student_feats": student_feats, "prototypes": prototypes, "patch_mask": patch_mask}


teacher_temp = 0.07
student_temp = 0.1


def reference(teacher_feats, student_feats, prototypes, patch_mask):
    teach_flat = teacher_feats.reshape(-1, K)
    student_flat = student_feats.reshape(-1, K)
    mask_float = patch_mask.astype(jnp.float32)
    count_float = jnp.sum(mask_float, axis=1)
    live_rows = mask_float.reshape(-1)
    weight_rows = (mask_float / count_float[:, None]).reshape(-1)
    teach_logits = jnp.dot(teach_flat, prototypes.T, preferred_element_type=jnp.float32) / teacher_temp
    teach_exp = jnp.exp(teach_logits - jnp.max(teach_logits, axis=1, keepdims=True))
    row_scale = live_rows
    column_scale = jnp.zeros((PROTO,), jnp.float32)
    for balancing_pass_index in range(BALANCING_PASSES):
        column_scale = 1.0 / jnp.dot(row_scale, teach_exp, precision=lax.Precision.HIGHEST)
        row_scale = live_rows / jnp.dot(teach_exp, column_scale, precision=lax.Precision.HIGHEST)
    grad_coef = weight_rows * (LOSS_SCALE / (IMAGES * student_temp))

    def image_block(running, image_index):
        loss_sum, prototype_total = running
        row_start = image_index * PATCHES
        student_block = lax.dynamic_slice_in_dim(student_flat, row_start, PATCHES, 0)
        exp_block = lax.dynamic_slice_in_dim(teach_exp, row_start, PATCHES, 0)
        scale_block = lax.dynamic_slice_in_dim(row_scale, row_start, PATCHES, 0)
        weight_block = lax.dynamic_slice_in_dim(weight_rows, row_start, PATCHES, 0)
        coef_block = lax.dynamic_slice_in_dim(grad_coef, row_start, PATCHES, 0)
        target = exp_block * scale_block[:, None] * column_scale[None, :]
        logits = jnp.dot(student_block, prototypes.T, preferred_element_type=jnp.float32) / student_temp
        row_peak = jnp.max(logits, axis=1, keepdims=True)
        log_prob = logits - (row_peak + jnp.log(jnp.sum(jnp.exp(logits - row_peak), axis=1, keepdims=True)))
        loss_sum = loss_sum - jnp.sum(weight_block * jnp.sum(target * log_prob, axis=1))
        grad_logits = (coef_block[:, None] * (jnp.exp(log_prob) - target)).astype(jnp.bfloat16)
        row_grads = jnp.dot(grad_logits, prototypes, preferred_element_type=jnp.float32)
        prototype_total = prototype_total + jnp.dot(grad_logits.T, student_block, preferred_element_type=jnp.float32)
        return (loss_sum, prototype_total), row_grads

    start_carry = (jnp.zeros((), jnp.float32), jnp.zeros((PROTO, K), jnp.float32))
    (loss_sum, prototype_total), row_grads = lax.scan(image_block, start_carry, jnp.arange(IMAGES, dtype=jnp.int32))
    loss_value = loss_sum / IMAGES
    return loss_value, row_grads, prototype_total.reshape(N_PROTO, PROTO // N_PROTO, K)
```

```python
import functools

import jax
import jax.numpy as jnp
from jax import lax
from jax.experimental import pallas as pl
from jax.experimental.pallas import tpu as pltpu
from jax.sharding import Mesh, PartitionSpec as P

BALANCING_PASSES = 3
LOSS_SCALE = 16384
TEACHER_INV = 1.0 / 0.07
STUDENT_INV = 1.0 / 0.1
IMAGES = 64
LIVE = 128
NT = (((1,), (1,)), ((), ()))
NN = (((1,), (0,)), ((), ()))
TN = (((0,), (0,)), ((), ()))
f32 = jnp.float32
bf16 = jnp.bfloat16


def dot(a, b, dims):
    return lax.dot_general(a, b, dims, preferred_element_type=f32)


def to_lanes(v):
    return jnp.concatenate([v[i : i + 1, :] for i in range(8)], axis=1)


def to_tile(v):
    return jnp.concatenate([v[:, 128 * i : 128 * (i + 1)] for i in range(8)], axis=0)


def split3(v):
    hi = v.astype(bf16).astype(f32)
    mid = (v - hi).astype(bf16).astype(f32)
    lo = (v - hi - mid).astype(bf16).astype(f32)
    return jnp.concatenate([hi, mid, lo, jnp.zeros((13, v.shape[1]), f32)], axis=0).astype(bf16)


def selection(mask):
    patches = mask.shape[1]
    maskf = mask.astype(f32)
    before = lax.broadcasted_iota(jnp.int32, (patches, patches), 0)
    after = lax.broadcasted_iota(jnp.int32, (patches, patches), 1)
    tri = jnp.where(before <= after, 1.0, 0.0).astype(bf16)
    rank = dot(jnp.broadcast_to(maskf, (16, patches)).astype(bf16), tri, NN)[0:1, :]
    slot = lax.broadcasted_iota(jnp.int32, (LIVE, patches), 0).astype(f32)
    hit = jnp.where(rank - 1.0 == slot, 1.0, 0.0) * maskf
    return hit


def pack_kernel(mask_ref, teach_ref, student_ref, out_ref):
    pick = selection(mask_ref[...]).astype(bf16)
    out_ref[0] = dot(pick, teach_ref[...], NN).astype(bf16)
    out_ref[1] = dot(pick, student_ref[...], NN).astype(bf16)


def peak_kernel(mask_ref, rows_ref, proto_ref, out_ref, peak_ref):
    step = pl.program_id(0)
    logits = dot(proto_ref[...], rows_ref[0], NT)
    top = jnp.max(logits, axis=0, keepdims=True)

    @pl.when(step == 0)
    def _():
        peak_ref[...] = top

    @pl.when(step > 0)
    def _():
        peak_ref[...] = jnp.maximum(peak_ref[...], top)

    @pl.when(step == pl.num_programs(0) - 1)
    def _():
        count = jnp.sum(mask_ref[...].astype(f32), axis=1, keepdims=True)
        tile = jnp.concatenate(
            [peak_ref[...] * TEACHER_INV, jnp.broadcast_to(count, (1, LIVE)), jnp.zeros((6, LIVE), f32)], axis=0
        )
        out_ref[...] = jnp.broadcast_to(tile[None], out_ref.shape)


def expo_kernel(me_ref, recv_ref, a_ref, b_ref, c_ref, d_ref, proto_ref, et_ref, srows_ref, stat_ref, pay_ref, trows):
    for k, piece in enumerate((a_ref, b_ref, c_ref, d_ref)):
        start = pl.multiple_of(((me_ref[0] - k) & 3) * 256, 256)
        for core in range(2):
            trows[pl.ds(start + core * 128, 128), :] = piece[core, 0]
            srows_ref[pl.ds(start + core * 128, 128), :] = piece[core, 1]
    peaks, counts = [], []
    for x in range(4):
        for core in range(2):
            at = [(x * 4 + y) * 2 + core for y in range(4)]
            top = recv_ref[at[0], 0:1, :]
            for i in at[1:]:
                top = jnp.maximum(top, recv_ref[i, 0:1, :])
            peaks.append(top)
            counts.append(recv_ref[at[0], 1:2, :])
    peak = jnp.concatenate(peaks, axis=1)
    count = jnp.concatenate(counts, axis=0)
    slot = lax.broadcasted_iota(jnp.int32, (8, 128), 1).astype(f32)
    live = jnp.where(slot < count, 1.0, 0.0)
    stat_ref[0] = live
    stat_ref[1] = live / count
    live_rows = jnp.broadcast_to(to_lanes(live), (16, 1024)).astype(bf16)
    sums = []
    for j in range(8):
        logits = dot(proto_ref[128 * j : 128 * (j + 1), :], trows[...], NT)
        block = jnp.exp(logits * TEACHER_INV - peak).astype(bf16)
        et_ref[128 * j : 128 * (j + 1), :] = block
        sums.append(dot(live_rows, block, NT)[0:1, :])
    tile = jnp.concatenate(sums, axis=0)
    pay_ref[...] = jnp.broadcast_to(tile[None], pay_ref.shape)


def col_kernel(recv_ref, et_ref, *refs):
    extra, (pay_ref, col_ref) = refs[:-2], refs[-2:]
    col = 1.0 / jnp.sum(recv_ref[...], axis=0)
    col_ref[...] = col
    lhs = split3(to_lanes(col))
    out = jnp.sum(dot(lhs, et_ref[...], NN), axis=0, keepdims=True)
    pay_ref[:, 0:8, :] = jnp.broadcast_to(to_tile(out)[None], (pay_ref.shape[0], 8, 128))
    for ref in extra:
        pay_ref[:, 8:, :] = jnp.broadcast_to(ref[...][None], (pay_ref.shape[0],) + ref.shape)


def last_col_kernel(recv_ref, et_ref, w_ref, pay_ref, col_ref):
    col = 1.0 / jnp.sum(recv_ref[...], axis=0)
    col_ref[...] = col
    lhs = split3(to_lanes(col))
    out = jnp.sum(dot(lhs, et_ref[...], NN), axis=0, keepdims=True)
    pay_ref[:, 0:8, :] = jnp.broadcast_to(to_tile(out)[None], (pay_ref.shape[0], 8, 128))
    out = jnp.sum(dot(lhs, w_ref[...], NN), axis=0, keepdims=True)
    pay_ref[:, 8:16, :] = jnp.broadcast_to(to_tile(out)[None], (pay_ref.shape[0], 8, 128))


def row_kernel(recv_ref, stat_ref, et_ref, pay_ref):
    row = stat_ref[0] / jnp.sum(recv_ref[:, 0:8, :], axis=0)
    lhs = split3(to_lanes(row))
    out = jnp.sum(dot(lhs, et_ref[...], NT), axis=0, keepdims=True)
    pay_ref[...] = jnp.broadcast_to(to_tile(out)[None], pay_ref.shape)


def student_sum_kernel(srows_ref, proto_ref, out_ref, logit_ref):
    top = None
    for j in range(8):
        logits = dot(proto_ref[128 * j : 128 * (j + 1), :], srows_ref[...], NT) * STUDENT_INV
        logit_ref[128 * j : 128 * (j + 1), :] = logits
        now = jnp.max(logits, axis=0, keepdims=True)
        top = now if top is None else jnp.maximum(top, now)
    total = jnp.zeros((1, 1024), f32)
    for j in range(8):
        total += jnp.sum(jnp.exp(logit_ref[128 * j : 128 * (j + 1), :] - top), axis=0, keepdims=True)
    out_ref[0:8, :] = to_tile(top)
    out_ref[8:16, :] = to_tile(total)


def student_prob_kernel(recv_ref, srows_ref, proto_ref, et_ref, prob_ref, w_ref):
    tops = recv_ref[:, 8:16, :]
    top = jnp.max(tops, axis=0)
    total = jnp.sum(recv_ref[:, 16:24, :] * jnp.exp(tops - top[None]), axis=0)
    norm = to_lanes(top + jnp.log(total))
    for j in range(8):
        at = slice(128 * j, 128 * (j + 1))
        log_prob = dot(proto_ref[at, :], srows_ref[...], NT) * STUDENT_INV - norm
        prob_ref[at, :] = jnp.exp(log_prob)
        w_ref[at, :] = (et_ref[at, :].astype(f32) * log_prob).astype(bf16)


def grad_kernel(recv_ref, stat_ref, col_ref, et_ref, prob_ref, srows_ref, proto_ref, pout_ref, sout_ref, grad_ref):
    sums = jnp.sum(recv_ref[...], axis=0)
    row = stat_ref[0] / sums[0:8]
    weight = stat_ref[1]
    loss = -jnp.sum(jnp.sum(weight * row * sums[8:16], axis=1, keepdims=True), axis=0, keepdims=True) / IMAGES
    hi = loss.astype(bf16).astype(f32)
    mid = (loss - hi).astype(bf16).astype(f32)
    lo = loss - hi - mid
    which = lax.broadcasted_iota(jnp.int32, (16, 256), 0)
    tail = jnp.where(which == 0, hi, jnp.where(which == 1, mid, jnp.where(which == 2, lo, 0.0))).astype(bf16)
    coef = weight * (LOSS_SCALE / (IMAGES * 0.1))
    coef_rows = to_lanes(coef)
    scale_rows = to_lanes(coef * row)
    for j in range(8):
        at = slice(128 * j, 128 * (j + 1))
        col = jnp.broadcast_to(col_ref[j : j + 1, :], (128, 128)).T
        col = jnp.concatenate([col] * 8, axis=1)
        grad = (prob_ref[at, :] * coef_rows - et_ref[at, :].astype(f32) * col * scale_rows).astype(bf16)
        grad_ref[at, :] = grad
        pout_ref[j, 0:128, :] = dot(grad, srows_ref[...], NN).astype(bf16)
        pout_ref[j, 128:144, :] = tail
    for i in range(8):
        sout_ref[i] = dot(grad_ref[:, 128 * i : 128 * (i + 1)], proto_ref[...], TN).astype(bf16)


def add_kernel(recv_ref, out_ref):
    out_ref[...] = jnp.sum(recv_ref[...].astype(f32), axis=0)


def end_kernel(mask_ref, recv_ref, a_ref, b_ref, c_ref, d_ref, student_ref, proto_ref, loss_ref):
    pick = selection(mask_ref[...]).astype(bf16)
    rows = (a_ref[...] + c_ref[...]) + (b_ref[...] + d_ref[...])
    hi = rows.astype(bf16)
    rest = rows - hi.astype(f32)
    mid = rest.astype(bf16)
    lo = (rest - mid.astype(f32)).astype(bf16)
    student_ref[...] = dot(pick, hi, TN) + dot(pick, mid, TN) + dot(pick, lo, TN)
    total = jnp.sum(recv_ref[...].astype(f32), axis=0)
    proto_ref[...] = total[0:128, :]
    loss_ref[...] = total[128:129, 0:128] + total[129:130, 0:128] + total[130:131, 0:128]


VM = pl.BlockSpec(memory_space=pltpu.VMEM)


def call(kernel, out, *args, scratch=(), limit=32, cost=None):
    out = [jax.ShapeDtypeStruct(s, d) for s, d in out]
    return pl.pallas_call(
        kernel,
        out_shape=out,
        in_specs=[VM] * len(args),
        out_specs=[VM] * len(out),
        scratch_shapes=list(scratch),
        compiler_params=pltpu.CompilerParams(vmem_limit_bytes=limit << 20),
        cost_estimate=cost and pl.CostEstimate(flops=cost, bytes_accessed=1 << 20, transcendentals=1 << 20),
    )(*args)


def a2a(v, axes):
    return lax.all_to_all(v, axes, 0, 0, tiled=True)


def shift(v, axis, n, k):
    return lax.ppermute(v, axis, [(i, (i + k) % n) for i in range(n)])


PLANE = ("x", "y", "c")


def local(teacher_feats, student_feats, prototypes, patch_mask):
    x, c = lax.axis_index("x"), lax.axis_index("c")
    (own,) = call(pack_kernel, [((2, LIVE, 256), bf16)], patch_mask, teacher_feats[0], student_feats[0])
    mine = lax.dynamic_index_in_dim(prototypes.reshape(8, 8, 128, 256), x * 2 + c, 1, keepdims=False)
    mine = mine.reshape(1024, 256)

    other = shift(own, "c", 2, 1)
    pair = jnp.where(c == 0, jnp.stack([own, other]), jnp.stack([other, own]))
    parts = [pair] + [shift(pair, "x", 4, k) for k in (1, 2, 3)]

    peak_pay = pl.pallas_call(
        peak_kernel,
        grid=(8,),
        out_shape=jax.ShapeDtypeStruct((32, 8, 128), f32),
        in_specs=[
            pl.BlockSpec((1, 256), lambda i: (0, 0)),
            pl.BlockSpec((1, LIVE, 256), lambda i: (0, 0, 0)),
            pl.BlockSpec((1024, 256), lambda i: (i, 0)),
        ],
        out_specs=pl.BlockSpec((32, 8, 128), lambda i: (0, 0, 0)),
        scratch_shapes=[pltpu.VMEM((1, LIVE), f32)],
        compiler_params=pltpu.CompilerParams(vmem_limit_bytes=16 << 20),
    )(patch_mask, own, prototypes)
    peak_recv = a2a(peak_pay, PLANE)

    et, srows, stat, pay = pl.pallas_call(
        expo_kernel,
        out_shape=[
            jax.ShapeDtypeStruct((1024, 1024), bf16),
            jax.ShapeDtypeStruct((1024, 256), bf16),
            jax.ShapeDtypeStruct((2, 8, 128), f32),
            jax.ShapeDtypeStruct((8, 8, 128), f32),
        ],
        in_specs=[pl.BlockSpec(memory_space=pltpu.SMEM)] + [VM] * 6,
        out_specs=[VM] * 4,
        scratch_shapes=[pltpu.VMEM((1024, 256), bf16)],
        compiler_params=pltpu.CompilerParams(vmem_limit_bytes=32 << 20),
    )(x.astype(jnp.int32)[None], peak_recv, *parts, mine)

    (student_sum,) = call(
        student_sum_kernel, [((16, 128), f32)], srows, mine,
        scratch=[pltpu.VMEM((1024, 1024), f32)], cost=1 << 29,
    )

    recv = a2a(pay, "z")
    pay, _ = call(col_kernel, [((32, 24, 128), f32), ((8, 128), f32)], recv, et, student_sum)
    recv = a2a(pay, PLANE)
    prob, w = call(
        student_prob_kernel, [((1024, 1024), f32), ((1024, 1024), bf16)], recv, srows, mine, et, cost=1 << 29
    )
    (pay,) = call(row_kernel, [((8, 8, 128), f32)], recv, stat, et)
    for _ in range(BALANCING_PASSES - 2):
        recv = a2a(pay, "z")
        pay, _ = call(col_kernel, [((32, 8, 128), f32), ((8, 128), f32)], recv, et)
        recv = a2a(pay, PLANE)
        (pay,) = call(row_kernel, [((8, 8, 128), f32)], recv, stat, et)
    recv = a2a(pay, "z")
    pay, col = call(last_col_kernel, [((32, 16, 128), f32), ((8, 128), f32)], recv, et, w)
    recv = a2a(pay, PLANE)

    proto_part, student_part = call(
        grad_kernel, [((8, 144, 256), bf16), ((8, 128, 256), bf16)], recv, stat, col, et, prob, srows, mine,
        scratch=[pltpu.VMEM((1024, 1024), bf16)],
    )
    (student_rows,) = call(add_kernel, [((128, 256), f32)], a2a(student_part, ("x", "c")))
    student_rows = [student_rows] + [shift(student_rows, "y", 4, k) for k in (1, 2, 3)]
    proto_recv = a2a(proto_part, "z")
    student, proto, loss = call(
        end_kernel, [((256, 256), f32), ((128, 256), f32), ((1, 128), f32)], patch_mask, proto_recv, *student_rows
    )
    return loss[0, 0], student[None], proto[None]


def solution(mesh):
    fine = Mesh(mesh.devices.reshape(8, 4, 2, 4), ("z", "x", "c", "y"))
    dp = ("z", "x", "c")
    return jax.shard_map(
        local,
        mesh=fine,
        in_specs=(P(dp, None, None), P(dp, None, None), P("y", None), P(dp, None)),
        out_specs=(P(), P(dp, None, None), P("y", dp, None)),
        check_vma=False,
    )
```

```python
import jax
import jax.numpy as jnp
from jax import lax
from jax.experimental import pallas as pl
from jax.experimental.pallas import tpu as pltpu
from jax.sharding import Mesh, PartitionSpec as P

BALANCING_PASSES = 3
LOSS_SCALE = 16384
TEACHER_INV = 1.0 / 0.07
STUDENT_INV = 1.0 / 0.1
IMAGES = 64
LIVE = 128
NT = (((1,), (1,)), ((), ()))
NN = (((1,), (0,)), ((), ()))
TN = (((0,), (0,)), ((), ()))
f32 = jnp.float32
bf16 = jnp.bfloat16


def dot(a, b, dims):
    return lax.dot_general(a, b, dims, preferred_element_type=f32)


def to_lanes(v):
    return jnp.concatenate([v[i : i + 1, :] for i in range(8)], axis=1)


def to_tile(v):
    return jnp.concatenate([v[:, 128 * i : 128 * (i + 1)] for i in range(8)], axis=0)


def split3(v):
    hi = v.astype(bf16).astype(f32)
    mid = (v - hi).astype(bf16).astype(f32)
    lo = (v - hi - mid).astype(bf16).astype(f32)
    return jnp.concatenate([hi, mid, lo, jnp.zeros((13, v.shape[1]), f32)], axis=0).astype(bf16)


def selection(mask):
    patches = mask.shape[1]
    maskf = mask.astype(f32)
    before = lax.broadcasted_iota(jnp.int32, (patches, patches), 0)
    after = lax.broadcasted_iota(jnp.int32, (patches, patches), 1)
    tri = jnp.where(before <= after, 1.0, 0.0).astype(bf16)
    rank = dot(jnp.broadcast_to(maskf, (16, patches)).astype(bf16), tri, NN)[0:1, :]
    slot = lax.broadcasted_iota(jnp.int32, (LIVE, patches), 0).astype(f32)
    hit = jnp.where(rank - 1.0 == slot, 1.0, 0.0) * maskf
    return hit


def pack_kernel(mask_hbm, teach_hbm, student_hbm, out_ref, mask_ref, teach_ref, student_ref, sems):
    copies = [
        pltpu.make_async_copy(src, dst, sems.at[i])
        for i, (src, dst) in enumerate(((mask_hbm, mask_ref), (teach_hbm, teach_ref), (student_hbm, student_ref)))
    ]
    for copy in copies:
        copy.start()
    copies[0].wait()
    pick = selection(mask_ref[...]).astype(bf16)
    copies[1].wait()
    out_ref[0] = dot(pick, teach_ref[0], NN).astype(bf16)
    copies[2].wait()
    out_ref[1] = dot(pick, student_ref[0], NN).astype(bf16)


def peak_kernel(mask_hbm, rows_hbm, proto_hbm, out_ref, mine_ref, mask_ref, rows_ref, proto_ref, sems):
    chunks = 8
    tall = proto_ref.shape[0] // chunks
    first = [
        pltpu.make_async_copy(rows_hbm.at[0], rows_ref, sems.at[chunks]),
        pltpu.make_async_copy(mask_hbm, mask_ref, sems.at[chunks + 1]),
    ]
    copies = [
        pltpu.make_async_copy(proto_hbm.at[pl.ds(i * tall, tall)], proto_ref.at[pl.ds(i * tall, tall)], sems.at[i])
        for i in range(chunks)
    ]
    for copy in first + copies:
        copy.start()
    for copy in first:
        copy.wait()
    image = lax.axis_index("x") * 2 + lax.axis_index("c")
    count = jnp.sum(mask_ref[...].astype(f32), axis=1, keepdims=True)
    peak = None
    for i in range(chunks):
        copies[i].wait()
        mine_ref[128 * i : 128 * (i + 1), :] = proto_ref[pl.ds(pl.multiple_of(i * tall + image * 128, 128), 128), :]
        logits = dot(proto_ref[i * tall : (i + 1) * tall, :], rows_ref[...], NT)
        top = jnp.max(logits, axis=0, keepdims=True)
        peak = top if peak is None else jnp.maximum(peak, top)
    tile = jnp.concatenate([peak * TEACHER_INV, jnp.broadcast_to(count, (1, LIVE)), jnp.zeros((6, LIVE), f32)], axis=0)
    out_ref[...] = jnp.broadcast_to(tile[None], out_ref.shape)


def expo_kernel(recv_ref, a_hbm, b_hbm, c_hbm, d_hbm, mine_ref, et_ref, srows_ref, stat_ref, pay_ref, trows, sems):
    x = lax.axis_index("x")
    tcopies, scopies = [], []
    for k, piece in enumerate((a_hbm, b_hbm, c_hbm, d_hbm)):
        start = pl.multiple_of(((x + 4 - k) & 3) * 256, 256)
        for core in range(2):
            at = pl.ds(start + core * 128, 128)
            tcopies.append(pltpu.make_async_copy(piece.at[core, 0], trows.at[at], sems.at[k * 4 + core]))
            scopies.append(pltpu.make_async_copy(piece.at[core, 1], srows_ref.at[at], sems.at[k * 4 + 2 + core]))
    for copy in tcopies + scopies:
        copy.start()
    peaks, counts = [], []
    for x in range(4):
        for core in range(2):
            at = [(x * 4 + y) * 2 + core for y in range(4)]
            top = recv_ref[at[0], 0:1, :]
            for i in at[1:]:
                top = jnp.maximum(top, recv_ref[i, 0:1, :])
            peaks.append(top)
            counts.append(recv_ref[at[0], 1:2, :])
    peak = jnp.concatenate(peaks, axis=1)
    count = jnp.concatenate(counts, axis=0)
    slot = lax.broadcasted_iota(jnp.int32, (8, 128), 1).astype(f32)
    live = jnp.where(slot < count, 1.0, 0.0)
    stat_ref[0] = live
    stat_ref[1] = live / count
    stat_ref[2] = jnp.concatenate(peaks, axis=0)
    live_rows = jnp.broadcast_to(to_lanes(live), (16, 1024)).astype(bf16)
    sums = []
    for copy in tcopies:
        copy.wait()
    for j in range(8):
        logits = dot(mine_ref[128 * j : 128 * (j + 1), :], trows[...], NT)
        block = jnp.exp(logits * TEACHER_INV - peak).astype(bf16)
        et_ref[128 * j : 128 * (j + 1), :] = block
        sums.append(dot(live_rows, block, NT)[0:1, :])
    tile = jnp.concatenate(sums, axis=0)
    pay_ref[...] = jnp.broadcast_to(tile[None], pay_ref.shape)
    for copy in scopies:
        copy.wait()


def col_kernel(recv_ref, et_ref, *refs):
    extra, (pay_ref, col_ref) = refs[:-2], refs[-2:]
    col = 1.0 / jnp.sum(recv_ref[...], axis=0)
    col_ref[...] = col
    lhs = split3(to_lanes(col))
    out = jnp.sum(dot(lhs, et_ref[...], NN), axis=0, keepdims=True)
    pay_ref[:, 0:8, :] = jnp.broadcast_to(to_tile(out)[None], (pay_ref.shape[0], 8, 128))
    for ref in extra:
        pay_ref[:, 8:, :] = jnp.broadcast_to(ref[...][None], (pay_ref.shape[0],) + ref.shape)


def last_col_kernel(recv_ref, et_ref, w_ref, pay_ref, col_ref):
    col = 1.0 / jnp.sum(recv_ref[...], axis=0)
    col_ref[...] = col
    lhs = split3(to_lanes(col))
    out = jnp.sum(dot(lhs, et_ref[...], NN), axis=0, keepdims=True)
    pay_ref[:, 0:8, :] = jnp.broadcast_to(to_tile(out)[None], (pay_ref.shape[0], 8, 128))
    out = jnp.sum(dot(lhs, w_ref[...], NN), axis=0, keepdims=True)
    pay_ref[:, 8:16, :] = jnp.broadcast_to(to_tile(out)[None], (pay_ref.shape[0], 8, 128))
    pay_ref[:, 16:24, :] = jnp.broadcast_to(col[None], (pay_ref.shape[0], 8, 128))


def row_kernel(recv_ref, stat_ref, et_ref, pay_ref):
    row = stat_ref[0] / jnp.sum(recv_ref[:, 0:8, :], axis=0)
    lhs = split3(to_lanes(row))
    out = jnp.sum(dot(lhs, et_ref[...], NT), axis=0, keepdims=True)
    pay_ref[...] = jnp.broadcast_to(to_tile(out)[None], pay_ref.shape)


def student_sum_kernel(srows_ref, proto_ref, out_ref, logit_ref):
    top = None
    for j in range(8):
        logits = dot(proto_ref[128 * j : 128 * (j + 1), :], srows_ref[...], NT) * STUDENT_INV
        logit_ref[128 * j : 128 * (j + 1), :] = logits
        now = jnp.max(logits, axis=0, keepdims=True)
        top = now if top is None else jnp.maximum(top, now)
    total = jnp.zeros((1, 1024), f32)
    for j in range(8):
        total += jnp.sum(jnp.exp(logit_ref[128 * j : 128 * (j + 1), :] - top), axis=0, keepdims=True)
    out_ref[0:8, :] = to_tile(top)
    out_ref[8:16, :] = to_tile(total)


def student_prob_kernel(recv_ref, srows_ref, proto_ref, et_ref, prob_ref, w_ref, norm_ref):
    tops = recv_ref[:, 8:16, :]
    top = jnp.max(tops, axis=0)
    total = jnp.sum(recv_ref[:, 16:24, :] * jnp.exp(tops - top[None]), axis=0)
    norm_ref[...] = top + jnp.log(total)
    norm = to_lanes(norm_ref[...])
    for j in range(8):
        at = slice(128 * j, 128 * (j + 1))
        log_prob = dot(proto_ref[at, :], srows_ref[...], NT) * STUDENT_INV - norm
        prob_ref[at, :] = jnp.exp(log_prob)
        w_ref[at, :] = (et_ref[at, :].astype(f32) * log_prob).astype(bf16)


def grad_kernel(recv_ref, stat_ref, col_ref, et_ref, prob_ref, srows_ref, pout_ref, scale_ref):
    sums = jnp.sum(recv_ref[:, 0:16, :], axis=0)
    row = stat_ref[0] / sums[0:8]
    weight = stat_ref[1]
    loss = -jnp.sum(jnp.sum(weight * row * sums[8:16], axis=1, keepdims=True), axis=0, keepdims=True) / IMAGES
    hi = loss.astype(bf16).astype(f32)
    mid = (loss - hi).astype(bf16).astype(f32)
    lo = loss - hi - mid
    which = lax.broadcasted_iota(jnp.int32, (16, 256), 0)
    tail = jnp.where(which == 0, hi, jnp.where(which == 1, mid, jnp.where(which == 2, lo, 0.0))).astype(bf16)
    coef = weight * (LOSS_SCALE / (IMAGES * 0.1))
    scale_ref[0] = coef
    scale_ref[1] = coef * row
    coef_rows = to_lanes(coef)
    scale_rows = to_lanes(coef * row)
    for j in range(8):
        at = slice(128 * j, 128 * (j + 1))
        col = jnp.broadcast_to(col_ref[j : j + 1, :], (128, 128)).T
        col = jnp.concatenate([col] * 8, axis=1)
        grad = (prob_ref[at, :] * coef_rows - et_ref[at, :].astype(f32) * col * scale_rows).astype(bf16)
        pout_ref[j, 0:128, :] = dot(grad, srows_ref[...], NN).astype(bf16)
        pout_ref[j, 128:144, :] = tail


def own_kernel(recv_ref, scale_ref, stat_ref, norm_ref, rows_ref, proto_ref, out_ref):
    step = pl.program_id(0)
    y = lax.axis_index("y")
    image = lax.axis_index("x") * 2 + lax.axis_index("c")

    def column(row):
        return jnp.concatenate([jnp.broadcast_to(row, (LIVE, 128)).T] * 8, axis=1)

    peak = column(stat_ref[2, pl.ds(image, 1), :])
    norm = column(norm_ref[pl.ds(image, 1), :])
    coef = column(scale_ref[0, pl.ds(image, 1), :])
    scale = column(scale_ref[1, pl.ds(image, 1), :])
    col = jnp.concatenate(
        [recv_ref[(x * 4 + y) * 2 + c, pl.ds(16 + step, 1), :] for x in range(4) for c in range(2)], axis=1
    )
    logits = dot(rows_ref[...].reshape(2 * LIVE, 256), proto_ref[...], NT)
    teach = jnp.exp(logits[0:LIVE] * TEACHER_INV - peak).astype(bf16).astype(f32)
    prob = jnp.exp(logits[LIVE:] * STUDENT_INV - norm)
    grad = (prob * coef - teach * col * scale).astype(bf16)
    part = dot(grad, proto_ref[...], NN)

    @pl.when(step == 0)
    def _():
        out_ref[...] = part

    @pl.when(step > 0)
    def _():
        out_ref[...] += part


def end_kernel(mask_ref, recv_ref, a_ref, b_ref, c_ref, d_ref, student_ref, proto_ref, loss_ref):
    pick = selection(mask_ref[...]).astype(bf16)
    rows = (a_ref[...] + c_ref[...]) + (b_ref[...] + d_ref[...])
    hi = rows.astype(bf16)
    rest = rows - hi.astype(f32)
    mid = rest.astype(bf16)
    lo = (rest - mid.astype(f32)).astype(bf16)
    student_ref[...] = dot(pick, hi, TN) + dot(pick, mid, TN) + dot(pick, lo, TN)
    total = jnp.sum(recv_ref[...].astype(f32), axis=0)
    proto_ref[...] = total[0:128, :]
    loss_ref[...] = total[128:129, 0:128] + total[129:130, 0:128] + total[130:131, 0:128]


VM = pl.BlockSpec(memory_space=pltpu.VMEM)


def call(kernel, out, *args, scratch=(), limit=8, cost=None):
    out = [jax.ShapeDtypeStruct(s, d) for s, d in out]
    return pl.pallas_call(
        kernel,
        out_shape=out,
        in_specs=[VM] * len(args),
        out_specs=[VM] * len(out),
        scratch_shapes=list(scratch),
        compiler_params=pltpu.CompilerParams(vmem_limit_bytes=limit << 20),
        cost_estimate=cost and pl.CostEstimate(flops=cost, bytes_accessed=1 << 20, transcendentals=1 << 20),
    )(*args)


def a2a(v, axes):
    return lax.all_to_all(v, axes, 0, 0, tiled=True)


def shift(v, axis, n, k):
    return lax.ppermute(v, axis, [(i, (i + k) % n) for i in range(n)])


PLANE = ("x", "y", "c")
HBM = pl.BlockSpec(memory_space=pl.ANY)


def local(teacher_feats, student_feats, prototypes, patch_mask):
    c = lax.axis_index("c")
    own = pl.pallas_call(
        pack_kernel,
        out_shape=jax.ShapeDtypeStruct((2, LIVE, 256), bf16),
        in_specs=[HBM] * 3,
        out_specs=VM,
        scratch_shapes=[
            pltpu.VMEM((1, 256), jnp.int32),
            pltpu.VMEM((1, 256, 256), bf16),
            pltpu.VMEM((1, 256, 256), bf16),
            pltpu.SemaphoreType.DMA((3,)),
        ],
        compiler_params=pltpu.CompilerParams(vmem_limit_bytes=60 << 20),
    )(patch_mask, teacher_feats, student_feats)

    other = shift(own, "c", 2, 1)
    pair = jnp.where(c == 0, jnp.stack([own, other]), jnp.stack([other, own]))
    parts = [pair] + [shift(pair, "x", 4, k) for k in (1, 2, 3)]

    peak_pay, mine = pl.pallas_call(
        peak_kernel,
        out_shape=[jax.ShapeDtypeStruct((32, 8, 128), f32), jax.ShapeDtypeStruct((1024, 256), bf16)],
        in_specs=[HBM] * 3,
        out_specs=[VM] * 2,
        scratch_shapes=[
            pltpu.VMEM((1, 256), jnp.int32),
            pltpu.VMEM((LIVE, 256), bf16),
            pltpu.VMEM((8192, 256), bf16),
            pltpu.SemaphoreType.DMA((10,)),
        ],
        compiler_params=pltpu.CompilerParams(vmem_limit_bytes=60 << 20),
    )(patch_mask, own, prototypes)
    peak_recv = a2a(peak_pay, PLANE)

    et, srows, stat, pay = pl.pallas_call(
        expo_kernel,
        out_shape=[
            jax.ShapeDtypeStruct((1024, 1024), bf16),
            jax.ShapeDtypeStruct((1024, 256), bf16),
            jax.ShapeDtypeStruct((3, 8, 128), f32),
            jax.ShapeDtypeStruct((8, 8, 128), f32),
        ],
        in_specs=[VM] + [HBM] * 4 + [VM],
        out_specs=[VM] * 4,
        scratch_shapes=[pltpu.VMEM((1024, 256), bf16), pltpu.SemaphoreType.DMA((16,))],
        compiler_params=pltpu.CompilerParams(vmem_limit_bytes=16 << 20),
    )(peak_recv, *parts, mine)

    (student_sum,) = call(
        student_sum_kernel, [((16, 128), f32)], srows, mine,
        scratch=[pltpu.VMEM((1024, 1024), f32)], cost=1 << 29, limit=16,
    )

    recv = a2a(pay, "z")
    pay, _ = call(col_kernel, [((32, 24, 128), f32), ((8, 128), f32)], recv, et, student_sum)
    recv = a2a(pay, PLANE)
    prob, w, norm = call(
        student_prob_kernel, [((1024, 1024), f32), ((1024, 1024), bf16), ((8, 128), f32)], recv, srows, mine, et,
        cost=1 << 29, limit=24,
    )
    (pay,) = call(row_kernel, [((8, 8, 128), f32)], recv, stat, et)
    for _ in range(BALANCING_PASSES - 2):
        recv = a2a(pay, "z")
        pay, _ = call(col_kernel, [((32, 8, 128), f32), ((8, 128), f32)], recv, et)
        recv = a2a(pay, PLANE)
        (pay,) = call(row_kernel, [((8, 8, 128), f32)], recv, stat, et)
    recv = a2a(pay, "z")
    pay, col = call(last_col_kernel, [((32, 24, 128), f32), ((8, 128), f32)], recv, et, w)
    recv = a2a(pay, PLANE)

    proto_part, scale = call(
        grad_kernel, [((8, 144, 256), bf16), ((2, 8, 128), f32)], recv, stat, col, et, prob, srows, limit=24
    )
    proto_recv = a2a(proto_part, "z")
    student_rows = pl.pallas_call(
        own_kernel,
        grid=(8,),
        out_shape=jax.ShapeDtypeStruct((LIVE, 256), f32),
        in_specs=[
            pl.BlockSpec((32, 24, 128), lambda i: (0, 0, 0)),
            pl.BlockSpec((2, 8, 128), lambda i: (0, 0, 0)),
            pl.BlockSpec((3, 8, 128), lambda i: (0, 0, 0)),
            pl.BlockSpec((8, 128), lambda i: (0, 0)),
            pl.BlockSpec((2, LIVE, 256), lambda i: (0, 0, 0)),
            pl.BlockSpec((1024, 256), lambda i: (i, 0)),
        ],
        out_specs=pl.BlockSpec((LIVE, 256), lambda i: (0, 0)),
        compiler_params=pltpu.CompilerParams(vmem_limit_bytes=24 << 20),
        cost_estimate=pl.CostEstimate(flops=1 << 31, bytes_accessed=4 << 20, transcendentals=2 << 20),
    )(recv, scale, stat, norm, own, prototypes)
    student_rows = [student_rows] + [shift(student_rows, "y", 4, k) for k in (1, 2, 3)]
    student, proto, loss = call(
        end_kernel, [((256, 256), f32), ((128, 256), f32), ((1, 128), f32)], patch_mask, proto_recv, *student_rows,
        limit=16,
    )
    return loss[0, 0], student[None], proto[None]


def solution(mesh):
    fine = Mesh(mesh.devices.reshape(8, 4, 2, 4), ("z", "x", "c", "y"))
    dp = ("z", "x", "c")
    return jax.shard_map(
        local,
        mesh=fine,
        in_specs=(P(dp, None, None), P(dp, None, None), P("y", None), P(dp, None)),
        out_specs=(P(), P(dp, None, None), P("y", dp, None)),
        check_vma=False,
    )
```

```python
import jax
import jax.numpy as jnp
from jax import lax
from jax.experimental import pallas as pl
from jax.experimental.pallas import tpu as pltpu
from jax.sharding import Mesh, PartitionSpec as P

BALANCING_PASSES = 3
LOSS_SCALE = 16384
TEACHER_INV = 1.0 / 0.07
STUDENT_INV = 1.0 / 0.1
IMAGES = 64
LIVE = 128
NT = (((1,), (1,)), ((), ()))
NN = (((1,), (0,)), ((), ()))
TN = (((0,), (0,)), ((), ()))
f32 = jnp.float32
bf16 = jnp.bfloat16


def dot(a, b, dims):
    return lax.dot_general(a, b, dims, preferred_element_type=f32)


def to_lanes(v):
    return jnp.concatenate([v[i : i + 1, :] for i in range(8)], axis=1)


def to_tile(v):
    return jnp.concatenate([v[:, 128 * i : 128 * (i + 1)] for i in range(8)], axis=0)


def split3(v):
    hi = v.astype(bf16).astype(f32)
    mid = (v - hi).astype(bf16).astype(f32)
    lo = (v - hi - mid).astype(bf16).astype(f32)
    return jnp.concatenate([hi, mid, lo, jnp.zeros((13, v.shape[1]), f32)], axis=0).astype(bf16)


def selection(mask):
    patches = mask.shape[1]
    maskf = mask.astype(f32)
    before = lax.broadcasted_iota(jnp.int32, (patches, patches), 0)
    after = lax.broadcasted_iota(jnp.int32, (patches, patches), 1)
    tri = jnp.where(before <= after, 1.0, 0.0).astype(bf16)
    rank = dot(jnp.broadcast_to(maskf, (16, patches)).astype(bf16), tri, NN)[0:1, :]
    slot = lax.broadcasted_iota(jnp.int32, (LIVE, patches), 0).astype(f32)
    hit = jnp.where(rank - 1.0 == slot, 1.0, 0.0) * maskf
    return hit


def head_kernel(
    mask_hbm, teach_hbm, student_hbm, proto_hbm, own_ref, out_ref, mine_ref, mask_ref, teach_ref, student_ref, proto_ref, sems
):
    chunks = 8
    tall = proto_ref.shape[0] // chunks
    small = ((mask_hbm, mask_ref), (teach_hbm, teach_ref), (student_hbm, student_ref))
    first = [pltpu.make_async_copy(src, dst, sems.at[chunks + i]) for i, (src, dst) in enumerate(small)]
    copies = [
        pltpu.make_async_copy(proto_hbm.at[pl.ds(i * tall, tall)], proto_ref.at[pl.ds(i * tall, tall)], sems.at[i])
        for i in range(chunks)
    ]
    for copy in first + copies:
        copy.start()
    image = lax.axis_index("x") * 2 + lax.axis_index("c")
    first[0].wait()
    pick = selection(mask_ref[...]).astype(bf16)
    count = jnp.sum(mask_ref[...].astype(f32), axis=1, keepdims=True)
    first[1].wait()
    own_ref[0] = dot(pick, teach_ref[0], NN).astype(bf16)
    first[2].wait()
    own_ref[1] = dot(pick, student_ref[0], NN).astype(bf16)
    rows = own_ref[0]
    peak = None
    for i in range(chunks):
        copies[i].wait()
        mine_ref[128 * i : 128 * (i + 1), :] = proto_ref[pl.ds(pl.multiple_of(i * tall + image * 128, 128), 128), :]
        logits = dot(proto_ref[i * tall : (i + 1) * tall, :], rows, NT)
        top = jnp.max(logits, axis=0, keepdims=True)
        peak = top if peak is None else jnp.maximum(peak, top)
    tile = jnp.concatenate([peak * TEACHER_INV, jnp.broadcast_to(count, (1, LIVE)), jnp.zeros((6, LIVE), f32)], axis=0)
    out_ref[...] = jnp.broadcast_to(tile[None], out_ref.shape)


def expo_kernel(recv_ref, a_hbm, b_hbm, c_hbm, d_hbm, mine_ref, et_ref, srows_ref, stat_ref, pay_ref, trows, sems):
    x = lax.axis_index("x")
    tcopies, scopies = [], []
    for k, piece in enumerate((a_hbm, b_hbm, c_hbm, d_hbm)):
        start = pl.multiple_of(((x + 4 - k) & 3) * 256, 256)
        for core in range(2):
            at = pl.ds(start + core * 128, 128)
            tcopies.append(pltpu.make_async_copy(piece.at[core, 0], trows.at[at], sems.at[k * 4 + core]))
            scopies.append(pltpu.make_async_copy(piece.at[core, 1], srows_ref.at[at], sems.at[k * 4 + 2 + core]))
    for copy in tcopies + scopies:
        copy.start()
    peaks, counts = [], []
    for x in range(4):
        for core in range(2):
            at = [(x * 4 + y) * 2 + core for y in range(4)]
            top = recv_ref[at[0], 0:1, :]
            for i in at[1:]:
                top = jnp.maximum(top, recv_ref[i, 0:1, :])
            peaks.append(top)
            counts.append(recv_ref[at[0], 1:2, :])
    peak = jnp.concatenate(peaks, axis=1)
    count = jnp.concatenate(counts, axis=0)
    slot = lax.broadcasted_iota(jnp.int32, (8, 128), 1).astype(f32)
    live = jnp.where(slot < count, 1.0, 0.0)
    stat_ref[0] = live
    stat_ref[1] = live / count
    stat_ref[2] = jnp.concatenate(peaks, axis=0)
    live_rows = jnp.broadcast_to(to_lanes(live), (16, 1024)).astype(bf16)
    total = jnp.zeros((16, 1024), f32)
    for copy in tcopies:
        copy.wait()
    for r in range(4):
        at = slice(256 * r, 256 * (r + 1))
        logits = dot(mine_ref[...], trows[at, :], NT)
        block = jnp.exp(logits * TEACHER_INV - peak[:, at]).astype(bf16)
        et_ref[:, at] = block
        total += dot(live_rows[:, at], block, NT)
    pay_ref[...] = jnp.broadcast_to(to_tile(total[0:1])[None], pay_ref.shape)
    for copy in scopies:
        copy.wait()


def col_kernel(recv_ref, et_ref, extra_ref, pay_ref):
    col = 1.0 / jnp.sum(recv_ref[...], axis=0)
    out = jnp.sum(dot(split3(to_lanes(col)), et_ref[...], NN), axis=0, keepdims=True)
    pay_ref[:, 0:8, :] = jnp.broadcast_to(to_tile(out)[None], (pay_ref.shape[0], 8, 128))
    if pay_ref.shape[1] > 8:
        pay_ref[:, 8:, :] = jnp.broadcast_to(extra_ref[...][None], (pay_ref.shape[0], 8, 128))


def last_col_kernel(recv_ref, et_ref, w_ref, pay_ref, col_ref):
    col = 1.0 / jnp.sum(recv_ref[...], axis=0)
    col_ref[...] = col
    lhs = split3(to_lanes(col))
    out = to_tile(jnp.sum(dot(lhs, et_ref[...], NN), axis=0, keepdims=True))
    hi = out.astype(bf16).astype(f32)
    sums = jnp.concatenate([hi, out - hi], axis=0).astype(bf16)
    out = to_tile(jnp.sum(dot(lhs, w_ref[...], NN), axis=0, keepdims=True))
    rest = jnp.concatenate([out, col], axis=0).astype(bf16)
    pay_ref[:, 0:16, :] = jnp.broadcast_to(sums[None], (pay_ref.shape[0], 16, 128))
    pay_ref[:, 16:32, :] = jnp.broadcast_to(rest[None], (pay_ref.shape[0], 16, 128))


def row_kernel(recv_ref, stat_ref, et_ref, pay_ref):
    row = stat_ref[0] / jnp.sum(recv_ref[:, 0:8, :], axis=0)
    lhs = split3(to_lanes(row))
    out = jnp.sum(dot(lhs, et_ref[...], NT), axis=0, keepdims=True)
    pay_ref[...] = jnp.broadcast_to(to_tile(out)[None], pay_ref.shape)


def student_sum_kernel(srows_ref, mine_ref, out_ref):
    parts = []
    for r in range(4):
        logits = dot(mine_ref[...], srows_ref[256 * r : 256 * (r + 1), :], NT) * STUDENT_INV
        top = jnp.max(logits, axis=0, keepdims=True)
        parts.append(top + jnp.log(jnp.sum(jnp.exp(logits - top), axis=0, keepdims=True)))
    out_ref[...] = to_tile(jnp.concatenate(parts, axis=1))


def student_prob_kernel(recv_ref, srows_ref, mine_ref, et_ref, prob_hbm, w_hbm, norm_ref, prob_ref, w_ref, sems):
    parts = recv_ref[:, 8:16, :]
    top = jnp.max(parts, axis=0)
    norm_ref[...] = top + jnp.log(jnp.sum(jnp.exp(parts - top[None]), axis=0))
    norm = to_lanes(norm_ref[...])
    copies = []
    for r in range(4):
        at = slice(256 * r, 256 * (r + 1))
        log_prob = dot(mine_ref[...], srows_ref[at, :], NT) * STUDENT_INV - norm[:, at]
        prob_ref[:, at] = jnp.exp(log_prob)
        w_ref[:, at] = (et_ref[:, at].astype(f32) * log_prob).astype(bf16)
        at = (pl.ds(0, 1024), pl.ds(256 * r, 256))
        copies.append(pltpu.make_async_copy(prob_ref.at[at], prob_hbm.at[at], sems.at[r]))
        copies.append(pltpu.make_async_copy(w_ref.at[at], w_hbm.at[at], sems.at[4 + r]))
        copies[-2].start()
        copies[-1].start()
    for copy in copies:
        copy.wait()


def grad_kernel(recv_ref, stat_ref, col_ref, et_ref, prob_ref, srows_ref, pout_ref, scale_ref):
    sums = jnp.sum(recv_ref[:, 0:16, :].astype(f32), axis=0)
    entropy = jnp.sum(recv_ref[:, 16:32, :].astype(f32), axis=0)[0:8]
    row = stat_ref[0] / (sums[0:8] + sums[8:16])
    weight = stat_ref[1]
    loss = -jnp.sum(jnp.sum(weight * row * entropy, axis=1, keepdims=True), axis=0, keepdims=True) / IMAGES
    hi = loss.astype(bf16).astype(f32)
    mid = (loss - hi).astype(bf16).astype(f32)
    lo = loss - hi - mid
    which = lax.broadcasted_iota(jnp.int32, (16, 256), 0)
    tail = jnp.where(which == 0, hi, jnp.where(which == 1, mid, jnp.where(which == 2, lo, 0.0))).astype(bf16)
    coef = weight * (LOSS_SCALE / (IMAGES * 0.1))
    scale_ref[0] = coef
    scale_ref[1] = coef * row
    coef_rows = to_lanes(coef)
    scale_rows = to_lanes(coef * row)
    for j in range(4):
        at = slice(256 * j, 256 * (j + 1))
        col = jnp.concatenate([jnp.broadcast_to(col_ref[i : i + 1, :], (128, 128)).T for i in (2 * j, 2 * j + 1)], axis=0)
        col = jnp.concatenate([col] * 8, axis=1)
        grad = (prob_ref[at, :] * coef_rows - et_ref[at, :].astype(f32) * col * scale_rows).astype(bf16)
        part = dot(grad, srows_ref[...], NN).astype(bf16)
        for i in (0, 1):
            pout_ref[2 * j + i, 0:128, :] = part[128 * i : 128 * (i + 1)]
            pout_ref[2 * j + i, 128:144, :] = tail


def own_kernel(recv_ref, scale_ref, stat_ref, norm_ref, rows_hbm, proto_hbm, out_ref, rows_ref, proto_ref, sems):
    chunks = 8
    tall = proto_ref.shape[0] // chunks
    rows_copy = pltpu.make_async_copy(rows_hbm, rows_ref, sems.at[chunks])
    copies = [
        pltpu.make_async_copy(proto_hbm.at[pl.ds(i * tall, tall)], proto_ref.at[pl.ds(i * tall, tall)], sems.at[i])
        for i in range(chunks)
    ]
    for copy in [rows_copy] + copies:
        copy.start()
    y = lax.axis_index("y")
    image = lax.axis_index("x") * 2 + lax.axis_index("c")

    def column(row):
        return jnp.concatenate([jnp.broadcast_to(row, (LIVE, 128)).T] * 8, axis=1)

    peak = column(stat_ref[2, pl.ds(image, 1), :])
    norm = column(norm_ref[pl.ds(image, 1), :])
    coef = column(scale_ref[0, pl.ds(image, 1), :])
    scale = column(scale_ref[1, pl.ds(image, 1), :])
    cols = [recv_ref[(x * 4 + y) * 2 + c, 16:32, :].astype(f32) for x in range(4) for c in range(2)]
    rows_copy.wait()
    rows = rows_ref[...].reshape(2 * LIVE, 256)
    total = jnp.zeros((LIVE, 256), f32)
    for i in range(chunks):
        col = jnp.concatenate([v[8 + i : 9 + i, :] for v in cols], axis=1)
        copies[i].wait()
        block = proto_ref[i * tall : (i + 1) * tall, :]
        logits = dot(rows, block, NT)
        teach = jnp.exp(logits[0:LIVE] * TEACHER_INV - peak).astype(bf16).astype(f32)
        prob = jnp.exp(logits[LIVE:] * STUDENT_INV - norm)
        grad = (prob * coef - teach * (col * scale)).astype(bf16)
        total += dot(grad, block, NN)
    out_ref[...] = total


def end_kernel(mask_ref, recv_ref, a_ref, b_ref, c_ref, d_ref, student_ref, proto_ref, loss_ref):
    pick = selection(mask_ref[...]).astype(bf16)
    rows = (a_ref[...] + c_ref[...]) + (b_ref[...] + d_ref[...])
    hi = rows.astype(bf16)
    rest = rows - hi.astype(f32)
    mid = rest.astype(bf16)
    lo = (rest - mid.astype(f32)).astype(bf16)
    student_ref[...] = dot(pick, hi, TN) + dot(pick, mid, TN) + dot(pick, lo, TN)
    total = jnp.sum(recv_ref[...].astype(f32), axis=0)
    proto_ref[...] = total[0:128, :]
    loss_ref[...] = total[128:129, 0:128] + total[129:130, 0:128] + total[130:131, 0:128]


VM = pl.BlockSpec(memory_space=pltpu.VMEM)


def call(kernel, out, *args, scratch=(), limit=8, cost=None):
    out = [jax.ShapeDtypeStruct(s, d) for s, d in out]
    return pl.pallas_call(
        kernel,
        out_shape=out,
        in_specs=[VM] * len(args),
        out_specs=[VM] * len(out),
        scratch_shapes=list(scratch),
        compiler_params=pltpu.CompilerParams(vmem_limit_bytes=limit << 20),
        cost_estimate=cost and pl.CostEstimate(flops=cost, bytes_accessed=1 << 20, transcendentals=1 << 20),
    )(*args)


def in_hbm(v):
    return pltpu.with_memory_space_constraint(v, pltpu.HBM)


def a2a(v, axes):
    return lax.all_to_all(v, axes, 0, 0, tiled=True)


def shift(v, axis, n, k):
    return lax.ppermute(v, axis, [(i, (i + k) % n) for i in range(n)])


PLANE = ("x", "y", "c")
HBM = pl.BlockSpec(memory_space=pl.ANY)


def local(teacher_feats, student_feats, prototypes, patch_mask):
    c = lax.axis_index("c")
    own, peak_pay, mine = pl.pallas_call(
        head_kernel,
        out_shape=[
            jax.ShapeDtypeStruct((2, LIVE, 256), bf16),
            jax.ShapeDtypeStruct((32, 8, 128), f32),
            jax.ShapeDtypeStruct((1024, 256), bf16),
        ],
        in_specs=[pl.BlockSpec(memory_space=pltpu.HBM)] * 4,
        out_specs=[VM] * 3,
        scratch_shapes=[
            pltpu.VMEM((1, 256), jnp.int32),
            pltpu.VMEM((1, 256, 256), bf16),
            pltpu.VMEM((1, 256, 256), bf16),
            pltpu.VMEM((8192, 256), bf16),
            pltpu.SemaphoreType.DMA((11,)),
        ],
        compiler_params=pltpu.CompilerParams(vmem_limit_bytes=32 << 20),
    )(*(in_hbm(v) for v in (patch_mask, teacher_feats, student_feats, prototypes)))

    other = shift(own, "c", 2, 1)
    pair = jnp.where(c == 0, jnp.stack([own, other]), jnp.stack([other, own]))
    parts = [pair] + [shift(pair, "x", 4, k) for k in (1, 2, 3)]

    peak_recv = a2a(peak_pay, PLANE)

    et, srows, stat, pay = pl.pallas_call(
        expo_kernel,
        out_shape=[
            jax.ShapeDtypeStruct((1024, 1024), bf16),
            jax.ShapeDtypeStruct((1024, 256), bf16),
            jax.ShapeDtypeStruct((3, 8, 128), f32),
            jax.ShapeDtypeStruct((8, 8, 128), f32),
        ],
        in_specs=[VM] + [HBM] * 4 + [VM],
        out_specs=[VM] * 4,
        scratch_shapes=[pltpu.VMEM((1024, 256), bf16), pltpu.SemaphoreType.DMA((16,))],
        compiler_params=pltpu.CompilerParams(vmem_limit_bytes=16 << 20),
    )(peak_recv, *parts, mine)

    (student_sum,) = call(student_sum_kernel, [((8, 128), f32)], srows, mine, cost=1 << 29, limit=16)

    recv = a2a(pay, "z")
    (pay,) = call(col_kernel, [((32, 16, 128), f32)], recv, et, student_sum)
    recv = a2a(pay, PLANE)
    prob, w, norm = pl.pallas_call(
        student_prob_kernel,
        out_shape=[
            pltpu.HBM((1024, 1024), f32),
            pltpu.HBM((1024, 1024), bf16),
            jax.ShapeDtypeStruct((8, 128), f32),
        ],
        in_specs=[VM] * 4,
        out_specs=[pl.BlockSpec(memory_space=pltpu.HBM)] * 2 + [VM],
        scratch_shapes=[
            pltpu.VMEM((1024, 1024), f32),
            pltpu.VMEM((1024, 1024), bf16),
            pltpu.SemaphoreType.DMA((8,)),
        ],
        compiler_params=pltpu.CompilerParams(vmem_limit_bytes=24 << 20),
        cost_estimate=pl.CostEstimate(flops=1 << 29, bytes_accessed=8 << 20, transcendentals=1 << 20),
    )(recv, srows, mine, et)
    (pay,) = call(row_kernel, [((8, 8, 128), f32)], recv, stat, et)
    for _ in range(BALANCING_PASSES - 2):
        recv = a2a(pay, "z")
        (pay,) = call(col_kernel, [((32, 8, 128), f32)], recv, et, norm)
        recv = a2a(pay, PLANE)
        (pay,) = call(row_kernel, [((8, 8, 128), f32)], recv, stat, et)
    recv = a2a(pay, "z")
    pay, col = call(last_col_kernel, [((32, 32, 128), bf16), ((8, 128), f32)], recv, et, w)
    recv = a2a(pay, PLANE)

    proto_part, scale = call(
        grad_kernel, [((8, 144, 256), bf16), ((2, 8, 128), f32)], recv, stat, col, et, prob, srows, limit=24
    )
    proto_recv = a2a(proto_part, "z")
    student_rows = pl.pallas_call(
        own_kernel,
        out_shape=jax.ShapeDtypeStruct((LIVE, 256), f32),
        in_specs=[VM] * 4 + [pl.BlockSpec(memory_space=pltpu.HBM)] * 2,
        out_specs=VM,
        scratch_shapes=[
            pltpu.VMEM((2, LIVE, 256), bf16),
            pltpu.VMEM((8192, 256), bf16),
            pltpu.SemaphoreType.DMA((9,)),
        ],
        compiler_params=pltpu.CompilerParams(vmem_limit_bytes=24 << 20),
        cost_estimate=pl.CostEstimate(flops=1 << 31, bytes_accessed=4 << 20, transcendentals=2 << 20),
    )(recv, scale, stat, norm, in_hbm(own), in_hbm(prototypes))
    student_rows = [student_rows] + [shift(student_rows, "y", 4, k) for k in (1, 2, 3)]
    student, proto, loss = call(
        end_kernel, [((256, 256), f32), ((128, 256), f32), ((1, 128), f32)], patch_mask, proto_recv, *student_rows,
        limit=16,
    )
    return loss[0, 0], student[None], proto[None]


def solution(mesh):
    fine = Mesh(mesh.devices.reshape(8, 4, 2, 4), ("z", "x", "c", "y"))
    dp = ("z", "x", "c")
    return jax.shard_map(
        local,
        mesh=fine,
        in_specs=(P(dp, None, None), P(dp, None, None), P("y", None), P(dp, None)),
        out_specs=(P(), P(dp, None, None), P("y", dp, None)),
        check_vma=False,
    )
```

```python
import jax
import jax.numpy as jnp
from jax import lax
from jax.experimental import pallas as pl
from jax.experimental.pallas import tpu as pltpu
from jax.sharding import Mesh, PartitionSpec as P

BALANCING_PASSES = 3
LOSS_SCALE = 16384
TEACHER_INV = 1.0 / 0.07
STUDENT_INV = 1.0 / 0.1
IMAGES = 64
LIVE = 128
NT = (((1,), (1,)), ((), ()))
NN = (((1,), (0,)), ((), ()))
TN = (((0,), (0,)), ((), ()))
f32 = jnp.float32
bf16 = jnp.bfloat16


def dot(a, b, dims):
    return lax.dot_general(a, b, dims, preferred_element_type=f32)


def to_lanes(v):
    return jnp.concatenate([v[i : i + 1, :] for i in range(8)], axis=1)


def to_tile(v):
    return jnp.concatenate([v[:, 128 * i : 128 * (i + 1)] for i in range(8)], axis=0)


def split3(v):
    hi = v.astype(bf16).astype(f32)
    mid = (v - hi).astype(bf16).astype(f32)
    lo = (v - hi - mid).astype(bf16).astype(f32)
    return jnp.concatenate([hi, mid, lo, jnp.zeros((13, v.shape[1]), f32)], axis=0).astype(bf16)


def selection(mask):
    patches = mask.shape[1]
    maskf = mask.astype(f32)
    before = lax.broadcasted_iota(jnp.int32, (patches, patches), 0)
    after = lax.broadcasted_iota(jnp.int32, (patches, patches), 1)
    tri = jnp.where(before <= after, 1.0, 0.0).astype(bf16)
    rank = dot(jnp.broadcast_to(maskf, (16, patches)).astype(bf16), tri, NN)[0:1, :]
    slot = lax.broadcasted_iota(jnp.int32, (LIVE, patches), 0).astype(f32)
    hit = jnp.where(rank - 1.0 == slot, 1.0, 0.0) * maskf
    return hit


def head_kernel(
    mask_hbm, teach_hbm, student_hbm, proto_hbm, own_ref, out_ref, mine_ref, mask_ref, teach_ref, student_ref, proto_ref, sems
):
    chunks = 4
    tall = proto_ref.shape[0] // chunks
    small = ((mask_hbm, mask_ref), (teach_hbm, teach_ref), (student_hbm, student_ref))
    first = [pltpu.make_async_copy(src, dst, sems.at[chunks + i]) for i, (src, dst) in enumerate(small)]
    copies = [
        pltpu.make_async_copy(proto_hbm.at[pl.ds(i * tall, tall)], proto_ref.at[pl.ds(i * tall, tall)], sems.at[i])
        for i in range(chunks)
    ]
    for copy in first + copies:
        copy.start()
    image = lax.axis_index("x") * 2 + lax.axis_index("c")
    first[0].wait()
    pick = selection(mask_ref[...]).astype(bf16)
    count = jnp.sum(mask_ref[...].astype(f32), axis=1, keepdims=True)
    first[1].wait()
    own_ref[0] = dot(pick, teach_ref[0], NN).astype(bf16)
    first[2].wait()
    own_ref[1] = dot(pick, student_ref[0], NN).astype(bf16)
    rows = own_ref[0]
    peak = None
    for i in range(chunks):
        copies[i].wait()
        for j in (2 * i, 2 * i + 1):
            mine_ref[128 * j : 128 * (j + 1), :] = proto_ref[pl.ds(pl.multiple_of(j * 1024 + image * 128, 128), 128), :]
        half = tall // 2
        low = dot(proto_ref[i * tall : i * tall + half, :], rows, NT)
        high = dot(proto_ref[i * tall + half : (i + 1) * tall, :], rows, NT)
        top = jnp.max(jnp.maximum(low, high), axis=0, keepdims=True)
        peak = top if peak is None else jnp.maximum(peak, top)
    tile = jnp.concatenate([peak * TEACHER_INV, jnp.broadcast_to(count, (1, LIVE)), jnp.zeros((6, LIVE), f32)], axis=0)
    out_ref[...] = jnp.broadcast_to(tile[None], out_ref.shape)


def expo_kernel(recv_ref, a_ref, b_ref, c_ref, d_ref, mine_ref, et_ref, srows_ref, stat_ref, pay_ref, peak_ref, live_ref):
    peaks, counts = [], []
    for x in range(4):
        for core in range(2):
            at = [(x * 4 + y) * 2 + core for y in range(4)]
            top = recv_ref[at[0], 0:1, :]
            for i in at[1:]:
                top = jnp.maximum(top, recv_ref[i, 0:1, :])
            peaks.append(top)
            counts.append(recv_ref[at[0], 1:2, :])
    count = jnp.concatenate(counts, axis=0)
    slot = lax.broadcasted_iota(jnp.int32, (8, 128), 1).astype(f32)
    live = jnp.where(slot < count, 1.0, 0.0)
    stat_ref[0] = live
    stat_ref[1] = live / count
    stat_ref[2] = jnp.concatenate(peaks, axis=0)
    for x in range(4):
        peak_ref[x : x + 1, :] = jnp.concatenate(peaks[2 * x : 2 * x + 2], axis=1)
        live_ref[x : x + 1, :] = jnp.concatenate([live[2 * x : 2 * x + 1], live[2 * x + 1 : 2 * x + 2]], axis=1)
    total = jnp.zeros((16, 1024), f32)
    for k, piece in enumerate((a_ref, b_ref, c_ref, d_ref)):
        x = (lax.axis_index("x") + 4 - k) & 3
        start = pl.multiple_of(x * 256, 256)
        rows = jnp.concatenate([piece[0, 0], piece[1, 0]], axis=0)
        logits = dot(mine_ref[...], rows, NT)
        block = jnp.exp(logits * TEACHER_INV - peak_ref[pl.ds(x, 1), :]).astype(bf16)
        et_ref[:, pl.ds(start, 256)] = block
        total += dot(jnp.broadcast_to(live_ref[pl.ds(x, 1), :], (16, 256)).astype(bf16), block, NT)
        for core in range(2):
            srows_ref[pl.ds(pl.multiple_of(start + core * 128, 128), 128), :] = piece[core, 1]
    pay_ref[...] = jnp.broadcast_to(to_tile(total[0:1])[None], pay_ref.shape)


def col_kernel(recv_ref, et_ref, extra_ref, pay_ref):
    col = 1.0 / jnp.sum(recv_ref[...], axis=0)
    out = jnp.sum(dot(split3(to_lanes(col)), et_ref[...], NN), axis=0, keepdims=True)
    pay_ref[:, 0:8, :] = jnp.broadcast_to(to_tile(out)[None], (pay_ref.shape[0], 8, 128))
    if pay_ref.shape[1] > 8:
        pay_ref[:, 8:, :] = jnp.broadcast_to(extra_ref[...][None], (pay_ref.shape[0], 8, 128))


def last_col_kernel(recv_ref, et_ref, w_ref, pay_ref, col_ref):
    col = 1.0 / jnp.sum(recv_ref[...], axis=0)
    col_ref[...] = col
    lhs = split3(to_lanes(col))
    out = to_tile(jnp.sum(dot(lhs, et_ref[...], NN), axis=0, keepdims=True))
    hi = out.astype(bf16).astype(f32)
    sums = jnp.concatenate([hi, out - hi], axis=0).astype(bf16)
    out = to_tile(jnp.sum(dot(lhs, w_ref[...], NN), axis=0, keepdims=True))
    rest = jnp.concatenate([out, col], axis=0).astype(bf16)
    pay_ref[:, 0:16, :] = jnp.broadcast_to(sums[None], (pay_ref.shape[0], 16, 128))
    pay_ref[:, 16:32, :] = jnp.broadcast_to(rest[None], (pay_ref.shape[0], 16, 128))


def row_kernel(recv_ref, stat_ref, et_ref, pay_ref):
    row = stat_ref[0] / jnp.sum(recv_ref[:, 0:8, :], axis=0)
    lhs = split3(to_lanes(row))
    out = jnp.sum(dot(lhs, et_ref[...], NT), axis=0, keepdims=True)
    pay_ref[...] = jnp.broadcast_to(to_tile(out)[None], pay_ref.shape)


def student_sum_kernel(srows_ref, mine_ref, out_ref):
    parts = []
    for r in range(4):
        logits = dot(mine_ref[...], srows_ref[256 * r : 256 * (r + 1), :], NT) * STUDENT_INV
        top = jnp.max(logits, axis=0, keepdims=True)
        parts.append(top + jnp.log(jnp.sum(jnp.exp(logits - top), axis=0, keepdims=True)))
    out_ref[...] = to_tile(jnp.concatenate(parts, axis=1))


def student_prob_kernel(recv_ref, srows_ref, mine_ref, et_ref, prob_hbm, w_hbm, norm_ref, prob_ref, w_ref, sems):
    parts = recv_ref[:, 8:16, :]
    top = jnp.max(parts, axis=0)
    norm_ref[...] = top + jnp.log(jnp.sum(jnp.exp(parts - top[None]), axis=0))
    norm = to_lanes(norm_ref[...])
    copies = []
    for r in range(4):
        at = slice(256 * r, 256 * (r + 1))
        log_prob = dot(mine_ref[...], srows_ref[at, :], NT) * STUDENT_INV - norm[:, at]
        prob_ref[:, at] = jnp.exp(log_prob)
        w_ref[:, at] = (et_ref[:, at].astype(f32) * log_prob).astype(bf16)
        at = (pl.ds(0, 1024), pl.ds(256 * r, 256))
        copies.append(pltpu.make_async_copy(prob_ref.at[at], prob_hbm.at[at], sems.at[r]))
        copies.append(pltpu.make_async_copy(w_ref.at[at], w_hbm.at[at], sems.at[4 + r]))
        copies[-2].start()
        copies[-1].start()
    for copy in copies:
        copy.wait()


def grad_kernel(recv_ref, stat_ref, col_ref, et_ref, prob_ref, srows_ref, pout_ref, scale_ref):
    sums = jnp.sum(recv_ref[:, 0:16, :].astype(f32), axis=0)
    entropy = jnp.sum(recv_ref[:, 16:32, :].astype(f32), axis=0)[0:8]
    row = stat_ref[0] / (sums[0:8] + sums[8:16])
    weight = stat_ref[1]
    loss = -jnp.sum(jnp.sum(weight * row * entropy, axis=1, keepdims=True), axis=0, keepdims=True) / IMAGES
    hi = loss.astype(bf16).astype(f32)
    mid = (loss - hi).astype(bf16).astype(f32)
    lo = loss - hi - mid
    which = lax.broadcasted_iota(jnp.int32, (8, 256), 0)
    tail = jnp.where(which == 0, hi, jnp.where(which == 1, mid, jnp.where(which == 2, lo, 0.0))).astype(bf16)
    coef = weight * (LOSS_SCALE / (IMAGES * 0.1))
    scale_ref[0] = coef
    scale_ref[1] = coef * row
    coef_rows = to_lanes(coef)
    scale_rows = to_lanes(coef * row)
    for j in range(4):
        at = slice(256 * j, 256 * (j + 1))
        col = jnp.concatenate([jnp.broadcast_to(col_ref[i : i + 1, :], (128, 128)).T for i in (2 * j, 2 * j + 1)], axis=0)
        col = jnp.concatenate([col] * 8, axis=1)
        grad = (prob_ref[at, :] * coef_rows - et_ref[at, :].astype(f32) * col * scale_rows).astype(bf16)
        part = dot(grad, srows_ref[...], NN).astype(bf16)
        for i in (0, 1):
            pout_ref[2 * j + i, 0:128, :] = part[128 * i : 128 * (i + 1)]
            pout_ref[2 * j + i, 128:136, :] = tail


def column(row, wide):
    return jnp.concatenate([jnp.broadcast_to(row, (128, 128)).T] * (wide // 128), axis=1)


def own_image():
    return pl.ds(lax.axis_index("x") * 2 + lax.axis_index("c"), 1)


def own_kernel(recv_ref, scale_ref, stat_ref, norm_ref, rows_hbm, proto_hbm, out_ref, rows_ref, proto_ref, sems):
    chunks = 4
    tall = proto_ref.shape[0] // chunks
    rows_copy = pltpu.make_async_copy(rows_hbm, rows_ref, sems.at[chunks])
    copies = [
        pltpu.make_async_copy(proto_hbm.at[pl.ds(i * tall, tall)], proto_ref.at[pl.ds(i * tall, tall)], sems.at[i])
        for i in range(chunks)
    ]
    for copy in [rows_copy] + copies:
        copy.start()
    y = lax.axis_index("y")
    peak = column(stat_ref[2, own_image(), :], 1024)
    norm = column(norm_ref[own_image(), :], 1024)
    coef = column(scale_ref[0, own_image(), :], 1024)
    scale = column(scale_ref[1, own_image(), :], 1024)
    cols = [recv_ref[(x * 4 + y) * 2 + c, 16:32, :].astype(f32) for x in range(4) for c in range(2)]
    rows_copy.wait()
    rows = rows_ref[...].reshape(2 * LIVE, 256)
    total = jnp.zeros((LIVE, 256), f32)
    for i in range(8):
        if i % 2 == 0:
            copies[i // 2].wait()
        col = jnp.concatenate([v[8 + i : 9 + i, :] for v in cols], axis=1)
        block = proto_ref[1024 * i : 1024 * (i + 1), :]
        logits = dot(rows, block, NT)
        teach = jnp.exp(logits[0:LIVE] * TEACHER_INV - peak).astype(bf16).astype(f32)
        prob = jnp.exp(logits[LIVE:] * STUDENT_INV - norm)
        grad = (prob * coef - teach * (col * scale)).astype(bf16)
        total += dot(grad, block, NN)
    out_ref[...] = total.astype(bf16)


def end_kernel(mask_ref, recv_ref, a_ref, b_ref, c_ref, d_ref, student_ref, proto_ref, loss_ref):
    pick = selection(mask_ref[...]).astype(bf16)
    parts = [ref[...].astype(f32) for ref in (a_ref, b_ref, c_ref, d_ref)]
    rows = (parts[0] + parts[2]) + (parts[1] + parts[3])
    hi = rows.astype(bf16)
    rest = rows - hi.astype(f32)
    mid = rest.astype(bf16)
    lo = (rest - mid.astype(f32)).astype(bf16)
    student_ref[...] = dot(pick, hi, TN) + dot(pick, mid, TN) + dot(pick, lo, TN)
    total = jnp.sum(recv_ref[...].astype(f32), axis=0)
    proto_ref[...] = total[0:128, :]
    loss_ref[...] = total[128:129, 0:128] + total[129:130, 0:128] + total[130:131, 0:128]


VM = pl.BlockSpec(memory_space=pltpu.VMEM)


def call(kernel, out, *args, scratch=(), limit=8, cost=None):
    out = [jax.ShapeDtypeStruct(s, d) for s, d in out]
    return pl.pallas_call(
        kernel,
        out_shape=out,
        in_specs=[VM] * len(args),
        out_specs=[VM] * len(out),
        scratch_shapes=list(scratch),
        compiler_params=pltpu.CompilerParams(vmem_limit_bytes=limit << 20),
        cost_estimate=cost and pl.CostEstimate(flops=cost, bytes_accessed=1 << 20, transcendentals=1 << 20),
    )(*args)


def in_hbm(v):
    return pltpu.with_memory_space_constraint(v, pltpu.HBM)


def a2a(v, axes):
    return lax.all_to_all(v, axes, 0, 0, tiled=True)


def shift(v, axis, n, k):
    return lax.ppermute(v, axis, [(i, (i + k) % n) for i in range(n)])


PLANE = ("x", "y", "c")
HBM = pl.BlockSpec(memory_space=pl.ANY)


def local(teacher_feats, student_feats, prototypes, patch_mask):
    c = lax.axis_index("c")
    own, peak_pay, mine = pl.pallas_call(
        head_kernel,
        out_shape=[
            jax.ShapeDtypeStruct((2, LIVE, 256), bf16),
            jax.ShapeDtypeStruct((32, 8, 128), f32),
            jax.ShapeDtypeStruct((1024, 256), bf16),
        ],
        in_specs=[HBM] * 4,
        out_specs=[VM] * 3,
        scratch_shapes=[
            pltpu.VMEM((1, 256), jnp.int32),
            pltpu.VMEM((1, 256, 256), bf16),
            pltpu.VMEM((1, 256, 256), bf16),
            pltpu.VMEM((8192, 256), bf16),
            pltpu.SemaphoreType.DMA((7,)),
        ],
        compiler_params=pltpu.CompilerParams(vmem_limit_bytes=32 << 20),
    )(*(in_hbm(v) for v in (patch_mask, teacher_feats, student_feats, prototypes)))

    other = shift(own, "c", 2, 1)
    pair = jnp.where(c == 0, jnp.stack([own, other]), jnp.stack([other, own]))
    parts = [pair] + [shift(pair, "x", 4, k) for k in (1, 2, 3)]

    peak_recv = a2a(peak_pay, PLANE)

    et, srows, stat, pay = call(
        expo_kernel,
        [((1024, 1024), bf16), ((1024, 256), bf16), ((3, 8, 128), f32), ((8, 8, 128), f32)],
        peak_recv, *parts, mine, limit=16, scratch=[pltpu.VMEM((8, 256), f32)] * 2,
    )

    (student_sum,) = call(student_sum_kernel, [((8, 128), f32)], srows, mine, cost=1 << 29, limit=16)

    recv = a2a(pay, "z")
    (pay,) = call(col_kernel, [((32, 16, 128), f32)], recv, et, student_sum)
    recv = a2a(pay, PLANE)
    prob, w, norm = pl.pallas_call(
        student_prob_kernel,
        out_shape=[
            pltpu.HBM((1024, 1024), f32),
            pltpu.HBM((1024, 1024), bf16),
            jax.ShapeDtypeStruct((8, 128), f32),
        ],
        in_specs=[VM] * 4,
        out_specs=[pl.BlockSpec(memory_space=pltpu.HBM)] * 2 + [VM],
        scratch_shapes=[
            pltpu.VMEM((1024, 1024), f32),
            pltpu.VMEM((1024, 1024), bf16),
            pltpu.SemaphoreType.DMA((8,)),
        ],
        compiler_params=pltpu.CompilerParams(vmem_limit_bytes=24 << 20),
        cost_estimate=pl.CostEstimate(flops=1 << 29, bytes_accessed=8 << 20, transcendentals=1 << 20),
    )(recv, srows, mine, et)
    (pay,) = call(row_kernel, [((8, 8, 128), f32)], recv, stat, et)
    for _ in range(BALANCING_PASSES - 2):
        recv = a2a(pay, "z")
        (pay,) = call(col_kernel, [((32, 8, 128), f32)], recv, et, norm)
        recv = a2a(pay, PLANE)
        (pay,) = call(row_kernel, [((8, 8, 128), f32)], recv, stat, et)
    recv = a2a(pay, "z")
    pay, col = call(last_col_kernel, [((32, 32, 128), bf16), ((8, 128), f32)], recv, et, w)
    recv = a2a(pay, PLANE)

    proto_part, scale = call(
        grad_kernel, [((8, 136, 256), bf16), ((2, 8, 128), f32)], recv, stat, col, et, prob, srows, limit=24
    )
    proto_recv = a2a(proto_part, "z")
    student_rows = pl.pallas_call(
        own_kernel,
        out_shape=jax.ShapeDtypeStruct((LIVE, 256), bf16),
        in_specs=[VM] * 4 + [HBM] * 2,
        out_specs=VM,
        scratch_shapes=[
            pltpu.VMEM((2, LIVE, 256), bf16),
            pltpu.VMEM((8192, 256), bf16),
            pltpu.SemaphoreType.DMA((5,)),
        ],
        compiler_params=pltpu.CompilerParams(vmem_limit_bytes=24 << 20),
        cost_estimate=pl.CostEstimate(flops=1 << 31, bytes_accessed=4 << 20, transcendentals=2 << 20),
    )(recv, scale, stat, norm, in_hbm(own), in_hbm(prototypes))
    student_rows = [student_rows] + [shift(student_rows, "y", 4, k) for k in (1, 2, 3)]
    student, proto, loss = call(
        end_kernel, [((256, 256), f32), ((128, 256), f32), ((1, 128), f32)], patch_mask, proto_recv, *student_rows,
        limit=16,
    )
    return loss[0, 0], student[None], proto[None]


def solution(mesh):
    fine = Mesh(mesh.devices.reshape(8, 4, 2, 4), ("z", "x", "c", "y"))
    dp = ("z", "x", "c")
    return jax.shard_map(
        local,
        mesh=fine,
        in_specs=(P(dp, None, None), P(dp, None, None), P("y", None), P(dp, None)),
        out_specs=(P(), P(dp, None, None), P("y", dp, None)),
        check_vma=False,
    )
```

```python
import jax
import jax.numpy as jnp
from jax import lax
from jax.experimental import pallas as pl
from jax.experimental.pallas import tpu as pltpu
from jax.sharding import Mesh, PartitionSpec as P

BALANCING_PASSES = 3
LOSS_SCALE = 16384
TEACHER_INV = 1.0 / 0.07
STUDENT_INV = 1.0 / 0.1
IMAGES = 64
LIVE = 128
NT = (((1,), (1,)), ((), ()))
NN = (((1,), (0,)), ((), ()))
TN = (((0,), (0,)), ((), ()))
f32 = jnp.float32
bf16 = jnp.bfloat16


def dot(a, b, dims):
    return lax.dot_general(a, b, dims, preferred_element_type=f32)


def to_lanes(v):
    return jnp.concatenate([v[i : i + 1, :] for i in range(8)], axis=1)


def to_tile(v):
    return jnp.concatenate([v[:, 128 * i : 128 * (i + 1)] for i in range(8)], axis=0)


def thirds(v):
    hi = v.astype(bf16).astype(f32)
    mid = (v - hi).astype(bf16).astype(f32)
    return [hi, mid, (v - hi - mid).astype(bf16).astype(f32)]


def split3(v):
    return jnp.concatenate(thirds(v) + [jnp.zeros((13, v.shape[1]), f32)], axis=0).astype(bf16)


def selection(mask):
    patches = mask.shape[1]
    maskf = mask.astype(f32)
    before = lax.broadcasted_iota(jnp.int32, (patches, patches), 0)
    after = lax.broadcasted_iota(jnp.int32, (patches, patches), 1)
    tri = jnp.where(before <= after, 1.0, 0.0).astype(bf16)
    rank = dot(jnp.broadcast_to(maskf, (16, patches)).astype(bf16), tri, NN)[0:1, :]
    slot = lax.broadcasted_iota(jnp.int32, (LIVE, patches), 0).astype(f32)
    hit = jnp.where(rank - 1.0 == slot, 1.0, 0.0) * maskf
    return hit


def head_kernel(
    mask_hbm, teach_hbm, student_hbm, proto_hbm, own_ref, out_ref, mine_ref, mask_ref, teach_ref, student_ref, proto_ref, sems
):
    chunks = 4
    tall = proto_ref.shape[0] // chunks
    small = ((mask_hbm, mask_ref), (teach_hbm, teach_ref), (student_hbm, student_ref))
    first = [pltpu.make_async_copy(src, dst, sems.at[chunks + i]) for i, (src, dst) in enumerate(small)]
    copies = [
        pltpu.make_async_copy(proto_hbm.at[pl.ds(i * tall, tall)], proto_ref.at[pl.ds(i * tall, tall)], sems.at[i])
        for i in range(chunks)
    ]
    for copy in first + copies:
        copy.start()
    image = lax.axis_index("x") * 2 + lax.axis_index("c")
    first[0].wait()
    pick = selection(mask_ref[...]).astype(bf16)
    count = jnp.sum(mask_ref[...].astype(f32), axis=1, keepdims=True)
    first[1].wait()
    own_ref[0] = dot(pick, teach_ref[0], NN).astype(bf16)
    first[2].wait()
    own_ref[1] = dot(pick, student_ref[0], NN).astype(bf16)
    rows = own_ref[...].reshape(2 * LIVE, 256)
    peak = top = total = None
    for i in range(chunks):
        copies[i].wait()
        for j in (2 * i, 2 * i + 1):
            mine_ref[128 * j : 128 * (j + 1), :] = proto_ref[pl.ds(pl.multiple_of(j * 1024 + image * 128, 128), 128), :]
            logits = dot(proto_ref[1024 * j : 1024 * (j + 1), :], rows, NT)
            teach = jnp.max(logits[:, :LIVE], axis=0, keepdims=True)
            student = logits[:, LIVE:] * STUDENT_INV
            now = jnp.max(student, axis=0, keepdims=True)
            part = jnp.sum(jnp.exp(student - now), axis=0, keepdims=True)
            if peak is None:
                peak, top, total = teach, now, part
            else:
                peak, both = jnp.maximum(peak, teach), jnp.maximum(top, now)
                total = total * jnp.exp(top - both) + part * jnp.exp(now - both)
                top = both
    tile = jnp.concatenate(
        thirds(peak * TEACHER_INV)
        + [jnp.broadcast_to(count, (1, LIVE))]
        + thirds(top + jnp.log(total))
        + [jnp.zeros((1, LIVE), f32)],
        axis=0,
    )
    out_ref[...] = jnp.broadcast_to(tile[None].astype(bf16), out_ref.shape)


def expo_kernel(recv_ref, a_ref, b_ref, c_ref, d_ref, mine_ref, et_ref, srows_ref, stat_ref, pay_ref, peak_ref, live_ref):
    peaks, counts = [], []
    for x in range(4):
        for core in range(2):
            got = [recv_ref[(x * 4 + y) * 2 + core].astype(f32) for y in range(4)]
            tops = [v[0:1] + v[1:2] + v[2:3] for v in got]
            peaks.append(jnp.maximum(jnp.maximum(tops[0], tops[1]), jnp.maximum(tops[2], tops[3])))
            counts.append(got[0][3:4])
    count = jnp.concatenate(counts, axis=0)
    slot = lax.broadcasted_iota(jnp.int32, (8, 128), 1).astype(f32)
    live = jnp.where(slot < count, 1.0, 0.0)
    stat_ref[0] = live
    stat_ref[1] = live / count
    stat_ref[2] = jnp.concatenate(peaks, axis=0)
    for x in range(4):
        peak_ref[x : x + 1, :] = jnp.concatenate(peaks[2 * x : 2 * x + 2], axis=1)
        live_ref[x : x + 1, :] = jnp.concatenate([live[2 * x : 2 * x + 1], live[2 * x + 1 : 2 * x + 2]], axis=1)
    total = jnp.zeros((16, 1024), f32)
    for k, piece in enumerate((a_ref, b_ref, c_ref, d_ref)):
        x = (lax.axis_index("x") + 4 - k) & 3
        start = pl.multiple_of(x * 256, 256)
        rows = jnp.concatenate([piece[0, 0], piece[1, 0]], axis=0)
        logits = dot(mine_ref[...], rows, NT)
        block = jnp.exp(logits * TEACHER_INV - peak_ref[pl.ds(x, 1), :]).astype(bf16)
        et_ref[:, pl.ds(start, 256)] = block
        total += dot(jnp.broadcast_to(live_ref[pl.ds(x, 1), :], (16, 256)).astype(bf16), block, NT)
        for core in range(2):
            srows_ref[pl.ds(pl.multiple_of(start + core * 128, 128), 128), :] = piece[core, 1]
    pay_ref[...] = jnp.broadcast_to(to_tile(total[0:1])[None], pay_ref.shape)


def spread(tile, ref):
    ref[...] = jnp.broadcast_to(tile[None].astype(ref.dtype), ref.shape)


def col_kernel(recv_ref, et_ref, *refs):
    col = 1.0 / jnp.sum(recv_ref[...], axis=0)
    out = jnp.sum(dot(split3(to_lanes(col)), et_ref[...], NN), axis=0, keepdims=True)
    spread(to_tile(out), refs[-1])


def last_col_kernel(recv_ref, et_ref, w_ref, pay_ref, col_ref):
    col = 1.0 / jnp.sum(recv_ref[...], axis=0)
    col_ref[...] = col
    lhs = split3(to_lanes(col))
    out = to_tile(jnp.sum(dot(lhs, et_ref[...], NN), axis=0, keepdims=True))
    entropy = to_tile(jnp.sum(dot(lhs, w_ref[...], NN), axis=0, keepdims=True))
    spread(jnp.concatenate([out, entropy, col], axis=0), pay_ref)


def row_kernel(recv_ref, stat_ref, et_ref, pay_ref):
    row = stat_ref[0] / jnp.sum(recv_ref[...].astype(f32), axis=0)
    out = jnp.sum(dot(split3(to_lanes(row)), et_ref[...], NT), axis=0, keepdims=True)
    spread(to_tile(out), pay_ref)


def student_prob_kernel(recv_ref, srows_ref, mine_ref, et_ref, prob_hbm, w_hbm, norm_ref, prob_ref, w_ref, sems):
    for image in range(8):
        got = [recv_ref[(image // 2 * 4 + y) * 2 + image % 2].astype(f32) for y in range(4)]
        parts = [v[4:5] + v[5:6] + v[6:7] for v in got]
        top = jnp.maximum(jnp.maximum(parts[0], parts[1]), jnp.maximum(parts[2], parts[3]))
        total = sum(jnp.exp(v - top) for v in parts)
        norm_ref[image : image + 1, :] = top + jnp.log(total)
    norm = to_lanes(norm_ref[...])
    copies = []
    for r in range(4):
        at = slice(256 * r, 256 * (r + 1))
        log_prob = dot(mine_ref[...], srows_ref[at, :], NT) * STUDENT_INV - norm[:, at]
        prob_ref[:, at] = jnp.exp(log_prob)
        w_ref[:, at] = (et_ref[:, at].astype(f32) * log_prob).astype(bf16)
        at = (pl.ds(0, 1024), pl.ds(256 * r, 256))
        copies.append(pltpu.make_async_copy(prob_ref.at[at], prob_hbm.at[at], sems.at[r]))
        copies.append(pltpu.make_async_copy(w_ref.at[at], w_hbm.at[at], sems.at[4 + r]))
        copies[-2].start()
        copies[-1].start()
    for copy in copies:
        copy.wait()


def grad_kernel(recv_ref, stat_ref, col_ref, et_ref, prob_ref, srows_ref, pout_hbm, scale_ref, pout_ref, sems):
    sums = jnp.sum(recv_ref[...].astype(f32), axis=0)
    entropy = sums[8:16]
    row = stat_ref[0] / sums[0:8]
    weight = stat_ref[1]
    loss = -jnp.sum(jnp.sum(weight * row * entropy, axis=1, keepdims=True), axis=0, keepdims=True) / IMAGES
    hi = loss.astype(bf16).astype(f32)
    mid = (loss - hi).astype(bf16).astype(f32)
    lo = loss - hi - mid
    which = lax.broadcasted_iota(jnp.int32, (8, 128), 0)
    tail = jnp.where(which == 0, hi, jnp.where(which == 1, mid, jnp.where(which == 2, lo, 0.0))).astype(bf16)
    coef = weight * (LOSS_SCALE / (IMAGES * 0.1))
    scale_ref[0] = coef
    scale_ref[1] = coef * row
    coef_rows = to_lanes(coef)
    scale_rows = to_lanes(coef * row)
    copies = []
    for j in range(4):
        at = slice(256 * j, 256 * (j + 1))
        col = jnp.concatenate([jnp.broadcast_to(col_ref[i : i + 1, :], (128, 128)).T for i in (2 * j, 2 * j + 1)], axis=0)
        col = jnp.concatenate([col] * 8, axis=1)
        grad = (prob_ref[at, :] * coef_rows - et_ref[at, :].astype(f32) * col * scale_rows).astype(bf16)
        part = dot(grad, srows_ref[...], NN).astype(bf16)
        for i in (0, 1):
            pout_ref[2 * j + i, 0:128, :] = part[128 * i : 128 * (i + 1), 0:128]
            pout_ref[2 * j + i, 128:256, :] = part[128 * i : 128 * (i + 1), 128:256]
            pout_ref[2 * j + i, 256:264, :] = tail
        at = pl.ds(2 * j, 2)
        copies.append(pltpu.make_async_copy(pout_ref.at[at], pout_hbm.at[at], sems.at[j]))
        copies[-1].start()
    for copy in copies:
        copy.wait()


def column(row, wide):
    return jnp.concatenate([jnp.broadcast_to(row, (128, 128)).T] * (wide // 128), axis=1)


def own_image():
    return pl.ds(lax.axis_index("x") * 2 + lax.axis_index("c"), 1)


def own_kernel(recv_ref, scale_ref, stat_ref, norm_ref, rows_hbm, proto_hbm, out_ref, rows_ref, proto_ref, sems):
    chunks = 4
    tall = proto_ref.shape[0] // chunks
    rows_copy = pltpu.make_async_copy(rows_hbm, rows_ref, sems.at[chunks])
    copies = [
        pltpu.make_async_copy(proto_hbm.at[pl.ds(i * tall, tall)], proto_ref.at[pl.ds(i * tall, tall)], sems.at[i])
        for i in range(chunks)
    ]
    for copy in [rows_copy] + copies:
        copy.start()
    y = lax.axis_index("y")
    peak = column(stat_ref[2, own_image(), :], 1024)
    norm = column(norm_ref[own_image(), :], 1024)
    coef = column(scale_ref[0, own_image(), :], 1024)
    scale = column(scale_ref[1, own_image(), :], 1024)
    cols = [recv_ref[(x * 4 + y) * 2 + c].astype(f32)[16:24] for x in range(4) for c in range(2)]
    rows_copy.wait()
    rows = rows_ref[...].reshape(2 * LIVE, 256)
    total = jnp.zeros((LIVE, 256), f32)
    for i in range(8):
        if i % 2 == 0:
            copies[i // 2].wait()
        col = jnp.concatenate([v[i : i + 1, :] for v in cols], axis=1)
        block = proto_ref[1024 * i : 1024 * (i + 1), :]
        logits = dot(rows, block, NT)
        teach = jnp.exp(logits[0:LIVE] * TEACHER_INV - peak).astype(bf16).astype(f32)
        prob = jnp.exp(logits[LIVE:] * STUDENT_INV - norm)
        grad = (prob * coef - teach * (col * scale)).astype(bf16)
        total += dot(grad, block, NN)
    out_ref[...] = total.astype(bf16)


def end_kernel(mask_ref, recv_ref, a_ref, b_ref, c_ref, d_ref, student_ref, proto_ref, loss_ref):
    pick = selection(mask_ref[...]).astype(bf16)
    parts = [ref[...].astype(f32) for ref in (a_ref, b_ref, c_ref, d_ref)]
    rows = (parts[0] + parts[2]) + (parts[1] + parts[3])
    hi = rows.astype(bf16)
    rest = rows - hi.astype(f32)
    mid = rest.astype(bf16)
    lo = (rest - mid.astype(f32)).astype(bf16)
    student_ref[...] = dot(pick, hi, TN) + dot(pick, mid, TN) + dot(pick, lo, TN)
    total = jnp.sum(recv_ref[...].astype(f32), axis=0)
    proto_ref[:, 0:128] = total[0:128]
    proto_ref[:, 128:256] = total[128:256]
    loss_ref[...] = total[256:257] + total[257:258] + total[258:259]


VM = pl.BlockSpec(memory_space=pltpu.VMEM)


def call(kernel, out, *args, scratch=(), limit=8, cost=None):
    out = [jax.ShapeDtypeStruct(s, d) for s, d in out]
    return pl.pallas_call(
        kernel,
        out_shape=out,
        in_specs=[VM] * len(args),
        out_specs=[VM] * len(out),
        scratch_shapes=list(scratch),
        compiler_params=pltpu.CompilerParams(vmem_limit_bytes=limit << 20),
        cost_estimate=cost and pl.CostEstimate(flops=cost, bytes_accessed=1 << 20, transcendentals=1 << 20),
    )(*args)


def in_hbm(v):
    return pltpu.with_memory_space_constraint(v, pltpu.HBM)


def a2a(v, axes):
    return lax.all_to_all(v, axes, 0, 0, tiled=True)


def shift(v, axis, n, k):
    return lax.ppermute(v, axis, [(i, (i + k) % n) for i in range(n)])


PLANE = ("x", "y", "c")
HBM = pl.BlockSpec(memory_space=pl.ANY)


def local(teacher_feats, student_feats, prototypes, patch_mask):
    c = lax.axis_index("c")
    own, peak_pay, mine = pl.pallas_call(
        head_kernel,
        out_shape=[
            jax.ShapeDtypeStruct((2, LIVE, 256), bf16),
            jax.ShapeDtypeStruct((32, 8, 128), bf16),
            jax.ShapeDtypeStruct((1024, 256), bf16),
        ],
        in_specs=[HBM] * 4,
        out_specs=[VM] * 3,
        scratch_shapes=[
            pltpu.VMEM((1, 256), jnp.int32),
            pltpu.VMEM((1, 256, 256), bf16),
            pltpu.VMEM((1, 256, 256), bf16),
            pltpu.VMEM((8192, 256), bf16),
            pltpu.SemaphoreType.DMA((7,)),
        ],
        compiler_params=pltpu.CompilerParams(vmem_limit_bytes=32 << 20),
    )(*(in_hbm(v) for v in (patch_mask, teacher_feats, student_feats, prototypes)))

    other = shift(own, "c", 2, 1)
    pair = jnp.where(c == 0, jnp.stack([own, other]), jnp.stack([other, own]))
    parts = [pair] + [shift(pair, "x", 4, k) for k in (1, 2, 3)]

    peak_recv = a2a(peak_pay, PLANE)

    et, srows, stat, pay = call(
        expo_kernel,
        [((1024, 1024), bf16), ((1024, 256), bf16), ((3, 8, 128), f32), ((8, 8, 128), f32)],
        peak_recv, *parts, mine, limit=16, scratch=[pltpu.VMEM((8, 256), f32)] * 2,
    )

    recv = a2a(pay, "z")
    (pay,) = call(col_kernel, [((32, 8, 128), bf16)], recv, et)
    recv = a2a(pay, PLANE)
    prob, w, norm = pl.pallas_call(
        student_prob_kernel,
        out_shape=[
            pltpu.HBM((1024, 1024), f32),
            pltpu.HBM((1024, 1024), bf16),
            jax.ShapeDtypeStruct((8, 128), f32),
        ],
        in_specs=[VM] * 4,
        out_specs=[pl.BlockSpec(memory_space=pltpu.HBM)] * 2 + [VM],
        scratch_shapes=[
            pltpu.VMEM((1024, 1024), f32),
            pltpu.VMEM((1024, 1024), bf16),
            pltpu.SemaphoreType.DMA((8,)),
        ],
        compiler_params=pltpu.CompilerParams(vmem_limit_bytes=24 << 20),
        cost_estimate=pl.CostEstimate(flops=1 << 29, bytes_accessed=8 << 20, transcendentals=1 << 20),
    )(peak_recv, srows, mine, et)
    (pay,) = call(row_kernel, [((8, 8, 128), f32)], recv, stat, et)
    for _ in range(BALANCING_PASSES - 2):
        recv = a2a(pay, "z")
        (pay,) = call(col_kernel, [((32, 8, 128), bf16)], recv, et, norm)
        recv = a2a(pay, PLANE)
        (pay,) = call(row_kernel, [((8, 8, 128), f32)], recv, stat, et)
    recv = a2a(pay, "z")
    pay, col = call(last_col_kernel, [((32, 24, 128), bf16), ((8, 128), f32)], recv, et, w)
    recv = a2a(pay, PLANE)

    proto_part, scale = pl.pallas_call(
        grad_kernel,
        out_shape=[pltpu.HBM((8, 264, 128), bf16), jax.ShapeDtypeStruct((2, 8, 128), f32)],
        in_specs=[VM] * 6,
        out_specs=[pl.BlockSpec(memory_space=pltpu.HBM), VM],
        scratch_shapes=[pltpu.VMEM((8, 264, 128), bf16), pltpu.SemaphoreType.DMA((4,))],
        compiler_params=pltpu.CompilerParams(vmem_limit_bytes=24 << 20),
    )(recv, stat, col, et, prob, srows)
    proto_recv = a2a(proto_part, "z")
    student_rows = pl.pallas_call(
        own_kernel,
        out_shape=jax.ShapeDtypeStruct((LIVE, 256), bf16),
        in_specs=[VM] * 4 + [HBM] * 2,
        out_specs=VM,
        scratch_shapes=[
            pltpu.VMEM((2, LIVE, 256), bf16),
            pltpu.VMEM((8192, 256), bf16),
            pltpu.SemaphoreType.DMA((5,)),
        ],
        compiler_params=pltpu.CompilerParams(vmem_limit_bytes=24 << 20),
        cost_estimate=pl.CostEstimate(flops=1 << 31, bytes_accessed=4 << 20, transcendentals=2 << 20),
    )(recv, scale, stat, norm, in_hbm(own), in_hbm(prototypes))
    student_rows = [student_rows] + [shift(student_rows, "y", 4, k) for k in (1, 2, 3)]
    student, proto, loss = call(
        end_kernel, [((256, 256), f32), ((128, 256), f32), ((1, 128), f32)], patch_mask, proto_recv, *student_rows,
        limit=16,
    )
    return loss[0, 0], student[None], proto[None]


def solution(mesh):
    fine = Mesh(mesh.devices.reshape(8, 4, 2, 4), ("z", "x", "c", "y"))
    dp = ("z", "x", "c")
    return jax.shard_map(
        local,
        mesh=fine,
        in_specs=(P(dp, None, None), P(dp, None, None), P("y", None), P(dp, None)),
        out_specs=(P(), P(dp, None, None), P("y", dp, None)),
        check_vma=False,
    )
```

```python
import jax
import jax.numpy as jnp
from jax import lax
from jax.experimental import pallas as pl
from jax.experimental.pallas import tpu as pltpu
from jax.sharding import Mesh, PartitionSpec as P

BALANCING_PASSES = 3
LOSS_SCALE = 16384
TEACHER_INV = 1.0 / 0.07
STUDENT_INV = 1.0 / 0.1
IMAGES = 64
GRAD_FACTOR = LOSS_SCALE / (IMAGES * 0.1)
LIVE = 128
NT = (((1,), (1,)), ((), ()))
NN = (((1,), (0,)), ((), ()))
TN = (((0,), (0,)), ((), ()))
f32 = jnp.float32
bf16 = jnp.bfloat16


def dot(a, b, dims):
    return lax.dot_general(a, b, dims, preferred_element_type=f32)


def to_lanes(v):
    return jnp.concatenate([v[i : i + 1, :] for i in range(8)], axis=1)


def to_tile(v):
    return jnp.concatenate([v[:, 128 * i : 128 * (i + 1)] for i in range(8)], axis=0)


def thirds(v):
    hi = v.astype(bf16).astype(f32)
    mid = (v - hi).astype(bf16).astype(f32)
    return [hi, mid, (v - hi - mid).astype(bf16).astype(f32)]


def split3(v):
    return jnp.concatenate(thirds(v) + [jnp.zeros((13, v.shape[1]), f32)], axis=0).astype(bf16)


def selection(mask):
    patches = mask.shape[1]
    maskf = mask.astype(f32)
    before = lax.broadcasted_iota(jnp.int32, (patches, patches), 0)
    after = lax.broadcasted_iota(jnp.int32, (patches, patches), 1)
    tri = jnp.where(before <= after, 1.0, 0.0).astype(bf16)
    rank = dot(jnp.broadcast_to(maskf, (16, patches)).astype(bf16), tri, NN)[0:1, :]
    slot = lax.broadcasted_iota(jnp.int32, (LIVE, patches), 0).astype(f32)
    hit = jnp.where(rank - 1.0 == slot, 1.0, 0.0) * maskf
    return hit


def head_kernel(
    mask_hbm, teach_hbm, student_hbm, proto_hbm, own_ref, out_ref, mine_ref, mask_ref, teach_ref, student_ref, proto_ref, sems
):
    chunks = 2
    tall = proto_ref.shape[0] // chunks
    small = ((mask_hbm, mask_ref), (teach_hbm, teach_ref), (student_hbm, student_ref))
    first = [pltpu.make_async_copy(src, dst, sems.at[chunks + i]) for i, (src, dst) in enumerate(small)]
    copies = [
        pltpu.make_async_copy(proto_hbm.at[pl.ds(i * tall, tall)], proto_ref.at[pl.ds(i * tall, tall)], sems.at[i])
        for i in range(chunks)
    ]
    for copy in first + copies:
        copy.start()
    image = lax.axis_index("x") * 2 + lax.axis_index("c")
    first[0].wait()
    pick = selection(mask_ref[...]).astype(bf16)
    count = jnp.sum(mask_ref[...].astype(f32), axis=1, keepdims=True)
    first[1].wait()
    own_ref[0] = dot(pick, teach_ref[0], NN).astype(bf16)
    first[2].wait()
    own_ref[1] = dot(pick, student_ref[0], NN).astype(bf16)
    rows = own_ref[...].reshape(2 * LIVE, 256)
    peak = top = total = None
    for i in range(0, 8192, 512):
        if i % tall == 0:
            copies[i // tall].wait()
        if i % 1024 == 0:
            at = pl.multiple_of(i + image * 128, 128)
            mine_ref[i // 8 : i // 8 + 128, :] = proto_ref[pl.ds(at, 128), :]
        low = dot(proto_ref[i : i + 256, :], rows, NT)
        high = dot(proto_ref[i + 256 : i + 512, :], rows, NT)
        teach = jnp.max(jnp.maximum(low[:, :LIVE], high[:, :LIVE]), axis=0, keepdims=True)
        student = jnp.concatenate([low[:, LIVE:], high[:, LIVE:]], axis=0) * STUDENT_INV
        now = jnp.max(student, axis=0, keepdims=True)
        part = jnp.sum(jnp.exp(student - now), axis=0, keepdims=True)
        if peak is None:
            peak, top, total = teach, now, part
        else:
            peak, both = jnp.maximum(peak, teach), jnp.maximum(top, now)
            total = total * jnp.exp(top - both) + part * jnp.exp(now - both)
            top = both
    tile = jnp.concatenate(
        thirds(peak * TEACHER_INV)
        + [jnp.broadcast_to(count, (1, LIVE))]
        + thirds(top + jnp.log(total))
        + [jnp.zeros((1, LIVE), f32)],
        axis=0,
    )
    out_ref[...] = jnp.broadcast_to(tile[None].astype(bf16), out_ref.shape)


def spread(tile, ref):
    ref[...] = jnp.broadcast_to(tile[None].astype(ref.dtype), ref.shape)


def expo_kernel(recv_ref, a_ref, b_ref, c_ref, d_ref, mine_ref, et_ref, srows_ref, stat_ref, pay_ref, peak_ref, live_ref):
    peaks, counts = [], []
    for x in range(4):
        for core in range(2):
            got = [recv_ref[(x * 4 + y) * 2 + core].astype(f32) for y in range(4)]
            tops = [v[0:1] + v[1:2] + v[2:3] for v in got]
            peaks.append(jnp.maximum(jnp.maximum(tops[0], tops[1]), jnp.maximum(tops[2], tops[3])))
            counts.append(got[0][3:4])
    count = jnp.concatenate(counts, axis=0)
    slot = lax.broadcasted_iota(jnp.int32, (8, 128), 1).astype(f32)
    live = jnp.where(slot < count, 1.0, 0.0)
    stat_ref[0] = live
    stat_ref[1] = live / count
    stat_ref[2] = jnp.concatenate(peaks, axis=0)
    for x in range(4):
        peak_ref[x : x + 1, :] = jnp.concatenate(peaks[2 * x : 2 * x + 2], axis=1)
        live_ref[x : x + 1, :] = jnp.concatenate([live[2 * x : 2 * x + 1], live[2 * x + 1 : 2 * x + 2]], axis=1)
    total = jnp.zeros((16, 1024), f32)
    for k, piece in enumerate((a_ref, b_ref, c_ref, d_ref)):
        x = (lax.axis_index("x") + 4 - k) & 3
        start = pl.multiple_of(x * 256, 256)
        rows = jnp.concatenate([piece[0, 0], piece[1, 0]], axis=0)
        logits = dot(mine_ref[...], rows, NT)
        block = jnp.exp(logits * TEACHER_INV - peak_ref[pl.ds(x, 1), :]).astype(bf16)
        et_ref[:, pl.ds(start, 256)] = block
        total += dot(jnp.broadcast_to(live_ref[pl.ds(x, 1), :], (16, 256)).astype(bf16), block, NT)
        for core in range(2):
            srows_ref[pl.ds(pl.multiple_of(start + core * 128, 128), 128), :] = piece[core, 1]
    spread(to_tile(total[0:1]), pay_ref)


def col_kernel(recv_ref, et_ref, *refs):
    col = 1.0 / jnp.sum(recv_ref[...].astype(f32), axis=0)
    out = jnp.sum(dot(split3(to_lanes(col)), et_ref[...], NN), axis=0, keepdims=True)
    spread(to_tile(out), refs[-1])


def last_col_kernel(recv_ref, et_ref, w_ref, pay_ref, col_ref):
    col = 1.0 / jnp.sum(recv_ref[...].astype(f32), axis=0)
    col_ref[...] = col
    lhs = split3(to_lanes(col))
    out = to_tile(jnp.sum(dot(lhs, et_ref[...], NN), axis=0, keepdims=True))
    entropy = to_tile(jnp.sum(dot(lhs, w_ref[...], NN), axis=0, keepdims=True))
    spread(jnp.concatenate([out, entropy, col], axis=0), pay_ref)


def row_kernel(recv_ref, stat_ref, et_ref, pay_ref):
    row = stat_ref[0] / jnp.sum(recv_ref[...].astype(f32), axis=0)
    out = jnp.sum(dot(split3(to_lanes(row)), et_ref[...], NT), axis=0, keepdims=True)
    spread(to_tile(out), pay_ref)


def student_prob_kernel(recv_ref, stat_ref, srows_ref, mine_ref, et_ref, prob_hbm, w_hbm, norm_ref, prob_ref, w_ref, sems):
    for image in range(8):
        got = [recv_ref[(image // 2 * 4 + y) * 2 + image % 2].astype(f32) for y in range(4)]
        parts = [v[4:5] + v[5:6] + v[6:7] for v in got]
        top = jnp.maximum(jnp.maximum(parts[0], parts[1]), jnp.maximum(parts[2], parts[3]))
        total = sum(jnp.exp(v - top) for v in parts)
        norm_ref[image : image + 1, :] = top + jnp.log(total)
    norm = to_lanes(norm_ref[...])
    coef = to_lanes(stat_ref[1]) * GRAD_FACTOR
    copies = []
    for r in range(4):
        at = slice(256 * r, 256 * (r + 1))
        log_prob = dot(mine_ref[...], srows_ref[at, :], NT) * STUDENT_INV - norm[:, at]
        prob_ref[:, at] = jnp.exp(log_prob) * coef[:, at]
        w_ref[:, at] = (et_ref[:, at].astype(f32) * log_prob).astype(bf16)
        if r % 2:
            at = (pl.ds(0, 1024), pl.ds(256 * (r - 1), 512))
            copies.append(pltpu.make_async_copy(prob_ref.at[at], prob_hbm.at[at], sems.at[r - 1]))
            copies.append(pltpu.make_async_copy(w_ref.at[at], w_hbm.at[at], sems.at[r]))
            copies[-2].start()
            copies[-1].start()
    for copy in copies:
        copy.wait()


def grad_kernel(recv_ref, stat_ref, col_ref, et_ref, prob_ref, srows_ref, pout_hbm, scale_ref, pout_ref, sems):
    sums = jnp.sum(recv_ref[...].astype(f32), axis=0)
    entropy = sums[8:16]
    row = stat_ref[0] / sums[0:8]
    weight = stat_ref[1]
    loss = -jnp.sum(jnp.sum(weight * row * entropy, axis=1, keepdims=True), axis=0, keepdims=True) / IMAGES
    hi = loss.astype(bf16).astype(f32)
    mid = (loss - hi).astype(bf16).astype(f32)
    lo = loss - hi - mid
    which = lax.broadcasted_iota(jnp.int32, (8, 128), 0)
    tail = jnp.where(which == 0, hi, jnp.where(which == 1, mid, jnp.where(which == 2, lo, 0.0))).astype(bf16)
    coef = weight * GRAD_FACTOR
    scale_ref[0] = coef
    scale_ref[1] = coef * row
    scale_rows = to_lanes(coef * row)
    copies = []
    for j in range(4):
        at = slice(256 * j, 256 * (j + 1))
        col = jnp.concatenate([jnp.broadcast_to(col_ref[i : i + 1, :], (128, 128)).T for i in (2 * j, 2 * j + 1)], axis=0)
        col = jnp.concatenate([col] * 8, axis=1)
        grad = (prob_ref[at, :] - et_ref[at, :].astype(f32) * col * scale_rows).astype(bf16)
        part = dot(grad, srows_ref[...], NN).astype(bf16)
        for i in (0, 1):
            pout_ref[2 * j + i, 0:128, :] = part[128 * i : 128 * (i + 1), 0:128]
            pout_ref[2 * j + i, 128:256, :] = part[128 * i : 128 * (i + 1), 128:256]
            pout_ref[2 * j + i, 256:264, :] = tail
        if j % 2:
            at = pl.ds(2 * j - 2, 4)
            copies.append(pltpu.make_async_copy(pout_ref.at[at], pout_hbm.at[at], sems.at[j // 2]))
            copies[-1].start()
    for copy in copies:
        copy.wait()


def column(row, wide):
    return jnp.concatenate([jnp.broadcast_to(row, (128, 128)).T] * (wide // 128), axis=1)


def own_image():
    return pl.ds(lax.axis_index("x") * 2 + lax.axis_index("c"), 1)


def own_kernel(recv_ref, scale_ref, stat_ref, norm_ref, rows_hbm, proto_hbm, out_ref, rows_ref, proto_ref, sems):
    chunks = 2
    tall = proto_ref.shape[0] // chunks
    rows_copy = pltpu.make_async_copy(rows_hbm, rows_ref, sems.at[chunks])
    copies = [
        pltpu.make_async_copy(proto_hbm.at[pl.ds(i * tall, tall)], proto_ref.at[pl.ds(i * tall, tall)], sems.at[i])
        for i in range(chunks)
    ]
    for copy in [rows_copy] + copies:
        copy.start()
    y = lax.axis_index("y")
    peak = column(stat_ref[2, own_image(), :], 1024)
    norm = column(norm_ref[own_image(), :], 1024)
    coef = column(scale_ref[0, own_image(), :], 1024)
    scale = column(scale_ref[1, own_image(), :], 1024)
    cols = [recv_ref[(x * 4 + y) * 2 + c].astype(f32)[16:24] for x in range(4) for c in range(2)]
    rows_copy.wait()
    rows = rows_ref[...].reshape(2 * LIVE, 256)
    total = jnp.zeros((LIVE, 256), f32)
    for i in range(8):
        if i % 4 == 0:
            copies[i // 4].wait()
        col = jnp.concatenate([v[i : i + 1, :] for v in cols], axis=1)
        block = proto_ref[1024 * i : 1024 * (i + 1), :]
        logits = dot(rows, block, NT)
        teach = jnp.exp(logits[0:LIVE] * TEACHER_INV - peak).astype(bf16).astype(f32)
        prob = jnp.exp(logits[LIVE:] * STUDENT_INV - norm)
        grad = (prob * coef - teach * (col * scale)).astype(bf16)
        total += dot(grad, block, NN)
    out_ref[...] = total.astype(bf16)


def place_kernel(mask_ref, a_ref, b_ref, c_ref, d_ref, student_ref):
    pick = selection(mask_ref[...]).astype(bf16)
    parts = [ref[...].astype(f32) for ref in (a_ref, b_ref, c_ref, d_ref)]
    rows = (parts[0] + parts[2]) + (parts[1] + parts[3])
    student_ref[...] = sum(dot(pick, part.astype(bf16), TN) for part in thirds(rows))


def end_kernel(recv_ref, proto_ref, loss_ref):
    total = jnp.sum(recv_ref[...].astype(f32), axis=0)
    proto_ref[:, 0:128] = total[0:128]
    proto_ref[:, 128:256] = total[128:256]
    loss_ref[...] = total[256:257] + total[257:258] + total[258:259]


VM = pl.BlockSpec(memory_space=pltpu.VMEM)


def call(kernel, out, *args, scratch=(), limit=8, cost=None):
    out = [jax.ShapeDtypeStruct(s, d) for s, d in out]
    return pl.pallas_call(
        kernel,
        out_shape=out,
        in_specs=[VM] * len(args),
        out_specs=[VM] * len(out),
        scratch_shapes=list(scratch),
        compiler_params=pltpu.CompilerParams(vmem_limit_bytes=limit << 20),
        cost_estimate=cost and pl.CostEstimate(flops=cost, bytes_accessed=1 << 20, transcendentals=1 << 20),
    )(*args)


def in_hbm(v):
    return pltpu.with_memory_space_constraint(v, pltpu.HBM)


def a2a(v, axes):
    return lax.all_to_all(v, axes, 0, 0, tiled=True)


def shift(v, axis, n, k):
    return lax.ppermute(v, axis, [(i, (i + k) % n) for i in range(n)])


PLANE = ("x", "y", "c")
HBM = pl.BlockSpec(memory_space=pl.ANY)


def local(teacher_feats, student_feats, prototypes, patch_mask):
    c = lax.axis_index("c")
    own, peak_pay, mine = pl.pallas_call(
        head_kernel,
        out_shape=[
            jax.ShapeDtypeStruct((2, LIVE, 256), bf16),
            jax.ShapeDtypeStruct((32, 8, 128), bf16),
            jax.ShapeDtypeStruct((1024, 256), bf16),
        ],
        in_specs=[HBM] * 4,
        out_specs=[VM] * 3,
        scratch_shapes=[
            pltpu.VMEM((1, 256), jnp.int32),
            pltpu.VMEM((1, 256, 256), bf16),
            pltpu.VMEM((1, 256, 256), bf16),
            pltpu.VMEM((8192, 256), bf16),
            pltpu.SemaphoreType.DMA((5,)),
        ],
        compiler_params=pltpu.CompilerParams(vmem_limit_bytes=32 << 20),
    )(*(in_hbm(v) for v in (patch_mask, teacher_feats, student_feats, prototypes)))

    other = shift(own, "c", 2, 1)
    pair = jnp.where(c == 0, jnp.stack([own, other]), jnp.stack([other, own]))
    parts = [pair] + [shift(pair, "x", 4, k) for k in (1, 2, 3)]

    peak_recv = a2a(peak_pay, PLANE)

    et, srows, stat, pay = call(
        expo_kernel,
        [((1024, 1024), bf16), ((1024, 256), bf16), ((3, 8, 128), f32), ((8, 8, 128), bf16)],
        peak_recv, *parts, mine, limit=16, scratch=[pltpu.VMEM((8, 256), f32)] * 2,
    )

    recv = a2a(pay, "z")
    (pay,) = call(col_kernel, [((32, 8, 128), bf16)], recv, et)
    recv = a2a(pay, PLANE)
    prob, w, norm = pl.pallas_call(
        student_prob_kernel,
        out_shape=[
            pltpu.HBM((1024, 1024), f32),
            pltpu.HBM((1024, 1024), bf16),
            jax.ShapeDtypeStruct((8, 128), f32),
        ],
        in_specs=[VM] * 5,
        out_specs=[pl.BlockSpec(memory_space=pltpu.HBM)] * 2 + [VM],
        scratch_shapes=[
            pltpu.VMEM((1024, 1024), f32),
            pltpu.VMEM((1024, 1024), bf16),
            pltpu.SemaphoreType.DMA((4,)),
        ],
        compiler_params=pltpu.CompilerParams(vmem_limit_bytes=24 << 20),
        cost_estimate=pl.CostEstimate(flops=1 << 29, bytes_accessed=8 << 20, transcendentals=1 << 20),
    )(peak_recv, stat, srows, mine, et)
    (pay,) = call(row_kernel, [((8, 8, 128), bf16)], recv, stat, et)
    for _ in range(BALANCING_PASSES - 2):
        recv = a2a(pay, "z")
        (pay,) = call(col_kernel, [((32, 8, 128), bf16)], recv, et, norm)
        recv = a2a(pay, PLANE)
        (pay,) = call(row_kernel, [((8, 8, 128), bf16)], recv, stat, et)
    recv = a2a(pay, "z")
    pay, col = call(last_col_kernel, [((32, 24, 128), bf16), ((8, 128), f32)], recv, et, w)
    recv = a2a(pay, PLANE)

    proto_part, scale = pl.pallas_call(
        grad_kernel,
        out_shape=[pltpu.HBM((8, 264, 128), bf16), jax.ShapeDtypeStruct((2, 8, 128), f32)],
        in_specs=[VM] * 6,
        out_specs=[pl.BlockSpec(memory_space=pltpu.HBM), VM],
        scratch_shapes=[pltpu.VMEM((8, 264, 128), bf16), pltpu.SemaphoreType.DMA((2,))],
        compiler_params=pltpu.CompilerParams(vmem_limit_bytes=24 << 20),
    )(recv, stat, col, et, prob, srows)
    proto_recv = a2a(proto_part, "z")
    student_rows = pl.pallas_call(
        own_kernel,
        out_shape=jax.ShapeDtypeStruct((LIVE, 256), bf16),
        in_specs=[VM] * 4 + [HBM] * 2,
        out_specs=VM,
        scratch_shapes=[
            pltpu.VMEM((2, LIVE, 256), bf16),
            pltpu.VMEM((8192, 256), bf16),
            pltpu.SemaphoreType.DMA((3,)),
        ],
        compiler_params=pltpu.CompilerParams(vmem_limit_bytes=24 << 20),
        cost_estimate=pl.CostEstimate(flops=1 << 31, bytes_accessed=4 << 20, transcendentals=2 << 20),
    )(recv, scale, stat, norm, in_hbm(own), in_hbm(prototypes))
    student_rows = [student_rows] + [shift(student_rows, "y", 4, k) for k in (1, 2, 3)]
    (student,) = call(place_kernel, [((256, 256), f32)], patch_mask, *student_rows, limit=16)
    proto, loss = call(end_kernel, [((128, 256), f32), ((1, 128), f32)], proto_recv, limit=16)
    return loss[0, 0], student[None], proto[None]


def solution(mesh):
    fine = Mesh(mesh.devices.reshape(8, 4, 2, 4), ("z", "x", "c", "y"))
    dp = ("z", "x", "c")
    return jax.shard_map(
        local,
        mesh=fine,
        in_specs=(P(dp, None, None), P(dp, None, None), P("y", None), P(dp, None)),
        out_specs=(P(), P(dp, None, None), P("y", dp, None)),
        check_vma=False,
    )
```

```python
import jax
import jax.numpy as jnp
from jax import lax
from jax.experimental import pallas as pl
from jax.experimental.pallas import tpu as pltpu
from jax.sharding import Mesh, PartitionSpec as P

BALANCING_PASSES = 3
LOSS_SCALE = 16384
TEACHER_INV = 1.0 / 0.07
STUDENT_INV = 1.0 / 0.1
IMAGES = 64
GRAD_FACTOR = LOSS_SCALE / (IMAGES * 0.1)
LIVE = 128
NT = (((1,), (1,)), ((), ()))
NN = (((1,), (0,)), ((), ()))
TN = (((0,), (0,)), ((), ()))
f32 = jnp.float32
bf16 = jnp.bfloat16


def dot(a, b, dims):
    return lax.dot_general(a, b, dims, preferred_element_type=f32)


def to_lanes(v):
    return jnp.concatenate([v[i : i + 1, :] for i in range(8)], axis=1)


def to_tile(v):
    return jnp.concatenate([v[:, 128 * i : 128 * (i + 1)] for i in range(8)], axis=0)


def thirds(v):
    hi = v.astype(bf16).astype(f32)
    mid = (v - hi).astype(bf16).astype(f32)
    return [hi, mid, (v - hi - mid).astype(bf16).astype(f32)]


def split3(v):
    return jnp.concatenate(thirds(v) + [jnp.zeros((13, v.shape[1]), f32)], axis=0).astype(bf16)


def selection(mask):
    patches = mask.shape[1]
    maskf = mask.astype(f32)
    before = lax.broadcasted_iota(jnp.int32, (patches, patches), 0)
    after = lax.broadcasted_iota(jnp.int32, (patches, patches), 1)
    tri = jnp.where(before <= after, 1.0, 0.0).astype(bf16)
    rank = dot(jnp.broadcast_to(maskf, (16, patches)).astype(bf16), tri, NN)[0:1, :]
    slot = lax.broadcasted_iota(jnp.int32, (LIVE, patches), 0).astype(f32)
    hit = jnp.where(rank - 1.0 == slot, 1.0, 0.0) * maskf
    return hit


def head_kernel(
    mask_hbm, teach_hbm, student_hbm, proto_hbm, own_ref, out_ref, mine_ref, mask_ref, teach_ref, student_ref, proto_ref, sems
):
    chunks = 2
    tall = proto_ref.shape[0] // chunks
    small = ((mask_hbm, mask_ref), (teach_hbm, teach_ref), (student_hbm, student_ref))
    first = [pltpu.make_async_copy(src, dst, sems.at[chunks + i]) for i, (src, dst) in enumerate(small)]
    copies = [
        pltpu.make_async_copy(proto_hbm.at[pl.ds(i * tall, tall)], proto_ref.at[pl.ds(i * tall, tall)], sems.at[i])
        for i in range(chunks)
    ]
    for copy in first + copies:
        copy.start()
    image = lax.axis_index("x") * 2 + lax.axis_index("c")
    first[0].wait()
    pick = selection(mask_ref[...]).astype(bf16)
    count = jnp.sum(mask_ref[...].astype(f32), axis=1, keepdims=True)
    first[1].wait()
    own_ref[0] = dot(pick, teach_ref[0], NN).astype(bf16)
    first[2].wait()
    own_ref[1] = dot(pick, student_ref[0], NN).astype(bf16)
    rows = own_ref[...].reshape(2 * LIVE, 256)
    peak = top = total = None
    for i in range(0, 8192, 512):
        if i % tall == 0:
            copies[i // tall].wait()
        if i % 1024 == 0:
            at = pl.multiple_of(i + image * 128, 128)
            mine_ref[i // 8 : i // 8 + 128, :] = proto_ref[pl.ds(at, 128), :]
        low = dot(proto_ref[i : i + 256, :], rows, NT)
        high = dot(proto_ref[i + 256 : i + 512, :], rows, NT)
        teach = jnp.max(jnp.maximum(low[:, :LIVE], high[:, :LIVE]), axis=0, keepdims=True)
        student = jnp.concatenate([low[:, LIVE:], high[:, LIVE:]], axis=0) * STUDENT_INV
        now = jnp.max(student, axis=0, keepdims=True)
        part = jnp.sum(jnp.exp(student - now), axis=0, keepdims=True)
        if peak is None:
            peak, top, total = teach, now, part
        else:
            peak, both = jnp.maximum(peak, teach), jnp.maximum(top, now)
            total = total * jnp.exp(top - both) + part * jnp.exp(now - both)
            top = both
    tile = jnp.concatenate(
        thirds(peak * TEACHER_INV)
        + [jnp.broadcast_to(count, (1, LIVE))]
        + thirds(top + jnp.log(total))
        + [jnp.zeros((1, LIVE), f32)],
        axis=0,
    )
    out_ref[...] = jnp.broadcast_to(tile[None].astype(bf16), out_ref.shape)


def spread(tile, ref):
    ref[...] = jnp.broadcast_to(tile[None].astype(ref.dtype), ref.shape)


def expo_kernel(recv_ref, *refs):
    pieces, (mine_ref, et_ref, srows_ref, stat_ref, pay_ref, trows_ref) = refs[:8], refs[8:]
    peaks, counts = [], []
    for x in range(4):
        for core in range(2):
            got = [recv_ref[(x * 4 + y) * 2 + core].astype(f32) for y in range(4)]
            tops = [v[0:1] + v[1:2] + v[2:3] for v in got]
            peaks.append(jnp.maximum(jnp.maximum(tops[0], tops[1]), jnp.maximum(tops[2], tops[3])))
            counts.append(got[0][3:4])
    count = jnp.concatenate(counts, axis=0)
    slot = lax.broadcasted_iota(jnp.int32, (8, 128), 1).astype(f32)
    live = jnp.where(slot < count, 1.0, 0.0)
    stat_ref[0] = live
    stat_ref[1] = live / count
    stat_ref[2] = jnp.concatenate(peaks, axis=0)
    peak = jnp.concatenate(peaks, axis=1)
    live_rows = jnp.broadcast_to(to_lanes(live), (16, 1024)).astype(bf16)
    here = lax.axis_index("c")
    for k in range(4):
        x = (lax.axis_index("x") + 4 - k) & 3
        for core, piece in ((here, pieces[2 * k]), (1 - here, pieces[2 * k + 1])):
            at = pl.ds(pl.multiple_of(x * 256 + core * 128, 128), 128)
            trows_ref[at, :] = piece[0]
            srows_ref[at, :] = piece[1]
    sums = [jnp.zeros((16, 512), f32)] * 2
    for r in range(4):
        at = slice(256 * r, 256 * (r + 1))
        for j in range(2):
            logits = dot(mine_ref[512 * j : 512 * (j + 1), :], trows_ref[at, :], NT)
            block = jnp.exp(logits * TEACHER_INV - peak[:, at]).astype(bf16)
            et_ref[512 * j : 512 * (j + 1), at] = block
            sums[j] += dot(live_rows[:, at], block, NT)
    spread(to_tile(jnp.concatenate(sums, axis=1)[0:1]), pay_ref)


def col_kernel(recv_ref, et_ref, *refs):
    col = 1.0 / jnp.sum(recv_ref[...].astype(f32), axis=0)
    out = jnp.sum(dot(split3(to_lanes(col)), et_ref[...], NN), axis=0, keepdims=True)
    spread(to_tile(out), refs[-1])


def last_col_kernel(recv_ref, et_ref, w_ref, pay_ref, col_ref):
    col = 1.0 / jnp.sum(recv_ref[...].astype(f32), axis=0)
    col_ref[...] = col
    lhs = split3(to_lanes(col))
    out = to_tile(jnp.sum(dot(lhs, et_ref[...], NN), axis=0, keepdims=True))
    entropy = to_tile(jnp.sum(dot(lhs, w_ref[...], NN), axis=0, keepdims=True))
    spread(jnp.concatenate([out, entropy, col], axis=0), pay_ref)


def row_kernel(recv_ref, stat_ref, et_ref, pay_ref):
    row = stat_ref[0] / jnp.sum(recv_ref[...].astype(f32), axis=0)
    out = jnp.sum(dot(split3(to_lanes(row)), et_ref[...], NT), axis=0, keepdims=True)
    spread(to_tile(out), pay_ref)


def student_prob_kernel(recv_ref, stat_ref, srows_ref, mine_ref, et_ref, prob_hbm, w_hbm, norm_ref, prob_ref, w_ref, sems):
    for image in range(8):
        got = [recv_ref[(image // 2 * 4 + y) * 2 + image % 2].astype(f32) for y in range(4)]
        parts = [v[4:5] + v[5:6] + v[6:7] for v in got]
        top = jnp.maximum(jnp.maximum(parts[0], parts[1]), jnp.maximum(parts[2], parts[3]))
        total = sum(jnp.exp(v - top) for v in parts)
        norm_ref[image : image + 1, :] = top + jnp.log(total)
    norm = to_lanes(norm_ref[...])
    coef = to_lanes(stat_ref[1]) * GRAD_FACTOR
    copies = []
    for r in range(4):
        at = slice(256 * r, 256 * (r + 1))
        log_prob = dot(mine_ref[...], srows_ref[at, :], NT) * STUDENT_INV - norm[:, at]
        prob_ref[:, at] = jnp.exp(log_prob) * coef[:, at]
        w_ref[:, at] = (et_ref[:, at].astype(f32) * log_prob).astype(bf16)
        if r % 2:
            at = (pl.ds(0, 1024), pl.ds(256 * (r - 1), 512))
            copies.append(pltpu.make_async_copy(prob_ref.at[at], prob_hbm.at[at], sems.at[r - 1]))
            copies.append(pltpu.make_async_copy(w_ref.at[at], w_hbm.at[at], sems.at[r]))
            copies[-2].start()
            copies[-1].start()
    for copy in copies:
        copy.wait()


def grad_kernel(recv_ref, stat_ref, col_ref, et_ref, prob_ref, srows_ref, pout_hbm, scale_ref, pout_ref, sems):
    sums = jnp.sum(recv_ref[...].astype(f32), axis=0)
    entropy = sums[8:16]
    row = stat_ref[0] / sums[0:8]
    weight = stat_ref[1]
    loss = -jnp.sum(jnp.sum(weight * row * entropy, axis=1, keepdims=True), axis=0, keepdims=True) / IMAGES
    hi = loss.astype(bf16).astype(f32)
    mid = (loss - hi).astype(bf16).astype(f32)
    lo = loss - hi - mid
    which = lax.broadcasted_iota(jnp.int32, (8, 128), 0)
    tail = jnp.where(which == 0, hi, jnp.where(which == 1, mid, jnp.where(which == 2, lo, 0.0))).astype(bf16)
    coef = weight * GRAD_FACTOR
    scale_ref[0] = coef
    scale_ref[1] = coef * row
    scale_rows = to_lanes(coef * row)
    copies = []
    for j in range(4):
        at = slice(256 * j, 256 * (j + 1))
        col = jnp.concatenate([jnp.broadcast_to(col_ref[i : i + 1, :], (128, 128)).T for i in (2 * j, 2 * j + 1)], axis=0)
        col = jnp.concatenate([col] * 8, axis=1)
        grad = (prob_ref[at, :] - et_ref[at, :].astype(f32) * col * scale_rows).astype(bf16)
        part = dot(grad, srows_ref[...], NN).astype(bf16)
        for i in (0, 1):
            pout_ref[2 * j + i, 0:128, :] = part[128 * i : 128 * (i + 1), 0:128]
            pout_ref[2 * j + i, 128:256, :] = part[128 * i : 128 * (i + 1), 128:256]
            pout_ref[2 * j + i, 256:264, :] = tail
        if j % 2:
            at = pl.ds(2 * j - 2, 4)
            copies.append(pltpu.make_async_copy(pout_ref.at[at], pout_hbm.at[at], sems.at[j // 2]))
            copies[-1].start()
    for copy in copies:
        copy.wait()


def column(row, wide):
    return jnp.concatenate([jnp.broadcast_to(row, (128, 128)).T] * (wide // 128), axis=1)


def own_image():
    return pl.ds(lax.axis_index("x") * 2 + lax.axis_index("c"), 1)


def own_kernel(recv_ref, scale_ref, stat_ref, norm_ref, rows_hbm, proto_hbm, out_ref, rows_ref, proto_ref, sems):
    chunks = 2
    tall = proto_ref.shape[0] // chunks
    rows_copy = pltpu.make_async_copy(rows_hbm, rows_ref, sems.at[chunks])
    copies = [
        pltpu.make_async_copy(proto_hbm.at[pl.ds(i * tall, tall)], proto_ref.at[pl.ds(i * tall, tall)], sems.at[i])
        for i in range(chunks)
    ]
    for copy in [rows_copy] + copies:
        copy.start()
    y = lax.axis_index("y")
    peak = column(stat_ref[2, own_image(), :], 1024)
    norm = column(norm_ref[own_image(), :], 1024)
    coef = column(scale_ref[0, own_image(), :], 1024)
    scale = column(scale_ref[1, own_image(), :], 1024)
    cols = [recv_ref[(x * 4 + y) * 2 + c].astype(f32)[16:24] for x in range(4) for c in range(2)]
    rows_copy.wait()
    rows = rows_ref[...].reshape(2 * LIVE, 256)
    total = jnp.zeros((LIVE, 256), f32)
    for i in range(8):
        if i % 4 == 0:
            copies[i // 4].wait()
        col = jnp.concatenate([v[i : i + 1, :] for v in cols], axis=1)
        block = proto_ref[1024 * i : 1024 * (i + 1), :]
        logits = dot(rows, block, NT)
        teach = jnp.exp(logits[0:LIVE] * TEACHER_INV - peak).astype(bf16).astype(f32)
        prob = jnp.exp(logits[LIVE:] * STUDENT_INV - norm)
        grad = (prob * coef - teach * (col * scale)).astype(bf16)
        total += dot(grad, block, NN)
    out_ref[...] = total.astype(bf16)


def place_kernel(mask_ref, a_ref, b_ref, c_ref, d_ref, student_ref):
    pick = selection(mask_ref[...]).astype(bf16)
    parts = [ref[...].astype(f32) for ref in (a_ref, b_ref, c_ref, d_ref)]
    rows = (parts[0] + parts[2]) + (parts[1] + parts[3])
    student_ref[...] = sum(dot(pick, part.astype(bf16), TN) for part in thirds(rows))


def end_kernel(recv_ref, proto_ref, loss_ref):
    total = jnp.sum(recv_ref[...].astype(f32), axis=0)
    proto_ref[:, 0:128] = total[0:128]
    proto_ref[:, 128:256] = total[128:256]
    loss_ref[...] = total[256:257] + total[257:258] + total[258:259]


VM = pl.BlockSpec(memory_space=pltpu.VMEM)


def call(kernel, out, *args, scratch=(), limit=8, cost=None):
    out = [jax.ShapeDtypeStruct(s, d) for s, d in out]
    return pl.pallas_call(
        kernel,
        out_shape=out,
        in_specs=[VM] * len(args),
        out_specs=[VM] * len(out),
        scratch_shapes=list(scratch),
        compiler_params=pltpu.CompilerParams(vmem_limit_bytes=limit << 20),
        cost_estimate=cost and pl.CostEstimate(flops=cost, bytes_accessed=1 << 20, transcendentals=1 << 20),
    )(*args)


def in_hbm(v):
    return pltpu.with_memory_space_constraint(v, pltpu.HBM)


def a2a(v, axes):
    return lax.all_to_all(v, axes, 0, 0, tiled=True)


def shift(v, axis, n, k):
    return lax.ppermute(v, axis, [(i, (i + k) % n) for i in range(n)])


PLANE = ("x", "y", "c")
HBM = pl.BlockSpec(memory_space=pl.ANY)


def local(teacher_feats, student_feats, prototypes, patch_mask):
    own, peak_pay, mine = pl.pallas_call(
        head_kernel,
        out_shape=[
            jax.ShapeDtypeStruct((2, LIVE, 256), bf16),
            jax.ShapeDtypeStruct((32, 8, 128), bf16),
            jax.ShapeDtypeStruct((1024, 256), bf16),
        ],
        in_specs=[HBM] * 4,
        out_specs=[VM] * 3,
        scratch_shapes=[
            pltpu.VMEM((1, 256), jnp.int32),
            pltpu.VMEM((1, 256, 256), bf16),
            pltpu.VMEM((1, 256, 256), bf16),
            pltpu.VMEM((8192, 256), bf16),
            pltpu.SemaphoreType.DMA((5,)),
        ],
        compiler_params=pltpu.CompilerParams(vmem_limit_bytes=32 << 20),
    )(*(in_hbm(v) for v in (patch_mask, teacher_feats, student_feats, prototypes)))

    parts = [own] + [shift(own, "x", 4, k) for k in (1, 2, 3)]
    peak_recv = a2a(peak_pay, PLANE)
    peak_recv, *parts = lax.optimization_barrier((peak_recv, *parts))
    pieces = [v for part in parts for v in (part, shift(part, "c", 2, 1))]

    et, srows, stat, pay = call(
        expo_kernel,
        [((1024, 1024), bf16), ((1024, 256), bf16), ((3, 8, 128), f32), ((8, 8, 128), bf16)],
        peak_recv, *pieces, mine, limit=16, scratch=[pltpu.VMEM((1024, 256), bf16)],
    )

    recv = a2a(pay, "z")
    (pay,) = call(col_kernel, [((32, 8, 128), bf16)], recv, et)
    recv = a2a(pay, PLANE)
    prob, w, norm = pl.pallas_call(
        student_prob_kernel,
        out_shape=[
            pltpu.HBM((1024, 1024), f32),
            pltpu.HBM((1024, 1024), bf16),
            jax.ShapeDtypeStruct((8, 128), f32),
        ],
        in_specs=[VM] * 5,
        out_specs=[pl.BlockSpec(memory_space=pltpu.HBM)] * 2 + [VM],
        scratch_shapes=[
            pltpu.VMEM((1024, 1024), f32),
            pltpu.VMEM((1024, 1024), bf16),
            pltpu.SemaphoreType.DMA((4,)),
        ],
        compiler_params=pltpu.CompilerParams(vmem_limit_bytes=24 << 20),
        cost_estimate=pl.CostEstimate(flops=1 << 29, bytes_accessed=8 << 20, transcendentals=1 << 20),
    )(peak_recv, stat, srows, mine, et)
    (pay,) = call(row_kernel, [((8, 8, 128), bf16)], recv, stat, et)
    for _ in range(BALANCING_PASSES - 2):
        recv = a2a(pay, "z")
        (pay,) = call(col_kernel, [((32, 8, 128), bf16)], recv, et, norm)
        recv = a2a(pay, PLANE)
        (pay,) = call(row_kernel, [((8, 8, 128), bf16)], recv, stat, et)
    recv = a2a(pay, "z")
    pay, col = call(last_col_kernel, [((32, 24, 128), bf16), ((8, 128), f32)], recv, et, w)
    recv = a2a(pay, PLANE)

    proto_part, scale = pl.pallas_call(
        grad_kernel,
        out_shape=[pltpu.HBM((8, 264, 128), bf16), jax.ShapeDtypeStruct((2, 8, 128), f32)],
        in_specs=[VM] * 6,
        out_specs=[pl.BlockSpec(memory_space=pltpu.HBM), VM],
        scratch_shapes=[pltpu.VMEM((8, 264, 128), bf16), pltpu.SemaphoreType.DMA((2,))],
        compiler_params=pltpu.CompilerParams(vmem_limit_bytes=24 << 20),
    )(recv, stat, col, et, prob, srows)
    proto_recv = a2a(proto_part, "z")
    student_rows = pl.pallas_call(
        own_kernel,
        out_shape=jax.ShapeDtypeStruct((LIVE, 256), bf16),
        in_specs=[VM] * 4 + [HBM] * 2,
        out_specs=VM,
        scratch_shapes=[
            pltpu.VMEM((2, LIVE, 256), bf16),
            pltpu.VMEM((8192, 256), bf16),
            pltpu.SemaphoreType.DMA((3,)),
        ],
        compiler_params=pltpu.CompilerParams(vmem_limit_bytes=24 << 20),
        cost_estimate=pl.CostEstimate(flops=1 << 31, bytes_accessed=4 << 20, transcendentals=2 << 20),
    )(recv, scale, stat, norm, in_hbm(own), in_hbm(prototypes))
    student_rows = [student_rows] + [shift(student_rows, "y", 4, k) for k in (1, 2, 3)]
    (student,) = call(place_kernel, [((256, 256), f32)], patch_mask, *student_rows, limit=16)
    proto, loss = call(end_kernel, [((128, 256), f32), ((1, 128), f32)], proto_recv, limit=16)
    return loss[0, 0], student[None], proto[None]


def solution(mesh):
    fine = Mesh(mesh.devices.reshape(8, 4, 2, 4), ("z", "x", "c", "y"))
    dp = ("z", "x", "c")
    return jax.shard_map(
        local,
        mesh=fine,
        in_specs=(P(dp, None, None), P(dp, None, None), P("y", None), P(dp, None)),
        out_specs=(P(), P(dp, None, None), P("y", dp, None)),
        check_vma=False,
    )
```

```python
import jax
import jax.numpy as jnp
from jax import lax
from jax.experimental import pallas as pl
from jax.experimental.pallas import tpu as pltpu
from jax.sharding import Mesh, PartitionSpec as P

BALANCING_PASSES = 3
LOSS_SCALE = 16384
TEACHER_INV = 1.0 / 0.07
STUDENT_INV = 1.0 / 0.1
IMAGES = 64
GRAD_FACTOR = LOSS_SCALE / (IMAGES * 0.1)
LIVE = 128
NT = (((1,), (1,)), ((), ()))
NN = (((1,), (0,)), ((), ()))
TN = (((0,), (0,)), ((), ()))
f32 = jnp.float32
bf16 = jnp.bfloat16


def dot(a, b, dims):
    return lax.dot_general(a, b, dims, preferred_element_type=f32)


def to_lanes(v):
    return jnp.concatenate([v[i : i + 1, :] for i in range(8)], axis=1)


def to_tile(v):
    return jnp.concatenate([v[:, 128 * i : 128 * (i + 1)] for i in range(8)], axis=0)


def halves(tile):
    even, odd = (jnp.concatenate([tile[i : i + 1] for i in range(start, 8, 2)], axis=1) for start in (0, 1))
    first = lax.axis_index("c") == 0
    return jnp.where(first, even, odd), jnp.where(first, odd, even)


def join(own, other):
    first = lax.axis_index("c") == 0
    even, odd = jnp.where(first, own, other), jnp.where(first, other, own)
    return jnp.concatenate([v[:, 128 * x : 128 * (x + 1)] for x in range(4) for v in (even, odd)], axis=0)


def thirds(v):
    hi = v.astype(bf16).astype(f32)
    mid = (v - hi).astype(bf16).astype(f32)
    return [hi, mid, (v - hi - mid).astype(bf16).astype(f32)]


def split3(v):
    return jnp.concatenate(thirds(v) + [jnp.zeros((13, v.shape[1]), f32)], axis=0).astype(bf16)


def selection(mask):
    patches = mask.shape[1]
    maskf = mask.astype(f32)
    before = lax.broadcasted_iota(jnp.int32, (patches, patches), 0)
    after = lax.broadcasted_iota(jnp.int32, (patches, patches), 1)
    tri = jnp.where(before <= after, 1.0, 0.0).astype(bf16)
    rank = dot(jnp.broadcast_to(maskf, (16, patches)).astype(bf16), tri, NN)[0:1, :]
    slot = lax.broadcasted_iota(jnp.int32, (LIVE, patches), 0).astype(f32)
    hit = jnp.where(rank - 1.0 == slot, 1.0, 0.0) * maskf
    return hit


def head_kernel(
    mask_hbm, teach_hbm, student_hbm, proto_hbm, own_ref, out_ref, mine_ref, mask_ref, teach_ref, student_ref, proto_ref, sems
):
    chunks = 2
    tall = proto_ref.shape[0] // chunks
    small = ((mask_hbm, mask_ref), (teach_hbm, teach_ref), (student_hbm, student_ref))
    first = [pltpu.make_async_copy(src, dst, sems.at[chunks + i]) for i, (src, dst) in enumerate(small)]
    copies = [
        pltpu.make_async_copy(proto_hbm.at[pl.ds(i * tall, tall)], proto_ref.at[pl.ds(i * tall, tall)], sems.at[i])
        for i in range(chunks)
    ]
    for copy in first + copies:
        copy.start()
    image = lax.axis_index("x") * 2 + lax.axis_index("c")
    first[0].wait()
    pick = selection(mask_ref[...]).astype(bf16)
    count = jnp.sum(mask_ref[...].astype(f32), axis=1, keepdims=True)
    first[1].wait()
    own_ref[0] = dot(pick, teach_ref[0], NN).astype(bf16)
    first[2].wait()
    own_ref[1] = dot(pick, student_ref[0], NN).astype(bf16)
    rows = own_ref[...].reshape(2 * LIVE, 256)
    peak = top = total = None
    for i in range(0, 8192, 512):
        if i % tall == 0:
            copies[i // tall].wait()
        if i % 1024 == 0:
            at = pl.multiple_of(i + image * 128, 128)
            mine_ref[i // 8 : i // 8 + 128, :] = proto_ref[pl.ds(at, 128), :]
        low = dot(proto_ref[i : i + 256, :], rows, NT)
        high = dot(proto_ref[i + 256 : i + 512, :], rows, NT)
        teach = jnp.max(jnp.maximum(low[:, :LIVE], high[:, :LIVE]), axis=0, keepdims=True)
        student = jnp.concatenate([low[:, LIVE:], high[:, LIVE:]], axis=0) * STUDENT_INV
        now = jnp.max(student, axis=0, keepdims=True)
        part = jnp.sum(jnp.exp(student - now), axis=0, keepdims=True)
        if peak is None:
            peak, top, total = teach, now, part
        else:
            peak, both = jnp.maximum(peak, teach), jnp.maximum(top, now)
            total = total * jnp.exp(top - both) + part * jnp.exp(now - both)
            top = both
    tile = jnp.concatenate(
        thirds(peak * TEACHER_INV)
        + [jnp.broadcast_to(count, (1, LIVE))]
        + thirds(top + jnp.log(total))
        + [jnp.zeros((1, LIVE), f32)],
        axis=0,
    )
    out_ref[...] = jnp.broadcast_to(tile[None].astype(bf16), out_ref.shape)


def spread(tile, ref):
    ref[...] = jnp.broadcast_to(tile[None].astype(ref.dtype), ref.shape)


def order_kernel(recv_ref, a_ref, b_ref, c_ref, d_ref, teach_ref, student_ref):
    for k, piece in enumerate((a_ref, b_ref, c_ref, d_ref)):
        x = (lax.axis_index("x") + 4 - k) & 3
        teach_ref[x] = piece[0]
        student_ref[x] = piece[1]


def expo_half(rows_ref, mine_ref, et_ref, peak, live, sums):
    for r in range(2):
        at = slice(256 * r, 256 * (r + 1))
        rows = rows_ref[2 * r : 2 * r + 2].reshape(256, 256)
        weights = jnp.broadcast_to(live[:, at], (16, 256)).astype(bf16)
        for j in range(2):
            logits = dot(mine_ref[512 * j : 512 * (j + 1), :], rows, NT)
            block = jnp.exp(logits * TEACHER_INV - peak[:, at]).astype(bf16)
            et_ref[512 * j : 512 * (j + 1), at] = block
            sums[j] += dot(weights, block, NT)


def expo_own_kernel(recv_ref, rows_ref, mine_ref, et_ref, stat_ref, sum_ref):
    peaks, counts = [], []
    for x in range(4):
        for core in range(2):
            got = [recv_ref[(x * 4 + y) * 2 + core].astype(f32) for y in range(4)]
            tops = [v[0:1] + v[1:2] + v[2:3] for v in got]
            peaks.append(jnp.maximum(jnp.maximum(tops[0], tops[1]), jnp.maximum(tops[2], tops[3])))
            counts.append(got[0][3:4])
    peak = jnp.concatenate(peaks, axis=0)
    count = jnp.concatenate(counts, axis=0)
    slot = lax.broadcasted_iota(jnp.int32, (8, 128), 1).astype(f32)
    live = jnp.where(slot < count, 1.0, 0.0)
    stat_ref[0] = live
    stat_ref[1] = live / count
    stat_ref[2] = peak
    sums = [jnp.zeros((16, 512), f32)] * 2
    expo_half(rows_ref, mine_ref, et_ref, halves(peak)[0], halves(live)[0], sums)
    sum_ref[...] = jnp.concatenate(sums, axis=1)


def expo_other_kernel(stat_ref, sum_ref, rows_ref, mine_ref, et_ref, pay_ref):
    sums = [sum_ref[:, 0:512], sum_ref[:, 512:1024]]
    expo_half(rows_ref, mine_ref, et_ref, halves(stat_ref[2])[1], halves(stat_ref[0])[1], sums)
    spread(to_tile(jnp.concatenate(sums, axis=1)[0:1]), pay_ref)


def over_columns(lhs, own_ref, other_ref):
    parts = [jnp.sum(dot(lhs, ref[...], NN), axis=0, keepdims=True) for ref in (own_ref, other_ref)]
    return join(*parts)


def col_kernel(recv_ref, own_ref, other_ref, *refs):
    col = 1.0 / jnp.sum(recv_ref[...].astype(f32), axis=0)
    spread(over_columns(split3(to_lanes(col)), own_ref, other_ref), refs[-1])


def last_col_kernel(recv_ref, own_ref, other_ref, w_ref, pay_ref, col_ref):
    col = 1.0 / jnp.sum(recv_ref[...].astype(f32), axis=0)
    col_ref[...] = col
    lhs = split3(to_lanes(col))
    out = over_columns(lhs, own_ref, other_ref)
    entropy = jnp.sum(dot(lhs, w_ref[...], NN), axis=0, keepdims=True)
    spread(jnp.concatenate([out, join(entropy[:, :512], entropy[:, 512:]), col], axis=0), pay_ref)


def row_kernel(recv_ref, stat_ref, own_ref, other_ref, pay_ref):
    row = stat_ref[0] / jnp.sum(recv_ref[...].astype(f32), axis=0)
    parts = [dot(split3(v), ref[...], NT) for v, ref in zip(halves(row), (own_ref, other_ref))]
    spread(to_tile(jnp.sum(parts[0] + parts[1], axis=0, keepdims=True)), pay_ref)


def student_prob_kernel(
    recv_ref, stat_ref, sown_ref, sother_ref, mine_ref, own_ref, other_ref, prob_hbm, w_hbm, norm_ref, prob_ref, w_ref, sems
):
    for image in range(8):
        got = [recv_ref[(image // 2 * 4 + y) * 2 + image % 2].astype(f32) for y in range(4)]
        parts = [v[4:5] + v[5:6] + v[6:7] for v in got]
        top = jnp.maximum(jnp.maximum(parts[0], parts[1]), jnp.maximum(parts[2], parts[3]))
        total = sum(jnp.exp(v - top) for v in parts)
        norm_ref[image : image + 1, :] = top + jnp.log(total)
    norm = jnp.concatenate(halves(norm_ref[...]), axis=1)
    coef = jnp.concatenate(halves(stat_ref[1]), axis=1) * GRAD_FACTOR
    copies = []
    for r in range(4):
        at = slice(256 * r, 256 * (r + 1))
        rows_ref, et_ref = ((sown_ref, own_ref), (sother_ref, other_ref))[r // 2]
        rows = rows_ref[2 * (r % 2) : 2 * (r % 2) + 2].reshape(256, 256)
        log_prob = dot(mine_ref[...], rows, NT) * STUDENT_INV - norm[:, at]
        prob_ref[:, at] = jnp.exp(log_prob) * coef[:, at]
        here = slice(256 * (r % 2), 256 * (r % 2) + 256)
        w_ref[:, at] = (et_ref[:, here].astype(f32) * log_prob).astype(bf16)
        if r % 2:
            at = (pl.ds(0, 1024), pl.ds(256 * (r - 1), 512))
            copies.append(pltpu.make_async_copy(prob_ref.at[at], prob_hbm.at[at], sems.at[r - 1]))
            copies.append(pltpu.make_async_copy(w_ref.at[at], w_hbm.at[at], sems.at[r]))
            copies[-2].start()
            copies[-1].start()
    for copy in copies:
        copy.wait()


def grad_kernel(
    recv_ref, stat_ref, col_ref, own_ref, other_ref, prob_ref, sown_ref, sother_ref, pout_hbm, scale_ref, pout_ref, sems
):
    sums = jnp.sum(recv_ref[...].astype(f32), axis=0)
    entropy = sums[8:16]
    row = stat_ref[0] / sums[0:8]
    weight = stat_ref[1]
    loss = -jnp.sum(jnp.sum(weight * row * entropy, axis=1, keepdims=True), axis=0, keepdims=True) / IMAGES
    hi = loss.astype(bf16).astype(f32)
    mid = (loss - hi).astype(bf16).astype(f32)
    lo = loss - hi - mid
    which = lax.broadcasted_iota(jnp.int32, (8, 128), 0)
    tail = jnp.where(which == 0, hi, jnp.where(which == 1, mid, jnp.where(which == 2, lo, 0.0))).astype(bf16)
    coef = weight * GRAD_FACTOR
    scale_ref[0] = coef
    scale_ref[1] = coef * row
    scale_rows = jnp.concatenate(halves(coef * row), axis=1)
    sown, sother = sown_ref[...].reshape(512, 256), sother_ref[...].reshape(512, 256)
    copies = []
    for j in range(4):
        at = slice(256 * j, 256 * (j + 1))
        col = jnp.concatenate([jnp.broadcast_to(col_ref[i : i + 1, :], (128, 128)).T for i in (2 * j, 2 * j + 1)], axis=0)
        col = jnp.concatenate([col] * 8, axis=1)
        teach = jnp.concatenate([own_ref[at, :], other_ref[at, :]], axis=1).astype(f32)
        grad = (prob_ref[at, :] - teach * col * scale_rows).astype(bf16)
        part = (dot(grad[:, :512], sown, NN) + dot(grad[:, 512:], sother, NN)).astype(bf16)
        for i in (0, 1):
            pout_ref[2 * j + i, 0:128, :] = part[128 * i : 128 * (i + 1), 0:128]
            pout_ref[2 * j + i, 128:256, :] = part[128 * i : 128 * (i + 1), 128:256]
            pout_ref[2 * j + i, 256:264, :] = tail
        if j % 2:
            at = pl.ds(2 * j - 2, 4)
            copies.append(pltpu.make_async_copy(pout_ref.at[at], pout_hbm.at[at], sems.at[j // 2]))
            copies[-1].start()
    for copy in copies:
        copy.wait()


def column(row, wide):
    return jnp.concatenate([jnp.broadcast_to(row, (128, 128)).T] * (wide // 128), axis=1)


def own_image():
    return pl.ds(lax.axis_index("x") * 2 + lax.axis_index("c"), 1)


def own_kernel(recv_ref, scale_ref, stat_ref, norm_ref, rows_hbm, proto_hbm, out_ref, rows_ref, proto_ref, sems):
    chunks = 2
    tall = proto_ref.shape[0] // chunks
    rows_copy = pltpu.make_async_copy(rows_hbm, rows_ref, sems.at[chunks])
    copies = [
        pltpu.make_async_copy(proto_hbm.at[pl.ds(i * tall, tall)], proto_ref.at[pl.ds(i * tall, tall)], sems.at[i])
        for i in range(chunks)
    ]
    for copy in [rows_copy] + copies:
        copy.start()
    y = lax.axis_index("y")
    peak = column(stat_ref[2, own_image(), :], 1024)
    norm = column(norm_ref[own_image(), :], 1024)
    coef = column(scale_ref[0, own_image(), :], 1024)
    scale = column(scale_ref[1, own_image(), :], 1024)
    cols = [recv_ref[(x * 4 + y) * 2 + c].astype(f32)[16:24] for x in range(4) for c in range(2)]
    rows_copy.wait()
    rows = rows_ref[...].reshape(2 * LIVE, 256)
    total = jnp.zeros((LIVE, 256), f32)
    for i in range(8):
        if i % 4 == 0:
            copies[i // 4].wait()
        col = jnp.concatenate([v[i : i + 1, :] for v in cols], axis=1)
        block = proto_ref[1024 * i : 1024 * (i + 1), :]
        logits = dot(rows, block, NT)
        teach = jnp.exp(logits[0:LIVE] * TEACHER_INV - peak).astype(bf16).astype(f32)
        prob = jnp.exp(logits[LIVE:] * STUDENT_INV - norm)
        grad = (prob * coef - teach * (col * scale)).astype(bf16)
        total += dot(grad, block, NN)
    out_ref[...] = total.astype(bf16)


def place_kernel(mask_ref, a_ref, b_ref, c_ref, d_ref, student_ref):
    pick = selection(mask_ref[...]).astype(bf16)
    parts = [ref[...].astype(f32) for ref in (a_ref, b_ref, c_ref, d_ref)]
    rows = (parts[0] + parts[2]) + (parts[1] + parts[3])
    student_ref[...] = sum(dot(pick, part.astype(bf16), TN) for part in thirds(rows))


def end_kernel(recv_ref, proto_ref, loss_ref):
    total = jnp.sum(recv_ref[...].astype(f32), axis=0)
    proto_ref[:, 0:128] = total[0:128]
    proto_ref[:, 128:256] = total[128:256]
    loss_ref[...] = total[256:257] + total[257:258] + total[258:259]


VM = pl.BlockSpec(memory_space=pltpu.VMEM)


def call(kernel, out, *args, scratch=(), limit=8, cost=None):
    out = [jax.ShapeDtypeStruct(s, d) for s, d in out]
    return pl.pallas_call(
        kernel,
        out_shape=out,
        in_specs=[VM] * len(args),
        out_specs=[VM] * len(out),
        scratch_shapes=list(scratch),
        compiler_params=pltpu.CompilerParams(vmem_limit_bytes=limit << 20),
        cost_estimate=cost and pl.CostEstimate(flops=cost, bytes_accessed=1 << 20, transcendentals=1 << 20),
    )(*args)


def in_hbm(v):
    return pltpu.with_memory_space_constraint(v, pltpu.HBM)


def a2a(v, axes):
    return lax.all_to_all(v, axes, 0, 0, tiled=True)


def shift(v, axis, n, k):
    return lax.ppermute(v, axis, [(i, (i + k) % n) for i in range(n)])


PLANE = ("x", "y", "c")
HBM = pl.BlockSpec(memory_space=pl.ANY)


def local(teacher_feats, student_feats, prototypes, patch_mask):
    own, peak_pay, mine = pl.pallas_call(
        head_kernel,
        out_shape=[
            jax.ShapeDtypeStruct((2, LIVE, 256), bf16),
            jax.ShapeDtypeStruct((32, 8, 128), bf16),
            jax.ShapeDtypeStruct((1024, 256), bf16),
        ],
        in_specs=[HBM] * 4,
        out_specs=[VM] * 3,
        scratch_shapes=[
            pltpu.VMEM((1, 256), jnp.int32),
            pltpu.VMEM((1, 256, 256), bf16),
            pltpu.VMEM((1, 256, 256), bf16),
            pltpu.VMEM((8192, 256), bf16),
            pltpu.SemaphoreType.DMA((5,)),
        ],
        compiler_params=pltpu.CompilerParams(vmem_limit_bytes=32 << 20),
    )(*(in_hbm(v) for v in (patch_mask, teacher_feats, student_feats, prototypes)))

    parts = [own] + [shift(own, "x", 4, k) for k in (1, 2, 3)]
    peak_recv = a2a(peak_pay, PLANE)
    teach_own, student_own = call(order_kernel, [((4, LIVE, 256), bf16)] * 2, peak_recv, *parts)
    teach_other, student_other = shift(teach_own, "c", 2, 1), shift(student_own, "c", 2, 1)
    et_own, stat, sums = call(
        expo_own_kernel,
        [((1024, 512), bf16), ((3, 8, 128), f32), ((16, 1024), f32)],
        peak_recv, teach_own, mine, limit=16, cost=1 << 28,
    )
    et_other, pay = call(
        expo_other_kernel, [((1024, 512), bf16), ((8, 8, 128), bf16)], stat, sums, teach_other, mine, limit=16
    )
    et = (et_own, et_other)

    recv = a2a(pay, "z")
    (pay,) = call(col_kernel, [((32, 8, 128), bf16)], recv, *et)
    recv = a2a(pay, PLANE)
    prob, w, norm = pl.pallas_call(
        student_prob_kernel,
        out_shape=[
            pltpu.HBM((1024, 1024), f32),
            pltpu.HBM((1024, 1024), bf16),
            jax.ShapeDtypeStruct((8, 128), f32),
        ],
        in_specs=[VM] * 7,
        out_specs=[pl.BlockSpec(memory_space=pltpu.HBM)] * 2 + [VM],
        scratch_shapes=[
            pltpu.VMEM((1024, 1024), f32),
            pltpu.VMEM((1024, 1024), bf16),
            pltpu.SemaphoreType.DMA((4,)),
        ],
        compiler_params=pltpu.CompilerParams(vmem_limit_bytes=24 << 20),
        cost_estimate=pl.CostEstimate(flops=1 << 29, bytes_accessed=8 << 20, transcendentals=1 << 20),
    )(peak_recv, stat, student_own, student_other, mine, *et)
    (pay,) = call(row_kernel, [((8, 8, 128), bf16)], recv, stat, *et)
    for _ in range(BALANCING_PASSES - 2):
        recv = a2a(pay, "z")
        (pay,) = call(col_kernel, [((32, 8, 128), bf16)], recv, *et, norm)
        recv = a2a(pay, PLANE)
        (pay,) = call(row_kernel, [((8, 8, 128), bf16)], recv, stat, *et)
    recv = a2a(pay, "z")
    pay, col = call(last_col_kernel, [((32, 24, 128), bf16), ((8, 128), f32)], recv, *et, w)
    recv = a2a(pay, PLANE)

    proto_part, scale = pl.pallas_call(
        grad_kernel,
        out_shape=[pltpu.HBM((8, 264, 128), bf16), jax.ShapeDtypeStruct((2, 8, 128), f32)],
        in_specs=[VM] * 8,
        out_specs=[pl.BlockSpec(memory_space=pltpu.HBM), VM],
        scratch_shapes=[pltpu.VMEM((8, 264, 128), bf16), pltpu.SemaphoreType.DMA((2,))],
        compiler_params=pltpu.CompilerParams(vmem_limit_bytes=24 << 20),
    )(recv, stat, col, *et, prob, student_own, student_other)
    proto_recv = a2a(proto_part, "z")
    student_rows = pl.pallas_call(
        own_kernel,
        out_shape=jax.ShapeDtypeStruct((LIVE, 256), bf16),
        in_specs=[VM] * 4 + [HBM] * 2,
        out_specs=VM,
        scratch_shapes=[
            pltpu.VMEM((2, LIVE, 256), bf16),
            pltpu.VMEM((8192, 256), bf16),
            pltpu.SemaphoreType.DMA((3,)),
        ],
        compiler_params=pltpu.CompilerParams(vmem_limit_bytes=24 << 20),
        cost_estimate=pl.CostEstimate(flops=1 << 31, bytes_accessed=4 << 20, transcendentals=2 << 20),
    )(recv, scale, stat, norm, in_hbm(own), in_hbm(prototypes))
    student_rows = [student_rows] + [shift(student_rows, "y", 4, k) for k in (1, 2, 3)]
    (student,) = call(place_kernel, [((256, 256), f32)], patch_mask, *student_rows, limit=16)
    proto, loss = call(end_kernel, [((128, 256), f32), ((1, 128), f32)], proto_recv, limit=16)
    return loss[0, 0], student[None], proto[None]


def solution(mesh):
    fine = Mesh(mesh.devices.reshape(8, 4, 2, 4), ("z", "x", "c", "y"))
    dp = ("z", "x", "c")
    return jax.shard_map(
        local,
        mesh=fine,
        in_specs=(P(dp, None, None), P(dp, None, None), P("y", None), P(dp, None)),
        out_specs=(P(), P(dp, None, None), P("y", dp, None)),
        check_vma=False,
    )
```

```python
import jax
import jax.numpy as jnp
from jax import lax
from jax.experimental import pallas as pl
from jax.experimental.pallas import tpu as pltpu
from jax.sharding import Mesh, PartitionSpec as P

BALANCING_PASSES = 3
LOSS_SCALE = 16384
TEACHER_INV = 1.0 / 0.07
STUDENT_INV = 1.0 / 0.1
IMAGES = 64
GRAD_FACTOR = LOSS_SCALE / (IMAGES * 0.1)
LIVE = 128
NT = (((1,), (1,)), ((), ()))
NN = (((1,), (0,)), ((), ()))
TN = (((0,), (0,)), ((), ()))
f32 = jnp.float32
bf16 = jnp.bfloat16


def dot(a, b, dims):
    return lax.dot_general(a, b, dims, preferred_element_type=f32)


def to_lanes(v):
    return jnp.concatenate([v[i : i + 1, :] for i in range(8)], axis=1)


def to_tile(v):
    return jnp.concatenate([v[:, 128 * i : 128 * (i + 1)] for i in range(8)], axis=0)


def halves(tile):
    even, odd = (jnp.concatenate([tile[i : i + 1] for i in range(start, 8, 2)], axis=1) for start in (0, 1))
    first = lax.axis_index("c") == 0
    return jnp.where(first, even, odd), jnp.where(first, odd, even)


def join(own, other):
    first = lax.axis_index("c") == 0
    even, odd = jnp.where(first, own, other), jnp.where(first, other, own)
    return jnp.concatenate([v[:, 128 * x : 128 * (x + 1)] for x in range(4) for v in (even, odd)], axis=0)


def thirds(v):
    hi = v.astype(bf16).astype(f32)
    mid = (v - hi).astype(bf16).astype(f32)
    return [hi, mid, (v - hi - mid).astype(bf16).astype(f32)]


def split3(v):
    return jnp.concatenate(thirds(v) + [jnp.zeros((13, v.shape[1]), f32)], axis=0).astype(bf16)


def selection(mask):
    patches = mask.shape[1]
    maskf = mask.astype(f32)
    before = lax.broadcasted_iota(jnp.int32, (patches, patches), 0)
    after = lax.broadcasted_iota(jnp.int32, (patches, patches), 1)
    tri = jnp.where(before <= after, 1.0, 0.0).astype(bf16)
    rank = dot(jnp.broadcast_to(maskf, (16, patches)).astype(bf16), tri, NN)[0:1, :]
    slot = lax.broadcasted_iota(jnp.int32, (LIVE, patches), 0).astype(f32)
    hit = jnp.where(rank - 1.0 == slot, 1.0, 0.0) * maskf
    return hit


def head_kernel(
    mask_hbm, teach_hbm, student_hbm, proto_hbm, own_ref, out_ref, mine_ref, mask_ref, teach_ref, student_ref, proto_ref, sems
):
    chunks = 2
    tall = proto_ref.shape[0] // chunks
    small = ((mask_hbm, mask_ref), (teach_hbm, teach_ref), (student_hbm, student_ref))
    first = [pltpu.make_async_copy(src, dst, sems.at[chunks + i]) for i, (src, dst) in enumerate(small)]
    copies = [
        pltpu.make_async_copy(proto_hbm.at[pl.ds(i * tall, tall)], proto_ref.at[pl.ds(i * tall, tall)], sems.at[i])
        for i in range(chunks)
    ]
    for copy in first + copies:
        copy.start()
    image = lax.axis_index("x") * 2 + lax.axis_index("c")
    first[0].wait()
    pick = selection(mask_ref[...]).astype(bf16)
    count = jnp.sum(mask_ref[...].astype(f32), axis=1, keepdims=True)
    first[1].wait()
    own_ref[0] = dot(pick, teach_ref[0], NN).astype(bf16)
    first[2].wait()
    own_ref[1] = dot(pick, student_ref[0], NN).astype(bf16)
    rows = own_ref[...].reshape(2 * LIVE, 256)
    peak = top = total = None
    for i in range(0, 8192, 512):
        if i % tall == 0:
            copies[i // tall].wait()
        if i % 1024 == 0:
            at = pl.multiple_of(i + image * 128, 128)
            mine_ref[i // 8 : i // 8 + 128, :] = proto_ref[pl.ds(at, 128), :]
        low = dot(proto_ref[i : i + 256, :], rows, NT)
        high = dot(proto_ref[i + 256 : i + 512, :], rows, NT)
        teach = jnp.max(jnp.maximum(low[:, :LIVE], high[:, :LIVE]), axis=0, keepdims=True)
        student = jnp.concatenate([low[:, LIVE:], high[:, LIVE:]], axis=0) * STUDENT_INV
        now = jnp.max(student, axis=0, keepdims=True)
        part = jnp.sum(jnp.exp(student - now), axis=0, keepdims=True)
        if peak is None:
            peak, top, total = teach, now, part
        else:
            peak, both = jnp.maximum(peak, teach), jnp.maximum(top, now)
            total = total * jnp.exp(top - both) + part * jnp.exp(now - both)
            top = both
    tile = jnp.concatenate(
        thirds(peak * TEACHER_INV)
        + [jnp.broadcast_to(count, (1, LIVE))]
        + thirds(top + jnp.log(total))
        + [jnp.zeros((1, LIVE), f32)],
        axis=0,
    )
    out_ref[...] = jnp.broadcast_to(tile[None].astype(bf16), out_ref.shape)


def spread(tile, ref):
    ref[...] = jnp.broadcast_to(tile[None].astype(ref.dtype), ref.shape)


def order_kernel(recv_ref, a_ref, b_ref, c_ref, d_ref, teach_ref, student_ref):
    for k, piece in enumerate((a_ref, b_ref, c_ref, d_ref)):
        x = (lax.axis_index("x") + 4 - k) & 3
        teach_ref[x] = piece[0]
        student_ref[x] = piece[1]


def expo_half(rows_ref, mine_ref, et_ref, peak, live, sums):
    for r in range(2):
        at = slice(256 * r, 256 * (r + 1))
        rows = rows_ref[2 * r : 2 * r + 2].reshape(256, 256)
        weights = jnp.broadcast_to(live[:, at], (16, 256)).astype(bf16)
        for j in range(2):
            logits = dot(mine_ref[512 * j : 512 * (j + 1), :], rows, NT)
            block = jnp.exp(logits * TEACHER_INV - peak[:, at]).astype(bf16)
            et_ref[512 * j : 512 * (j + 1), at] = block
            sums[j] += dot(weights, block, NT)


def expo_own_kernel(recv_ref, rows_ref, mine_ref, et_ref, stat_ref, sum_ref):
    peaks, counts = [], []
    for x in range(4):
        for core in range(2):
            got = [recv_ref[(x * 4 + y) * 2 + core].astype(f32) for y in range(4)]
            tops = [v[0:1] + v[1:2] + v[2:3] for v in got]
            peaks.append(jnp.maximum(jnp.maximum(tops[0], tops[1]), jnp.maximum(tops[2], tops[3])))
            counts.append(got[0][3:4])
    peak = jnp.concatenate(peaks, axis=0)
    count = jnp.concatenate(counts, axis=0)
    slot = lax.broadcasted_iota(jnp.int32, (8, 128), 1).astype(f32)
    live = jnp.where(slot < count, 1.0, 0.0)
    stat_ref[0] = live
    stat_ref[1] = live / count
    stat_ref[2] = peak
    sums = [jnp.zeros((16, 512), f32)] * 2
    expo_half(rows_ref, mine_ref, et_ref, halves(peak)[0], halves(live)[0], sums)
    sum_ref[...] = jnp.concatenate(sums, axis=1)


def expo_other_kernel(stat_ref, sum_ref, rows_ref, mine_ref, et_ref, pay_ref):
    sums = [sum_ref[:, 0:512], sum_ref[:, 512:1024]]
    expo_half(rows_ref, mine_ref, et_ref, halves(stat_ref[2])[1], halves(stat_ref[0])[1], sums)
    spread(to_tile(jnp.concatenate(sums, axis=1)[0:1]), pay_ref)


def over_columns(lhs, own_ref, other_ref):
    parts = [jnp.sum(dot(lhs, ref[...], NN), axis=0, keepdims=True) for ref in (own_ref, other_ref)]
    return join(*parts)


def col_kernel(recv_ref, own_ref, other_ref, *refs):
    col = 1.0 / jnp.sum(recv_ref[...].astype(f32), axis=0)
    spread(over_columns(split3(to_lanes(col)), own_ref, other_ref), refs[-1])


def last_col_kernel(recv_ref, own_ref, other_ref, w_ref, pay_ref, col_ref):
    col = 1.0 / jnp.sum(recv_ref[...].astype(f32), axis=0)
    col_ref[...] = col
    lhs = split3(to_lanes(col))
    out = over_columns(lhs, own_ref, other_ref)
    entropy = jnp.sum(dot(lhs, w_ref[...], NN), axis=0, keepdims=True)
    spread(jnp.concatenate([out, join(entropy[:, :512], entropy[:, 512:]), col], axis=0), pay_ref)


def row_kernel(recv_ref, stat_ref, own_ref, other_ref, pay_ref):
    row = stat_ref[0] / jnp.sum(recv_ref[...].astype(f32), axis=0)
    parts = [dot(split3(v), ref[...], NT) for v, ref in zip(halves(row), (own_ref, other_ref))]
    spread(to_tile(jnp.sum(parts[0] + parts[1], axis=0, keepdims=True)), pay_ref)


def student_prob_kernel(
    recv_ref, stat_ref, sown_ref, sother_ref, mine_ref, own_ref, other_ref, prob_ref, w_ref, norm_ref
):
    for image in range(8):
        got = [recv_ref[(image // 2 * 4 + y) * 2 + image % 2].astype(f32) for y in range(4)]
        parts = [v[4:5] + v[5:6] + v[6:7] for v in got]
        top = jnp.maximum(jnp.maximum(parts[0], parts[1]), jnp.maximum(parts[2], parts[3]))
        total = sum(jnp.exp(v - top) for v in parts)
        norm_ref[image : image + 1, :] = top + jnp.log(total)
    norm = jnp.concatenate(halves(norm_ref[...]), axis=1)
    coef = jnp.concatenate(halves(stat_ref[1]), axis=1) * GRAD_FACTOR
    for r in range(4):
        at = slice(256 * r, 256 * (r + 1))
        rows_ref, et_ref = ((sown_ref, own_ref), (sother_ref, other_ref))[r // 2]
        rows = rows_ref[2 * (r % 2) : 2 * (r % 2) + 2].reshape(256, 256)
        log_prob = dot(mine_ref[...], rows, NT) * STUDENT_INV - norm[:, at]
        prob_ref[:, at] = jnp.exp(log_prob) * coef[:, at]
        here = slice(256 * (r % 2), 256 * (r % 2) + 256)
        w_ref[:, at] = (et_ref[:, here].astype(f32) * log_prob).astype(bf16)


def grad_kernel(
    recv_ref, stat_ref, col_ref, own_ref, other_ref, prob_ref, sown_ref, sother_ref, pout_hbm, scale_ref, pout_ref, sems
):
    sums = jnp.sum(recv_ref[...].astype(f32), axis=0)
    entropy = sums[8:16]
    row = stat_ref[0] / sums[0:8]
    weight = stat_ref[1]
    loss = -jnp.sum(jnp.sum(weight * row * entropy, axis=1, keepdims=True), axis=0, keepdims=True) / IMAGES
    hi = loss.astype(bf16).astype(f32)
    mid = (loss - hi).astype(bf16).astype(f32)
    lo = loss - hi - mid
    which = lax.broadcasted_iota(jnp.int32, (8, 128), 0)
    tail = jnp.where(which == 0, hi, jnp.where(which == 1, mid, jnp.where(which == 2, lo, 0.0))).astype(bf16)
    coef = weight * GRAD_FACTOR
    scale_ref[0] = coef
    scale_ref[1] = coef * row
    scale_rows = jnp.concatenate(halves(coef * row), axis=1)
    sown, sother = sown_ref[...].reshape(512, 256), sother_ref[...].reshape(512, 256)
    copies = []
    for j in range(4):
        at = slice(256 * j, 256 * (j + 1))
        col = jnp.concatenate([jnp.broadcast_to(col_ref[i : i + 1, :], (128, 128)).T for i in (2 * j, 2 * j + 1)], axis=0)
        col = jnp.concatenate([col] * 8, axis=1)
        teach = jnp.concatenate([own_ref[at, :], other_ref[at, :]], axis=1).astype(f32)
        grad = (prob_ref[at, :] - teach * col * scale_rows).astype(bf16)
        part = (dot(grad[:, :512], sown, NN) + dot(grad[:, 512:], sother, NN)).astype(bf16)
        for i in (0, 1):
            pout_ref[2 * j + i, 0:128, :] = part[128 * i : 128 * (i + 1), 0:128]
            pout_ref[2 * j + i, 128:256, :] = part[128 * i : 128 * (i + 1), 128:256]
            pout_ref[2 * j + i, 256:264, :] = tail
        if j % 2:
            at = pl.ds(2 * j - 2, 4)
            copies.append(pltpu.make_async_copy(pout_ref.at[at], pout_hbm.at[at], sems.at[j // 2]))
            copies[-1].start()
    for copy in copies:
        copy.wait()


def column(row, wide):
    return jnp.concatenate([jnp.broadcast_to(row, (128, 128)).T] * (wide // 128), axis=1)


def own_image():
    return pl.ds(lax.axis_index("x") * 2 + lax.axis_index("c"), 1)


def own_kernel(recv_ref, scale_ref, stat_ref, norm_ref, rows_hbm, proto_hbm, out_ref, rows_ref, proto_ref, sems):
    chunks = 2
    tall = proto_ref.shape[0] // chunks
    rows_copy = pltpu.make_async_copy(rows_hbm, rows_ref, sems.at[chunks])
    copies = [
        pltpu.make_async_copy(proto_hbm.at[pl.ds(i * tall, tall)], proto_ref.at[pl.ds(i * tall, tall)], sems.at[i])
        for i in range(chunks)
    ]
    for copy in [rows_copy] + copies:
        copy.start()
    y = lax.axis_index("y")
    peak = column(stat_ref[2, own_image(), :], 1024)
    norm = column(norm_ref[own_image(), :], 1024)
    coef = column(scale_ref[0, own_image(), :], 1024)
    scale = column(scale_ref[1, own_image(), :], 1024)
    cols = [recv_ref[(x * 4 + y) * 2 + c].astype(f32)[16:24] for x in range(4) for c in range(2)]
    rows_copy.wait()
    rows = rows_ref[...].reshape(2 * LIVE, 256)
    total = jnp.zeros((LIVE, 256), f32)
    for i in range(8):
        if i % 4 == 0:
            copies[i // 4].wait()
        col = jnp.concatenate([v[i : i + 1, :] for v in cols], axis=1)
        block = proto_ref[1024 * i : 1024 * (i + 1), :]
        logits = dot(rows, block, NT)
        teach = jnp.exp(logits[0:LIVE] * TEACHER_INV - peak).astype(bf16).astype(f32)
        prob = jnp.exp(logits[LIVE:] * STUDENT_INV - norm)
        grad = (prob * coef - teach * (col * scale)).astype(bf16)
        total += dot(grad, block, NN)
    out_ref[...] = total.astype(bf16)


def place_kernel(mask_ref, a_ref, b_ref, c_ref, d_ref, student_ref):
    pick = selection(mask_ref[...]).astype(bf16)
    parts = [ref[...].astype(f32) for ref in (a_ref, b_ref, c_ref, d_ref)]
    rows = (parts[0] + parts[2]) + (parts[1] + parts[3])
    student_ref[...] = sum(dot(pick, part.astype(bf16), TN) for part in thirds(rows))


def end_kernel(recv_ref, proto_ref, loss_ref):
    total = jnp.sum(recv_ref[...].astype(f32), axis=0)
    proto_ref[:, 0:128] = total[0:128]
    proto_ref[:, 128:256] = total[128:256]
    loss_ref[...] = total[256:257] + total[257:258] + total[258:259]


VM = pl.BlockSpec(memory_space=pltpu.VMEM)


def call(kernel, out, *args, scratch=(), limit=8, cost=None):
    out = [jax.ShapeDtypeStruct(s, d) for s, d in out]
    return pl.pallas_call(
        kernel,
        out_shape=out,
        in_specs=[VM] * len(args),
        out_specs=[VM] * len(out),
        scratch_shapes=list(scratch),
        compiler_params=pltpu.CompilerParams(vmem_limit_bytes=limit << 20),
        cost_estimate=cost and pl.CostEstimate(flops=cost, bytes_accessed=1 << 20, transcendentals=1 << 20),
    )(*args)


def in_hbm(v):
    return pltpu.with_memory_space_constraint(v, pltpu.HBM)


def a2a(v, axes):
    return lax.all_to_all(v, axes, 0, 0, tiled=True)


def shift(v, axis, n, k):
    return lax.ppermute(v, axis, [(i, (i + k) % n) for i in range(n)])


PLANE = ("x", "y", "c")
HBM = pl.BlockSpec(memory_space=pl.ANY)


def local(teacher_feats, student_feats, prototypes, patch_mask):
    own, peak_pay, mine = pl.pallas_call(
        head_kernel,
        out_shape=[
            jax.ShapeDtypeStruct((2, LIVE, 256), bf16),
            jax.ShapeDtypeStruct((32, 8, 128), bf16),
            jax.ShapeDtypeStruct((1024, 256), bf16),
        ],
        in_specs=[HBM] * 4,
        out_specs=[VM] * 3,
        scratch_shapes=[
            pltpu.VMEM((1, 256), jnp.int32),
            pltpu.VMEM((1, 256, 256), bf16),
            pltpu.VMEM((1, 256, 256), bf16),
            pltpu.VMEM((8192, 256), bf16),
            pltpu.SemaphoreType.DMA((5,)),
        ],
        compiler_params=pltpu.CompilerParams(vmem_limit_bytes=32 << 20),
    )(*(in_hbm(v) for v in (patch_mask, teacher_feats, student_feats, prototypes)))

    parts = [own] + [shift(own, "x", 4, k) for k in (1, 2, 3)]
    peak_recv = a2a(peak_pay, PLANE)
    teach_own, student_own = call(order_kernel, [((4, LIVE, 256), bf16)] * 2, peak_recv, *parts)
    teach_other, student_other = shift(teach_own, "c", 2, 1), shift(student_own, "c", 2, 1)
    et_own, stat, sums = call(
        expo_own_kernel,
        [((1024, 512), bf16), ((3, 8, 128), f32), ((16, 1024), f32)],
        peak_recv, teach_own, mine, limit=16, cost=1 << 28,
    )
    et_other, pay = call(
        expo_other_kernel, [((1024, 512), bf16), ((8, 8, 128), bf16)], stat, sums, teach_other, mine, limit=16
    )
    et = (et_own, et_other)

    recv = a2a(pay, "z")
    (pay,) = call(col_kernel, [((32, 8, 128), bf16)], recv, *et)
    recv = a2a(pay, PLANE)
    recv, stat2 = lax.optimization_barrier((recv, stat))
    prob, w, norm = call(
        student_prob_kernel, [((1024, 1024), f32), ((1024, 1024), bf16), ((8, 128), f32)],
        peak_recv, stat2, student_own, student_other, mine, *et, limit=24,
    )
    (pay,) = call(row_kernel, [((8, 8, 128), bf16)], recv, stat, *et)
    pay, prob, w, norm = lax.optimization_barrier((pay, prob, w, norm))
    for _ in range(BALANCING_PASSES - 2):
        recv = a2a(pay, "z")
        (pay,) = call(col_kernel, [((32, 8, 128), bf16)], recv, *et)
        recv = a2a(pay, PLANE)
        (pay,) = call(row_kernel, [((8, 8, 128), bf16)], recv, stat, *et)
    recv = a2a(pay, "z")
    pay, col = call(last_col_kernel, [((32, 24, 128), bf16), ((8, 128), f32)], recv, *et, w)
    recv = a2a(pay, PLANE)

    proto_part, scale = pl.pallas_call(
        grad_kernel,
        out_shape=[pltpu.HBM((8, 264, 128), bf16), jax.ShapeDtypeStruct((2, 8, 128), f32)],
        in_specs=[VM] * 8,
        out_specs=[pl.BlockSpec(memory_space=pltpu.HBM), VM],
        scratch_shapes=[pltpu.VMEM((8, 264, 128), bf16), pltpu.SemaphoreType.DMA((2,))],
        compiler_params=pltpu.CompilerParams(vmem_limit_bytes=24 << 20),
    )(recv, stat, col, *et, prob, student_own, student_other)
    proto_recv = a2a(proto_part, "z")
    student_rows = pl.pallas_call(
        own_kernel,
        out_shape=jax.ShapeDtypeStruct((LIVE, 256), bf16),
        in_specs=[VM] * 4 + [HBM] * 2,
        out_specs=VM,
        scratch_shapes=[
            pltpu.VMEM((2, LIVE, 256), bf16),
            pltpu.VMEM((8192, 256), bf16),
            pltpu.SemaphoreType.DMA((3,)),
        ],
        compiler_params=pltpu.CompilerParams(vmem_limit_bytes=24 << 20),
        cost_estimate=pl.CostEstimate(flops=1 << 31, bytes_accessed=4 << 20, transcendentals=2 << 20),
    )(recv, scale, stat, norm, in_hbm(own), in_hbm(prototypes))
    student_rows = [student_rows] + [shift(student_rows, "y", 4, k) for k in (1, 2, 3)]
    (student,) = call(place_kernel, [((256, 256), f32)], patch_mask, *student_rows, limit=16)
    proto, loss = call(end_kernel, [((128, 256), f32), ((1, 128), f32)], proto_recv, limit=16)
    return loss[0, 0], student[None], proto[None]


def solution(mesh):
    fine = Mesh(mesh.devices.reshape(8, 4, 2, 4), ("z", "x", "c", "y"))
    dp = ("z", "x", "c")
    return jax.shard_map(
        local,
        mesh=fine,
        in_specs=(P(dp, None, None), P(dp, None, None), P("y", None), P(dp, None)),
        out_specs=(P(), P(dp, None, None), P("y", dp, None)),
        check_vma=False,
    )
```

```python
import jax
import jax.numpy as jnp
from jax import lax
from jax.experimental import pallas as pl
from jax.experimental.pallas import tpu as pltpu
from jax.sharding import Mesh, PartitionSpec as P

BALANCING_PASSES = 3
LOSS_SCALE = 16384
TEACHER_INV = 1.0 / 0.07
STUDENT_INV = 1.0 / 0.1
IMAGES = 64
GRAD_FACTOR = LOSS_SCALE / (IMAGES * 0.1)
LIVE = 128
NT = (((1,), (1,)), ((), ()))
NN = (((1,), (0,)), ((), ()))
TN = (((0,), (0,)), ((), ()))
f32 = jnp.float32
bf16 = jnp.bfloat16


def dot(a, b, dims):
    return lax.dot_general(a, b, dims, preferred_element_type=f32)


def to_lanes(v):
    return jnp.concatenate([v[i : i + 1, :] for i in range(8)], axis=1)


def to_tile(v):
    return jnp.concatenate([v[:, 128 * i : 128 * (i + 1)] for i in range(8)], axis=0)


def halves(tile):
    left = lax.broadcasted_iota(jnp.int32, (1, 128), 1) < 64
    turned = pltpu.roll(tile, 64, 1)
    low = [jnp.where(left, tile[i : i + 1], turned[i + 1 : i + 2]) for i in range(0, 8, 2)]
    high = [jnp.where(left, turned[i : i + 1], tile[i + 1 : i + 2]) for i in range(0, 8, 2)]
    low, high = jnp.concatenate(low, axis=1), jnp.concatenate(high, axis=1)
    first = lax.axis_index("c") == 0
    return jnp.where(first, low, high), jnp.where(first, high, low)


def join(own, other):
    first = lax.axis_index("c") == 0
    low, high = jnp.where(first, own, other), jnp.where(first, other, own)
    low, high = (jnp.concatenate([v[:, 128 * i : 128 * (i + 1)] for i in range(4)], axis=0) for v in (low, high))
    left = lax.broadcasted_iota(jnp.int32, (4, 128), 1) < 64
    even = jnp.where(left, low, pltpu.roll(high, 64, 1))
    odd = jnp.where(left, pltpu.roll(low, 64, 1), high)
    return jnp.concatenate([v[i : i + 1] for i in range(4) for v in (even, odd)], axis=0)


def thirds(v):
    hi = v.astype(bf16).astype(f32)
    mid = (v - hi).astype(bf16).astype(f32)
    return [hi, mid, (v - hi - mid).astype(bf16).astype(f32)]


def split3(v):
    return jnp.concatenate(thirds(v) + [jnp.zeros((13, v.shape[1]), f32)], axis=0).astype(bf16)


def selection(mask):
    patches = mask.shape[1]
    maskf = mask.astype(f32)
    before = lax.broadcasted_iota(jnp.int32, (patches, patches), 0)
    after = lax.broadcasted_iota(jnp.int32, (patches, patches), 1)
    tri = jnp.where(before <= after, 1.0, 0.0).astype(bf16)
    rank = dot(jnp.broadcast_to(maskf, (16, patches)).astype(bf16), tri, NN)[0:1, :]
    slot = lax.broadcasted_iota(jnp.int32, (LIVE, patches), 0).astype(f32)
    hit = jnp.where(rank - 1.0 == slot, 1.0, 0.0) * maskf
    return hit


def head_kernel(
    mask_hbm, teach_hbm, student_hbm, proto_hbm, own_ref, out_ref, mine_ref, mask_ref, teach_ref, student_ref, proto_ref, sems
):
    chunks = 2
    tall = proto_ref.shape[0] // chunks
    small = ((mask_hbm, mask_ref), (teach_hbm, teach_ref), (student_hbm, student_ref))
    first = [pltpu.make_async_copy(src, dst, sems.at[chunks + i]) for i, (src, dst) in enumerate(small)]
    copies = [
        pltpu.make_async_copy(proto_hbm.at[pl.ds(i * tall, tall)], proto_ref.at[pl.ds(i * tall, tall)], sems.at[i])
        for i in range(chunks)
    ]
    for copy in first + copies:
        copy.start()
    image = lax.axis_index("x") * 2 + lax.axis_index("c")
    first[0].wait()
    pick = selection(mask_ref[...]).astype(bf16)
    count = jnp.sum(mask_ref[...].astype(f32), axis=1, keepdims=True)
    first[1].wait()
    own_ref[0] = dot(pick, teach_ref[0], NN).astype(bf16)
    first[2].wait()
    own_ref[1] = dot(pick, student_ref[0], NN).astype(bf16)
    rows = own_ref[...].reshape(2 * LIVE, 256)
    peak = top = total = None
    for i in range(0, 8192, 512):
        if i % tall == 0:
            copies[i // tall].wait()
        if i % 1024 == 0:
            at = pl.multiple_of(i + image * 128, 128)
            mine_ref[i // 8 : i // 8 + 128, :] = proto_ref[pl.ds(at, 128), :]
        low = dot(proto_ref[i : i + 256, :], rows, NT)
        high = dot(proto_ref[i + 256 : i + 512, :], rows, NT)
        teach = jnp.max(jnp.maximum(low[:, :LIVE], high[:, :LIVE]), axis=0, keepdims=True)
        student = jnp.concatenate([low[:, LIVE:], high[:, LIVE:]], axis=0) * STUDENT_INV
        now = jnp.max(student, axis=0, keepdims=True)
        part = jnp.sum(jnp.exp(student - now), axis=0, keepdims=True)
        if peak is None:
            peak, top, total = teach, now, part
        else:
            peak, both = jnp.maximum(peak, teach), jnp.maximum(top, now)
            total = total * jnp.exp(top - both) + part * jnp.exp(now - both)
            top = both
    tile = jnp.concatenate(
        thirds(peak * TEACHER_INV)
        + [jnp.broadcast_to(count, (1, LIVE))]
        + thirds(top + jnp.log(total))
        + [jnp.zeros((1, LIVE), f32)],
        axis=0,
    )
    out_ref[:, :, 64:72, :] = jnp.broadcast_to(tile[None, None].astype(bf16), (16, 2, 8, 128))
    for core in range(2):
        at = pl.ds(pl.multiple_of(core * 64 + lax.axis_index("y") * 16, 16), 16)
        for i in range(2):
            block = own_ref[i, at, :]
            block = jnp.concatenate([block[:, :128], block[:, 128:]], axis=0)
            out_ref[:, core, 32 * i : 32 * i + 32, :] = jnp.broadcast_to(block[None], (16, 32, 128))


def spread(tile, ref):
    ref[...] = jnp.broadcast_to(tile[None].astype(ref.dtype), ref.shape)


def order_kernel(recv_ref, teach_ref, student_ref):
    for image in range(8):
        for y in range(4):
            at = slice(64 * image + 16 * y, 64 * image + 16 * y + 16)
            source = (image // 2 * 4 + y) * 2 + image % 2
            for i, ref in enumerate((teach_ref, student_ref)):
                ref[at, 0:128] = recv_ref[source, 32 * i : 32 * i + 16, :]
                ref[at, 128:256] = recv_ref[source, 32 * i + 16 : 32 * i + 32, :]


def expo_half(rows_ref, mine_ref, et_ref, peak, live, sums):
    for r in range(2):
        at = slice(256 * r, 256 * (r + 1))
        rows = rows_ref[at, :]
        weights = jnp.broadcast_to(live[:, at], (16, 256)).astype(bf16)
        for j in range(2):
            logits = dot(mine_ref[512 * j : 512 * (j + 1), :], rows, NT)
            block = jnp.exp(logits * TEACHER_INV - peak[:, at]).astype(bf16)
            et_ref[512 * j : 512 * (j + 1), at] = block
            sums[j] += dot(weights, block, NT)


def expo_own_kernel(recv_ref, rows_ref, mine_ref, et_ref, stat_ref, sum_ref):
    peaks, counts = [], []
    for x in range(4):
        for core in range(2):
            got = [recv_ref[(x * 4 + y) * 2 + core, 64:72, :].astype(f32) for y in range(4)]
            tops = [v[0:1] + v[1:2] + v[2:3] for v in got]
            peaks.append(jnp.maximum(jnp.maximum(tops[0], tops[1]), jnp.maximum(tops[2], tops[3])))
            counts.append(got[0][3:4])
    peak = jnp.concatenate(peaks, axis=0)
    count = jnp.concatenate(counts, axis=0)
    slot = lax.broadcasted_iota(jnp.int32, (8, 128), 1).astype(f32)
    live = jnp.where(slot < count, 1.0, 0.0)
    stat_ref[0] = live
    stat_ref[1] = live / count
    stat_ref[2] = peak
    sums = [jnp.zeros((16, 512), f32)] * 2
    expo_half(rows_ref, mine_ref, et_ref, halves(peak)[0], halves(live)[0], sums)
    sum_ref[...] = jnp.concatenate(sums, axis=1)


def expo_other_kernel(stat_ref, sum_ref, rows_ref, mine_ref, et_ref, pay_ref):
    sums = [sum_ref[:, 0:512], sum_ref[:, 512:1024]]
    expo_half(rows_ref, mine_ref, et_ref, halves(stat_ref[2])[1], halves(stat_ref[0])[1], sums)
    spread(to_tile(jnp.concatenate(sums, axis=1)[0:1]), pay_ref)


def over_columns(lhs, own_ref, other_ref):
    parts = [jnp.sum(dot(lhs, ref[...], NN), axis=0, keepdims=True) for ref in (own_ref, other_ref)]
    return join(*parts)


def col_kernel(recv_ref, own_ref, other_ref, *refs):
    col = 1.0 / jnp.sum(recv_ref[...].astype(f32), axis=0)
    spread(over_columns(split3(to_lanes(col)), own_ref, other_ref), refs[-1])


def last_col_kernel(recv_ref, own_ref, other_ref, w_ref, pay_ref, col_ref):
    col = 1.0 / jnp.sum(recv_ref[...].astype(f32), axis=0)
    col_ref[...] = col
    lhs = split3(to_lanes(col))
    out = over_columns(lhs, own_ref, other_ref)
    entropy = jnp.sum(dot(lhs, w_ref[...], NN), axis=0, keepdims=True)
    spread(jnp.concatenate([out, join(entropy[:, :512], entropy[:, 512:]), col], axis=0), pay_ref)


def row_kernel(recv_ref, stat_ref, own_ref, other_ref, pay_ref):
    row = stat_ref[0] / jnp.sum(recv_ref[...].astype(f32), axis=0)
    parts = [dot(split3(v), ref[...], NT) for v, ref in zip(halves(row), (own_ref, other_ref))]
    spread(to_tile(jnp.sum(parts[0] + parts[1], axis=0, keepdims=True)), pay_ref)


def student_prob_kernel(
    recv_ref, stat_ref, sown_ref, sother_ref, mine_ref, own_ref, other_ref, prob_ref, w_ref, norm_ref
):
    for image in range(8):
        got = [recv_ref[(image // 2 * 4 + y) * 2 + image % 2, 64:72, :].astype(f32) for y in range(4)]
        parts = [v[4:5] + v[5:6] + v[6:7] for v in got]
        top = jnp.maximum(jnp.maximum(parts[0], parts[1]), jnp.maximum(parts[2], parts[3]))
        total = sum(jnp.exp(v - top) for v in parts)
        norm_ref[image : image + 1, :] = top + jnp.log(total)
    norm = jnp.concatenate(halves(norm_ref[...]), axis=1)
    coef = jnp.concatenate(halves(stat_ref[1]), axis=1) * GRAD_FACTOR
    for r in range(4):
        at = slice(256 * r, 256 * (r + 1))
        rows_ref, et_ref = ((sown_ref, own_ref), (sother_ref, other_ref))[r // 2]
        rows = rows_ref[256 * (r % 2) : 256 * (r % 2) + 256, :]
        log_prob = dot(mine_ref[...], rows, NT) * STUDENT_INV - norm[:, at]
        prob_ref[:, at] = jnp.exp(log_prob) * coef[:, at]
        here = slice(256 * (r % 2), 256 * (r % 2) + 256)
        w_ref[:, at] = (et_ref[:, here].astype(f32) * log_prob).astype(bf16)


def grad_kernel(
    recv_ref, stat_ref, col_ref, own_ref, other_ref, prob_ref, sown_ref, sother_ref, pout_hbm, scale_ref, pout_ref, sems
):
    sums = jnp.sum(recv_ref[...].astype(f32), axis=0)
    entropy = sums[8:16]
    row = stat_ref[0] / sums[0:8]
    weight = stat_ref[1]
    loss = -jnp.sum(jnp.sum(weight * row * entropy, axis=1, keepdims=True), axis=0, keepdims=True) / IMAGES
    hi = loss.astype(bf16).astype(f32)
    mid = (loss - hi).astype(bf16).astype(f32)
    lo = loss - hi - mid
    which = lax.broadcasted_iota(jnp.int32, (8, 128), 0)
    tail = jnp.where(which == 0, hi, jnp.where(which == 1, mid, jnp.where(which == 2, lo, 0.0))).astype(bf16)
    coef = weight * GRAD_FACTOR
    scale_ref[0] = coef
    scale_ref[1] = coef * row
    scale_rows = jnp.concatenate(halves(coef * row), axis=1)
    sown, sother = sown_ref[...], sother_ref[...]
    copies = []
    for j in range(4):
        at = slice(256 * j, 256 * (j + 1))
        col = jnp.concatenate([jnp.broadcast_to(col_ref[i : i + 1, :], (128, 128)).T for i in (2 * j, 2 * j + 1)], axis=0)
        col = jnp.concatenate([col] * 8, axis=1)
        teach = jnp.concatenate([own_ref[at, :], other_ref[at, :]], axis=1).astype(f32)
        grad = (prob_ref[at, :] - teach * col * scale_rows).astype(bf16)
        part = (dot(grad[:, :512], sown, NN) + dot(grad[:, 512:], sother, NN)).astype(bf16)
        for i in (0, 1):
            pout_ref[2 * j + i, 0:128, :] = part[128 * i : 128 * (i + 1), 0:128]
            pout_ref[2 * j + i, 128:256, :] = part[128 * i : 128 * (i + 1), 128:256]
            pout_ref[2 * j + i, 256:264, :] = tail
        if j % 2:
            at = pl.ds(2 * j - 2, 4)
            copies.append(pltpu.make_async_copy(pout_ref.at[at], pout_hbm.at[at], sems.at[j // 2]))
            copies[-1].start()
    for copy in copies:
        copy.wait()


def column(row, wide):
    return jnp.concatenate([jnp.broadcast_to(row, (128, 128)).T] * (wide // 128), axis=1)


def own_image():
    return pl.ds(lax.axis_index("x") * 2 + lax.axis_index("c"), 1)


def own_kernel(recv_ref, scale_ref, stat_ref, norm_ref, rows_hbm, proto_hbm, out_ref, rows_ref, proto_ref, sems):
    chunks = 2
    tall = proto_ref.shape[0] // chunks
    rows_copy = pltpu.make_async_copy(rows_hbm, rows_ref, sems.at[chunks])
    copies = [
        pltpu.make_async_copy(proto_hbm.at[pl.ds(i * tall, tall)], proto_ref.at[pl.ds(i * tall, tall)], sems.at[i])
        for i in range(chunks)
    ]
    for copy in [rows_copy] + copies:
        copy.start()
    y = lax.axis_index("y")
    peak = column(stat_ref[2, own_image(), :], 1024)
    norm = column(norm_ref[own_image(), :], 1024)
    coef = column(scale_ref[0, own_image(), :], 1024)
    scale = column(scale_ref[1, own_image(), :], 1024)
    cols = [recv_ref[(x * 4 + y) * 2 + c].astype(f32)[16:24] for x in range(4) for c in range(2)]
    rows_copy.wait()
    rows = rows_ref[...].reshape(2 * LIVE, 256)
    total = jnp.zeros((LIVE, 256), f32)
    for i in range(8):
        if i % 4 == 0:
            copies[i // 4].wait()
        col = jnp.concatenate([v[i : i + 1, :] for v in cols], axis=1)
        block = proto_ref[1024 * i : 1024 * (i + 1), :]
        logits = dot(rows, block, NT)
        teach = jnp.exp(logits[0:LIVE] * TEACHER_INV - peak).astype(bf16).astype(f32)
        prob = jnp.exp(logits[LIVE:] * STUDENT_INV - norm)
        grad = (prob * coef - teach * (col * scale)).astype(bf16)
        total += dot(grad, block, NN)
    out_ref[...] = total.astype(bf16)


def place_kernel(mask_ref, a_ref, b_ref, c_ref, d_ref, student_ref):
    pick = selection(mask_ref[...]).astype(bf16)
    parts = [ref[...].astype(f32) for ref in (a_ref, b_ref, c_ref, d_ref)]
    rows = (parts[0] + parts[2]) + (parts[1] + parts[3])
    student_ref[...] = sum(dot(pick, part.astype(bf16), TN) for part in thirds(rows))


def end_kernel(recv_ref, proto_ref, loss_ref):
    total = jnp.sum(recv_ref[...].astype(f32), axis=0)
    proto_ref[:, 0:128] = total[0:128]
    proto_ref[:, 128:256] = total[128:256]
    loss_ref[...] = total[256:257] + total[257:258] + total[258:259]


VM = pl.BlockSpec(memory_space=pltpu.VMEM)


def call(kernel, out, *args, scratch=(), limit=8, cost=None):
    out = [jax.ShapeDtypeStruct(s, d) for s, d in out]
    return pl.pallas_call(
        kernel,
        out_shape=out,
        in_specs=[VM] * len(args),
        out_specs=[VM] * len(out),
        scratch_shapes=list(scratch),
        compiler_params=pltpu.CompilerParams(vmem_limit_bytes=limit << 20),
        cost_estimate=cost and pl.CostEstimate(flops=cost, bytes_accessed=1 << 20, transcendentals=1 << 20),
    )(*args)


def in_hbm(v):
    return pltpu.with_memory_space_constraint(v, pltpu.HBM)


def a2a(v, axes):
    return lax.all_to_all(v, axes, 0, 0, tiled=True)


def shift(v, axis, n, k):
    return lax.ppermute(v, axis, [(i, (i + k) % n) for i in range(n)])


PLANE = ("x", "y", "c")
HBM = pl.BlockSpec(memory_space=pl.ANY)


def local(teacher_feats, student_feats, prototypes, patch_mask):
    own, peak_pay, mine = pl.pallas_call(
        head_kernel,
        out_shape=[
            jax.ShapeDtypeStruct((2, LIVE, 256), bf16),
            jax.ShapeDtypeStruct((16, 2, 72, 128), bf16),
            jax.ShapeDtypeStruct((1024, 256), bf16),
        ],
        in_specs=[HBM] * 4,
        out_specs=[VM] * 3,
        scratch_shapes=[
            pltpu.VMEM((1, 256), jnp.int32),
            pltpu.VMEM((1, 256, 256), bf16),
            pltpu.VMEM((1, 256, 256), bf16),
            pltpu.VMEM((8192, 256), bf16),
            pltpu.SemaphoreType.DMA((5,)),
        ],
        compiler_params=pltpu.CompilerParams(vmem_limit_bytes=32 << 20),
    )(*(in_hbm(v) for v in (patch_mask, teacher_feats, student_feats, prototypes)))

    peak_recv = a2a(peak_pay.reshape(32, 72, 128), PLANE)
    teach_own, student_own = call(order_kernel, [((512, 256), bf16)] * 2, peak_recv)
    teach_other, student_other = shift(teach_own, "c", 2, 1), shift(student_own, "c", 2, 1)
    et_own, stat, sums = call(
        expo_own_kernel,
        [((1024, 512), bf16), ((3, 8, 128), f32), ((16, 1024), f32)],
        peak_recv, teach_own, mine, limit=16, cost=1 << 28,
    )
    et_other, pay = call(
        expo_other_kernel, [((1024, 512), bf16), ((8, 8, 128), bf16)], stat, sums, teach_other, mine, limit=16
    )
    et = (et_own, et_other)

    recv = a2a(pay, "z")
    (pay,) = call(col_kernel, [((32, 8, 128), bf16)], recv, *et)
    recv = a2a(pay, PLANE)
    recv, stat2 = lax.optimization_barrier((recv, stat))
    prob, w, norm = call(
        student_prob_kernel, [((1024, 1024), f32), ((1024, 1024), bf16), ((8, 128), f32)],
        peak_recv, stat2, student_own, student_other, mine, *et, limit=24,
    )
    (pay,) = call(row_kernel, [((8, 8, 128), bf16)], recv, stat, *et)
    pay, prob, w, norm = lax.optimization_barrier((pay, prob, w, norm))
    for _ in range(BALANCING_PASSES - 2):
        recv = a2a(pay, "z")
        (pay,) = call(col_kernel, [((32, 8, 128), bf16)], recv, *et)
        recv = a2a(pay, PLANE)
        (pay,) = call(row_kernel, [((8, 8, 128), bf16)], recv, stat, *et)
    recv = a2a(pay, "z")
    pay, col = call(last_col_kernel, [((32, 24, 128), bf16), ((8, 128), f32)], recv, *et, w)
    recv = a2a(pay, PLANE)

    proto_part, scale = pl.pallas_call(
        grad_kernel,
        out_shape=[pltpu.HBM((8, 264, 128), bf16), jax.ShapeDtypeStruct((2, 8, 128), f32)],
        in_specs=[VM] * 8,
        out_specs=[pl.BlockSpec(memory_space=pltpu.HBM), VM],
        scratch_shapes=[pltpu.VMEM((8, 264, 128), bf16), pltpu.SemaphoreType.DMA((2,))],
        compiler_params=pltpu.CompilerParams(vmem_limit_bytes=24 << 20),
    )(recv, stat, col, *et, prob, student_own, student_other)
    proto_recv = a2a(proto_part, "z")
    student_rows = pl.pallas_call(
        own_kernel,
        out_shape=jax.ShapeDtypeStruct((LIVE, 256), bf16),
        in_specs=[VM] * 4 + [HBM] * 2,
        out_specs=VM,
        scratch_shapes=[
            pltpu.VMEM((2, LIVE, 256), bf16),
            pltpu.VMEM((8192, 256), bf16),
            pltpu.SemaphoreType.DMA((3,)),
        ],
        compiler_params=pltpu.CompilerParams(vmem_limit_bytes=24 << 20),
        cost_estimate=pl.CostEstimate(flops=1 << 31, bytes_accessed=4 << 20, transcendentals=2 << 20),
    )(recv, scale, stat, norm, in_hbm(own), in_hbm(prototypes))
    student_rows = [student_rows] + [shift(student_rows, "y", 4, k) for k in (1, 2, 3)]
    (student,) = call(place_kernel, [((256, 256), f32)], patch_mask, *student_rows, limit=16)
    proto, loss = call(end_kernel, [((128, 256), f32), ((1, 128), f32)], proto_recv, limit=16)
    return loss[0, 0], student[None], proto[None]


def solution(mesh):
    fine = Mesh(mesh.devices.reshape(8, 4, 2, 4), ("z", "x", "c", "y"))
    dp = ("z", "x", "c")
    return jax.shard_map(
        local,
        mesh=fine,
        in_specs=(P(dp, None, None), P(dp, None, None), P("y", None), P(dp, None)),
        out_specs=(P(), P(dp, None, None), P("y", dp, None)),
        check_vma=False,
    )
```

```python
import jax
import jax.numpy as jnp
from jax import lax
from jax.experimental import pallas as pl
from jax.experimental.pallas import tpu as pltpu
from jax.sharding import Mesh, PartitionSpec as P

BALANCING_PASSES = 3
LOSS_SCALE = 16384
TEACHER_INV = 1.0 / 0.07
STUDENT_INV = 1.0 / 0.1
IMAGES = 64
LOG2E = 1.4426950408889634
TEACHER_LOG2 = TEACHER_INV * LOG2E
STUDENT_LOG2 = STUDENT_INV * LOG2E
GRAD_FACTOR = LOSS_SCALE / (IMAGES * 0.1)
LIVE = 128
NT = (((1,), (1,)), ((), ()))
NN = (((1,), (0,)), ((), ()))
TN = (((0,), (0,)), ((), ()))
f32 = jnp.float32
bf16 = jnp.bfloat16


def dot(a, b, dims):
    return lax.dot_general(a, b, dims, preferred_element_type=f32)


def to_lanes(v):
    return jnp.concatenate([v[i : i + 1, :] for i in range(8)], axis=1)


def to_tile(v):
    return jnp.concatenate([v[:, 128 * i : 128 * (i + 1)] for i in range(8)], axis=0)


def halves(tile):
    even, odd = (jnp.concatenate([tile[i : i + 1] for i in range(start, 8, 2)], axis=1) for start in (0, 1))
    first = lax.axis_index("c") == 0
    return jnp.where(first, even, odd), jnp.where(first, odd, even)


def join(own, other):
    first = lax.axis_index("c") == 0
    even, odd = jnp.where(first, own, other), jnp.where(first, other, own)
    return jnp.concatenate([v[:, 128 * x : 128 * (x + 1)] for x in range(4) for v in (even, odd)], axis=0)


def thirds(v):
    hi = v.astype(bf16).astype(f32)
    mid = (v - hi).astype(bf16).astype(f32)
    return [hi, mid, (v - hi - mid).astype(bf16).astype(f32)]


def split3(v):
    return jnp.concatenate(thirds(v) + [jnp.zeros((13, v.shape[1]), f32)], axis=0).astype(bf16)


def selection(mask):
    patches = mask.shape[1]
    maskf = mask.astype(f32)
    before = lax.broadcasted_iota(jnp.int32, (patches, patches), 0)
    after = lax.broadcasted_iota(jnp.int32, (patches, patches), 1)
    tri = jnp.where(before <= after, 1.0, 0.0).astype(bf16)
    rank = dot(jnp.broadcast_to(maskf, (16, patches)).astype(bf16), tri, NN)[0:1, :]
    slot = lax.broadcasted_iota(jnp.int32, (LIVE, patches), 0).astype(f32)
    hit = jnp.where(rank - 1.0 == slot, 1.0, 0.0) * maskf
    return hit


def head_kernel(
    mask_hbm, teach_hbm, student_hbm, proto_hbm, own_ref, out_ref, mine_ref, mask_ref, teach_ref, student_ref, proto_ref, sems
):
    starts, sizes = (0, 3072), (3072, 5120)
    small = ((mask_hbm, mask_ref), (teach_hbm, teach_ref), (student_hbm, student_ref))
    first = [pltpu.make_async_copy(src, dst, sems.at[2 + i]) for i, (src, dst) in enumerate(small)]
    copies = [
        pltpu.make_async_copy(proto_hbm.at[pl.ds(at, size)], proto_ref.at[pl.ds(at, size)], sems.at[i])
        for i, (at, size) in enumerate(zip(starts, sizes))
    ]
    for copy in first + copies:
        copy.start()
    image = lax.axis_index("x") * 2 + lax.axis_index("c")
    first[0].wait()
    pick = selection(mask_ref[...]).astype(bf16)
    count = jnp.sum(mask_ref[...].astype(f32), axis=1, keepdims=True)
    first[1].wait()
    own_ref[0] = dot(pick, teach_ref[0], NN).astype(bf16)
    first[2].wait()
    own_ref[1] = dot(pick, student_ref[0], NN).astype(bf16)
    rows = own_ref[...].reshape(2 * LIVE, 256)
    peak = top = total = None
    for i in range(0, 8192, 512):
        if i in starts:
            copies[starts.index(i)].wait()
        if i % 1024 == 0:
            at = pl.multiple_of(i + image * 128, 128)
            mine_ref[i // 8 : i // 8 + 128, :] = proto_ref[pl.ds(at, 128), :]
        low = dot(proto_ref[i : i + 256, :], rows, NT)
        high = dot(proto_ref[i + 256 : i + 512, :], rows, NT)
        teach = jnp.max(jnp.maximum(low[:, :LIVE], high[:, :LIVE]), axis=0, keepdims=True)
        student = jnp.concatenate([low[:, LIVE:], high[:, LIVE:]], axis=0)
        now = jnp.max(student, axis=0, keepdims=True) * STUDENT_LOG2
        part = jnp.sum(jnp.exp2(student * STUDENT_LOG2 - now), axis=0, keepdims=True)
        if peak is None:
            peak, top, total = teach, now, part
        else:
            peak, both = jnp.maximum(peak, teach), jnp.maximum(top, now)
            total = total * jnp.exp2(top - both) + part * jnp.exp2(now - both)
            top = both
    tile = jnp.concatenate(
        thirds(peak * TEACHER_INV)
        + [jnp.broadcast_to(count, (1, LIVE))]
        + thirds(top / LOG2E + jnp.log(total))
        + [jnp.zeros((1, LIVE), f32)],
        axis=0,
    )
    out_ref[...] = jnp.broadcast_to(tile[None].astype(bf16), out_ref.shape)


def spread(tile, ref):
    ref[...] = jnp.broadcast_to(tile[None].astype(ref.dtype), ref.shape)


def order_kernel(recv_ref, a_ref, b_ref, c_ref, d_ref, teach_ref, student_ref):
    for k, piece in enumerate((a_ref, b_ref, c_ref, d_ref)):
        x = (lax.axis_index("x") + 4 - k) & 3
        teach_ref[x] = piece[0]
        student_ref[x] = piece[1]


def expo_half(rows_ref, mine_ref, et_ref, peak, live, sums):
    for r in range(2):
        at = slice(256 * r, 256 * (r + 1))
        rows = rows_ref[2 * r : 2 * r + 2].reshape(256, 256)
        weights = jnp.broadcast_to(live[:, at], (16, 256)).astype(bf16)
        for j in range(2):
            logits = dot(mine_ref[512 * j : 512 * (j + 1), :], rows, NT)
            block = jnp.exp2(logits * TEACHER_LOG2 - peak[:, at]).astype(bf16)
            et_ref[512 * j : 512 * (j + 1), at] = block
            sums[j] += dot(weights, block, NT)


def expo_own_kernel(recv_ref, rows_ref, mine_ref, et_ref, stat_ref, sum_ref):
    peaks, counts = [], []
    for x in range(4):
        for core in range(2):
            got = [recv_ref[(x * 4 + y) * 2 + core].astype(f32) for y in range(4)]
            tops = [v[0:1] + v[1:2] + v[2:3] for v in got]
            peaks.append(jnp.maximum(jnp.maximum(tops[0], tops[1]), jnp.maximum(tops[2], tops[3])))
            counts.append(got[0][3:4])
    peak = jnp.concatenate(peaks, axis=0)
    count = jnp.concatenate(counts, axis=0)
    slot = lax.broadcasted_iota(jnp.int32, (8, 128), 1).astype(f32)
    live = jnp.where(slot < count, 1.0, 0.0)
    stat_ref[0] = live
    stat_ref[1] = live / count
    stat_ref[2] = peak
    sums = [jnp.zeros((16, 512), f32)] * 2
    expo_half(rows_ref, mine_ref, et_ref, halves(peak * LOG2E)[0], halves(live)[0], sums)
    sum_ref[...] = jnp.concatenate(sums, axis=1)


def expo_other_kernel(stat_ref, sum_ref, rows_ref, mine_ref, et_ref, pay_ref):
    sums = [sum_ref[:, 0:512], sum_ref[:, 512:1024]]
    expo_half(rows_ref, mine_ref, et_ref, halves(stat_ref[2] * LOG2E)[1], halves(stat_ref[0])[1], sums)
    spread(to_tile(jnp.concatenate(sums, axis=1)[0:1]), pay_ref)


def over_columns(lhs, own_ref, other_ref):
    parts = [jnp.sum(dot(lhs, ref[...], NN), axis=0, keepdims=True) for ref in (own_ref, other_ref)]
    return join(*parts)


def col_kernel(recv_ref, own_ref, other_ref, *refs):
    col = 1.0 / jnp.sum(recv_ref[...].astype(f32), axis=0)
    spread(over_columns(split3(to_lanes(col)), own_ref, other_ref), refs[-1])


def last_col_kernel(recv_ref, own_ref, other_ref, w_ref, pay_ref, col_ref):
    col = 1.0 / jnp.sum(recv_ref[...].astype(f32), axis=0)
    col_ref[...] = col
    lhs = split3(to_lanes(col))
    out = over_columns(lhs, own_ref, other_ref)
    entropy = jnp.sum(dot(lhs, w_ref[...], NN), axis=0, keepdims=True)
    spread(jnp.concatenate([out, join(entropy[:, :512], entropy[:, 512:]), col], axis=0), pay_ref)


def row_kernel(recv_ref, stat_ref, own_ref, other_ref, pay_ref):
    row = stat_ref[0] / jnp.sum(recv_ref[...].astype(f32), axis=0)
    parts = [dot(split3(v), ref[...], NT) for v, ref in zip(halves(row), (own_ref, other_ref))]
    spread(to_tile(jnp.sum(parts[0] + parts[1], axis=0, keepdims=True)), pay_ref)


def student_prob_kernel(
    recv_ref, stat_ref, sown_ref, sother_ref, mine_ref, own_ref, other_ref, prob_ref, w_ref, norm_ref
):
    for image in range(8):
        got = [recv_ref[(image // 2 * 4 + y) * 2 + image % 2].astype(f32) for y in range(4)]
        parts = [v[4:5] + v[5:6] + v[6:7] for v in got]
        top = jnp.maximum(jnp.maximum(parts[0], parts[1]), jnp.maximum(parts[2], parts[3]))
        total = sum(jnp.exp(v - top) for v in parts)
        norm_ref[image : image + 1, :] = top + jnp.log(total)
    norm = jnp.concatenate(halves(norm_ref[...]), axis=1)
    coef = jnp.concatenate(halves(stat_ref[1]), axis=1) * GRAD_FACTOR
    for r in range(4):
        at = slice(256 * r, 256 * (r + 1))
        rows_ref, et_ref = ((sown_ref, own_ref), (sother_ref, other_ref))[r // 2]
        rows = rows_ref[2 * (r % 2) : 2 * (r % 2) + 2].reshape(256, 256)
        here = slice(256 * (r % 2), 256 * (r % 2) + 256)
        for j in (slice(0, 512), slice(512, 1024)):
            log_prob = dot(mine_ref[j, :], rows, NT) * STUDENT_INV - norm[:, at]
            prob_ref[j, at] = jnp.exp(log_prob) * coef[:, at]
            w_ref[j, at] = (et_ref[j, here].astype(f32) * log_prob).astype(bf16)


def grad_kernel(
    recv_ref, stat_ref, col_ref, own_ref, other_ref, prob_ref, sown_ref, sother_ref, pout_hbm, scale_ref, pout_ref, sems
):
    sums = jnp.sum(recv_ref[...].astype(f32), axis=0)
    entropy = sums[8:16]
    row = stat_ref[0] / sums[0:8]
    weight = stat_ref[1]
    loss = -jnp.sum(jnp.sum(weight * row * entropy, axis=1, keepdims=True), axis=0, keepdims=True) / IMAGES
    hi = loss.astype(bf16).astype(f32)
    mid = (loss - hi).astype(bf16).astype(f32)
    lo = loss - hi - mid
    which = lax.broadcasted_iota(jnp.int32, (8, 128), 0)
    tail = jnp.where(which == 0, hi, jnp.where(which == 1, mid, jnp.where(which == 2, lo, 0.0))).astype(bf16)
    coef = weight * GRAD_FACTOR
    scale_ref[0] = coef
    scale_ref[1] = coef * row
    scale_rows = jnp.concatenate(halves(coef * row), axis=1)
    sown, sother = sown_ref[...].reshape(512, 256), sother_ref[...].reshape(512, 256)
    copies = []
    for j in range(4):
        at = slice(256 * j, 256 * (j + 1))
        col = jnp.concatenate([jnp.broadcast_to(col_ref[i : i + 1, :], (128, 128)).T for i in (2 * j, 2 * j + 1)], axis=0)
        col = jnp.concatenate([col] * 8, axis=1)
        teach = jnp.concatenate([own_ref[at, :], other_ref[at, :]], axis=1).astype(f32)
        grad = (prob_ref[at, :] - teach * col * scale_rows).astype(bf16)
        part = (dot(grad[:, :512], sown, NN) + dot(grad[:, 512:], sother, NN)).astype(bf16)
        for i in (0, 1):
            pout_ref[2 * j + i, 0:128, :] = part[128 * i : 128 * (i + 1), 0:128]
            pout_ref[2 * j + i, 128:256, :] = part[128 * i : 128 * (i + 1), 128:256]
            pout_ref[2 * j + i, 256:264, :] = tail
        if j % 2:
            at = pl.ds(2 * j - 2, 4)
            copies.append(pltpu.make_async_copy(pout_ref.at[at], pout_hbm.at[at], sems.at[j // 2]))
            copies[-1].start()
    for copy in copies:
        copy.wait()


def column(row, wide):
    return jnp.concatenate([jnp.broadcast_to(row, (128, 128)).T] * (wide // 128), axis=1)


def own_image():
    return pl.ds(lax.axis_index("x") * 2 + lax.axis_index("c"), 1)


def own_kernel(recv_ref, scale_ref, stat_ref, norm_ref, rows_hbm, proto_hbm, out_ref, rows_ref, proto_ref, sems):
    chunks = 2
    tall = proto_ref.shape[0] // chunks
    rows_copy = pltpu.make_async_copy(rows_hbm, rows_ref, sems.at[chunks])
    copies = [
        pltpu.make_async_copy(proto_hbm.at[pl.ds(i * tall, tall)], proto_ref.at[pl.ds(i * tall, tall)], sems.at[i])
        for i in range(chunks)
    ]
    for copy in [rows_copy] + copies:
        copy.start()
    y = lax.axis_index("y")
    peak = column(stat_ref[2, own_image(), :] * LOG2E, 1024)
    norm = column(norm_ref[own_image(), :] * LOG2E, 1024)
    coef = column(scale_ref[0, own_image(), :], 1024)
    scale = column(scale_ref[1, own_image(), :], 1024)
    cols = [recv_ref[(x * 4 + y) * 2 + c].astype(f32)[16:24] for x in range(4) for c in range(2)]
    rows_copy.wait()
    rows = rows_ref[...].reshape(2 * LIVE, 256)
    total = jnp.zeros((LIVE, 256), f32)
    for i in range(8):
        if i % 4 == 0:
            copies[i // 4].wait()
        col = jnp.concatenate([v[i : i + 1, :] for v in cols], axis=1)
        block = proto_ref[1024 * i : 1024 * (i + 1), :]
        logits = dot(rows, block, NT)
        teach = jnp.exp2(logits[0:LIVE] * TEACHER_LOG2 - peak).astype(bf16).astype(f32)
        prob = jnp.exp2(logits[LIVE:] * STUDENT_LOG2 - norm)
        grad = (prob * coef - teach * (col * scale)).astype(bf16)
        total += dot(grad, block, NN)
    out_ref[...] = total.astype(bf16)


def place_kernel(mask_ref, a_ref, b_ref, c_ref, d_ref, student_ref):
    pick = selection(mask_ref[...]).astype(bf16)
    parts = [ref[...].astype(f32) for ref in (a_ref, b_ref, c_ref, d_ref)]
    rows = (parts[0] + parts[2]) + (parts[1] + parts[3])
    student_ref[...] = sum(dot(pick, part.astype(bf16), TN) for part in thirds(rows))


def end_kernel(recv_ref, proto_ref, loss_ref):
    total = jnp.sum(recv_ref[...].astype(f32), axis=0)
    proto_ref[:, 0:128] = total[0:128]
    proto_ref[:, 128:256] = total[128:256]
    loss_ref[...] = total[256:257] + total[257:258] + total[258:259]


VM = pl.BlockSpec(memory_space=pltpu.VMEM)


def call(kernel, out, *args, scratch=(), limit=8, cost=None):
    out = [jax.ShapeDtypeStruct(s, d) for s, d in out]
    return pl.pallas_call(
        kernel,
        out_shape=out,
        in_specs=[VM] * len(args),
        out_specs=[VM] * len(out),
        scratch_shapes=list(scratch),
        compiler_params=pltpu.CompilerParams(vmem_limit_bytes=limit << 20),
        cost_estimate=cost and pl.CostEstimate(flops=cost, bytes_accessed=1 << 20, transcendentals=1 << 20),
    )(*args)


def in_hbm(v):
    return pltpu.with_memory_space_constraint(v, pltpu.HBM)


def a2a(v, axes):
    return lax.all_to_all(v, axes, 0, 0, tiled=True)


def shift(v, axis, n, k):
    return lax.ppermute(v, axis, [(i, (i + k) % n) for i in range(n)])


PLANE = ("x", "y", "c")
HBM = pl.BlockSpec(memory_space=pl.ANY)


def local(teacher_feats, student_feats, prototypes, patch_mask):
    own, peak_pay, mine = pl.pallas_call(
        head_kernel,
        out_shape=[
            jax.ShapeDtypeStruct((2, LIVE, 256), bf16),
            jax.ShapeDtypeStruct((32, 8, 128), bf16),
            jax.ShapeDtypeStruct((1024, 256), bf16),
        ],
        in_specs=[HBM] * 4,
        out_specs=[VM] * 3,
        scratch_shapes=[
            pltpu.VMEM((1, 256), jnp.int32),
            pltpu.VMEM((1, 256, 256), bf16),
            pltpu.VMEM((1, 256, 256), bf16),
            pltpu.VMEM((8192, 256), bf16),
            pltpu.SemaphoreType.DMA((5,)),
        ],
        compiler_params=pltpu.CompilerParams(vmem_limit_bytes=32 << 20),
    )(*(in_hbm(v) for v in (patch_mask, teacher_feats, student_feats, prototypes)))

    parts = [own] + [shift(own, "x", 4, k) for k in (1, 2, 3)]
    peak_recv = a2a(peak_pay, PLANE)
    teach_own, student_own = call(order_kernel, [((4, LIVE, 256), bf16)] * 2, peak_recv, *parts)
    teach_other, student_other = shift(teach_own, "c", 2, 1), shift(student_own, "c", 2, 1)
    et_own, stat, sums = call(
        expo_own_kernel,
        [((1024, 512), bf16), ((3, 8, 128), f32), ((16, 1024), f32)],
        peak_recv, teach_own, mine, limit=16, cost=1 << 28,
    )
    et_other, pay = call(
        expo_other_kernel, [((1024, 512), bf16), ((8, 8, 128), bf16)], stat, sums, teach_other, mine, limit=16
    )
    et = (et_own, et_other)

    recv = a2a(pay, "z")
    (pay,) = call(col_kernel, [((32, 8, 128), bf16)], recv, *et)
    recv = a2a(pay, PLANE)
    recv, stat2 = lax.optimization_barrier((recv, stat))
    prob, w, norm = call(
        student_prob_kernel, [((1024, 1024), f32), ((1024, 1024), bf16), ((8, 128), f32)],
        peak_recv, stat2, student_own, student_other, mine, *et, limit=24,
    )
    (pay,) = call(row_kernel, [((8, 8, 128), bf16)], recv, stat, *et)
    pay, prob, w, norm = lax.optimization_barrier((pay, prob, w, norm))
    for _ in range(BALANCING_PASSES - 2):
        recv = a2a(pay, "z")
        (pay,) = call(col_kernel, [((32, 8, 128), bf16)], recv, *et)
        recv = a2a(pay, PLANE)
        (pay,) = call(row_kernel, [((8, 8, 128), bf16)], recv, stat, *et)
    recv = a2a(pay, "z")
    pay, col = call(last_col_kernel, [((32, 24, 128), bf16), ((8, 128), f32)], recv, *et, w)
    recv = a2a(pay, PLANE)

    proto_part, scale = pl.pallas_call(
        grad_kernel,
        out_shape=[pltpu.HBM((8, 264, 128), bf16), jax.ShapeDtypeStruct((2, 8, 128), f32)],
        in_specs=[VM] * 8,
        out_specs=[pl.BlockSpec(memory_space=pltpu.HBM), VM],
        scratch_shapes=[pltpu.VMEM((8, 264, 128), bf16), pltpu.SemaphoreType.DMA((2,))],
        compiler_params=pltpu.CompilerParams(vmem_limit_bytes=24 << 20),
    )(recv, stat, col, *et, prob, student_own, student_other)
    proto_recv = a2a(proto_part, "z")
    student_rows = pl.pallas_call(
        own_kernel,
        out_shape=jax.ShapeDtypeStruct((LIVE, 256), bf16),
        in_specs=[VM] * 4 + [HBM] * 2,
        out_specs=VM,
        scratch_shapes=[
            pltpu.VMEM((2, LIVE, 256), bf16),
            pltpu.VMEM((8192, 256), bf16),
            pltpu.SemaphoreType.DMA((3,)),
        ],
        compiler_params=pltpu.CompilerParams(vmem_limit_bytes=24 << 20),
        cost_estimate=pl.CostEstimate(flops=1 << 31, bytes_accessed=4 << 20, transcendentals=2 << 20),
    )(recv, scale, stat, norm, in_hbm(own), in_hbm(prototypes))
    student_rows = [student_rows] + [shift(student_rows, "y", 4, k) for k in (1, 2, 3)]
    (student,) = call(place_kernel, [((256, 256), f32)], patch_mask, *student_rows, limit=16)
    proto, loss = call(end_kernel, [((128, 256), f32), ((1, 128), f32)], proto_recv, limit=16)
    return loss[0, 0], student[None], proto[None]


def solution(mesh):
    fine = Mesh(mesh.devices.reshape(8, 4, 2, 4), ("z", "x", "c", "y"))
    dp = ("z", "x", "c")
    return jax.shard_map(
        local,
        mesh=fine,
        in_specs=(P(dp, None, None), P(dp, None, None), P("y", None), P(dp, None)),
        out_specs=(P(), P(dp, None, None), P("y", dp, None)),
        check_vma=False,
    )
```

```python
import jax
import jax.numpy as jnp
from jax import lax
from jax.experimental import pallas as pl
from jax.experimental.pallas import tpu as pltpu
from jax.sharding import Mesh, PartitionSpec as P

BALANCING_PASSES = 3
LOSS_SCALE = 16384
TEACHER_INV = 1.0 / 0.07
STUDENT_INV = 1.0 / 0.1
IMAGES = 64
GRAD_FACTOR = LOSS_SCALE / (IMAGES * 0.1)
LIVE = 128
NT = (((1,), (1,)), ((), ()))
NN = (((1,), (0,)), ((), ()))
TN = (((0,), (0,)), ((), ()))
f32 = jnp.float32
bf16 = jnp.bfloat16


def dot(a, b, dims):
    return lax.dot_general(a, b, dims, preferred_element_type=f32)


def to_lanes(v):
    return jnp.concatenate([v[i : i + 1, :] for i in range(8)], axis=1)


def to_tile(v):
    return jnp.concatenate([v[:, 128 * i : 128 * (i + 1)] for i in range(8)], axis=0)


def halves(tile):
    even, odd = (jnp.concatenate([tile[i : i + 1] for i in range(start, 8, 2)], axis=1) for start in (0, 1))
    first = lax.axis_index("c") == 0
    return jnp.where(first, even, odd), jnp.where(first, odd, even)


def join(own, other):
    first = lax.axis_index("c") == 0
    even, odd = jnp.where(first, own, other), jnp.where(first, other, own)
    return jnp.concatenate([v[:, 128 * x : 128 * (x + 1)] for x in range(4) for v in (even, odd)], axis=0)


def thirds(v):
    hi = v.astype(bf16).astype(f32)
    mid = (v - hi).astype(bf16).astype(f32)
    return [hi, mid, (v - hi - mid).astype(bf16).astype(f32)]


def split3(v):
    return jnp.concatenate(thirds(v) + [jnp.zeros((13, v.shape[1]), f32)], axis=0).astype(bf16)


def selection(mask):
    patches = mask.shape[1]
    maskf = mask.astype(f32)
    before = lax.broadcasted_iota(jnp.int32, (patches, patches), 0)
    after = lax.broadcasted_iota(jnp.int32, (patches, patches), 1)
    tri = jnp.where(before <= after, 1.0, 0.0).astype(bf16)
    rank = dot(jnp.broadcast_to(maskf, (16, patches)).astype(bf16), tri, NN)[0:1, :]
    slot = lax.broadcasted_iota(jnp.int32, (LIVE, patches), 0).astype(f32)
    hit = jnp.where(rank - 1.0 == slot, 1.0, 0.0) * maskf
    return hit


def head_kernel(
    mask_hbm, teach_hbm, student_hbm, proto_hbm, own_ref, out_ref, mine_ref, mask_ref, teach_ref, student_ref, proto_ref, sems
):
    chunks = 2
    tall = proto_ref.shape[0] // chunks
    small = ((mask_hbm, mask_ref), (teach_hbm, teach_ref), (student_hbm, student_ref))
    first = [pltpu.make_async_copy(src, dst, sems.at[chunks + i]) for i, (src, dst) in enumerate(small)]
    copies = [
        pltpu.make_async_copy(proto_hbm.at[pl.ds(i * tall, tall)], proto_ref.at[pl.ds(i * tall, tall)], sems.at[i])
        for i in range(chunks)
    ]
    for copy in first + copies:
        copy.start()
    image = lax.axis_index("x") * 2 + lax.axis_index("c")
    first[0].wait()
    pick = selection(mask_ref[...]).astype(bf16)
    count = jnp.sum(mask_ref[...].astype(f32), axis=1, keepdims=True)
    first[1].wait()
    own_ref[0] = dot(pick, teach_ref[0], NN).astype(bf16)
    first[2].wait()
    own_ref[1] = dot(pick, student_ref[0], NN).astype(bf16)
    rows = own_ref[...].reshape(2 * LIVE, 256)
    peak = top = total = None
    for i in range(0, 8192, 512):
        if i % tall == 0:
            copies[i // tall].wait()
        if i % 1024 == 0:
            at = pl.multiple_of(i + image * 128, 128)
            mine_ref[i // 8 : i // 8 + 128, :] = proto_ref[pl.ds(at, 128), :]
        low = dot(proto_ref[i : i + 256, :], rows, NT)
        high = dot(proto_ref[i + 256 : i + 512, :], rows, NT)
        teach = jnp.max(jnp.maximum(low[:, :LIVE], high[:, :LIVE]), axis=0, keepdims=True)
        student = jnp.concatenate([low[:, LIVE:], high[:, LIVE:]], axis=0) * STUDENT_INV
        now = jnp.max(student, axis=0, keepdims=True)
        part = jnp.sum(jnp.exp(student - now), axis=0, keepdims=True)
        if peak is None:
            peak, top, total = teach, now, part
        else:
            peak, both = jnp.maximum(peak, teach), jnp.maximum(top, now)
            total = total * jnp.exp(top - both) + part * jnp.exp(now - both)
            top = both
    tile = jnp.concatenate(
        thirds(peak * TEACHER_INV)
        + [jnp.broadcast_to(count, (1, LIVE))]
        + thirds(top + jnp.log(total))
        + [jnp.zeros((1, LIVE), f32)],
        axis=0,
    )
    out_ref[...] = jnp.broadcast_to(tile[None].astype(bf16), out_ref.shape)


def spread(tile, ref):
    ref[...] = jnp.broadcast_to(tile[None].astype(ref.dtype), ref.shape)


def order_kernel(recv_ref, a_ref, b_ref, c_ref, d_ref, teach_ref, student_ref):
    for k, piece in enumerate((a_ref, b_ref, c_ref, d_ref)):
        x = (lax.axis_index("x") + 4 - k) & 3
        teach_ref[x] = piece[0]
        student_ref[x] = piece[1]


def expo_half(rows_ref, mine_ref, et_ref, peak, live, sums):
    for r in range(2):
        at = slice(256 * r, 256 * (r + 1))
        rows = rows_ref[2 * r : 2 * r + 2].reshape(256, 256)
        weights = jnp.broadcast_to(live[:, at], (16, 256)).astype(bf16)
        for j in range(2):
            logits = dot(mine_ref[512 * j : 512 * (j + 1), :], rows, NT)
            block = jnp.exp(logits * TEACHER_INV - peak[:, at]).astype(bf16)
            et_ref[512 * j : 512 * (j + 1), at] = block
            sums[j] += dot(weights, block, NT)


def expo_own_kernel(recv_ref, rows_ref, mine_ref, et_ref, stat_ref, sum_ref):
    peaks, counts = [], []
    for x in range(4):
        for core in range(2):
            got = [recv_ref[(x * 4 + y) * 2 + core].astype(f32) for y in range(4)]
            tops = [v[0:1] + v[1:2] + v[2:3] for v in got]
            peaks.append(jnp.maximum(jnp.maximum(tops[0], tops[1]), jnp.maximum(tops[2], tops[3])))
            counts.append(got[0][3:4])
    peak = jnp.concatenate(peaks, axis=0)
    count = jnp.concatenate(counts, axis=0)
    slot = lax.broadcasted_iota(jnp.int32, (8, 128), 1).astype(f32)
    live = jnp.where(slot < count, 1.0, 0.0)
    stat_ref[0] = live
    stat_ref[1] = live / count
    stat_ref[2] = peak
    sums = [jnp.zeros((16, 512), f32)] * 2
    expo_half(rows_ref, mine_ref, et_ref, halves(peak)[0], halves(live)[0], sums)
    sum_ref[...] = jnp.concatenate(sums, axis=1)


def expo_other_kernel(stat_ref, sum_ref, rows_ref, mine_ref, et_ref, pay_ref):
    sums = [sum_ref[:, 0:512], sum_ref[:, 512:1024]]
    expo_half(rows_ref, mine_ref, et_ref, halves(stat_ref[2])[1], halves(stat_ref[0])[1], sums)
    spread(to_tile(jnp.concatenate(sums, axis=1)[0:1]), pay_ref)


def over_columns(lhs, own_ref, other_ref):
    parts = [jnp.sum(dot(lhs, ref[...], NN), axis=0, keepdims=True) for ref in (own_ref, other_ref)]
    return join(*parts)


def col_kernel(recv_ref, own_ref, other_ref, *refs):
    col = 1.0 / jnp.sum(recv_ref[...].astype(f32), axis=0)
    spread(over_columns(split3(to_lanes(col)), own_ref, other_ref), refs[-1])


def last_col_kernel(recv_ref, own_ref, other_ref, w_ref, pay_ref, col_ref):
    col = 1.0 / jnp.sum(recv_ref[...].astype(f32), axis=0)
    col_ref[...] = col
    lhs = split3(to_lanes(col))
    out = over_columns(lhs, own_ref, other_ref)
    entropy = jnp.sum(dot(lhs, w_ref[...], NN), axis=0, keepdims=True)
    spread(jnp.concatenate([out, join(entropy[:, :512], entropy[:, 512:]), col], axis=0), pay_ref)


def row_kernel(recv_ref, stat_ref, own_ref, other_ref, pay_ref):
    row = stat_ref[0] / jnp.sum(recv_ref[...].astype(f32), axis=0)
    parts = [dot(split3(v), ref[...], NT) for v, ref in zip(halves(row), (own_ref, other_ref))]
    spread(to_tile(jnp.sum(parts[0] + parts[1], axis=0, keepdims=True)), pay_ref)


def student_prob_kernel(
    recv_ref, stat_ref, sown_ref, sother_ref, mine_ref, own_ref, other_ref, prob_ref, w_ref, norm_ref
):
    for image in range(8):
        got = [recv_ref[(image // 2 * 4 + y) * 2 + image % 2].astype(f32) for y in range(4)]
        parts = [v[4:5] + v[5:6] + v[6:7] for v in got]
        top = jnp.maximum(jnp.maximum(parts[0], parts[1]), jnp.maximum(parts[2], parts[3]))
        total = sum(jnp.exp(v - top) for v in parts)
        norm_ref[image : image + 1, :] = top + jnp.log(total)
    norm = jnp.concatenate(halves(norm_ref[...]), axis=1)
    coef = jnp.concatenate(halves(stat_ref[1]), axis=1) * GRAD_FACTOR
    for r in range(4):
        at = slice(256 * r, 256 * (r + 1))
        rows_ref, et_ref = ((sown_ref, own_ref), (sother_ref, other_ref))[r // 2]
        rows = rows_ref[2 * (r % 2) : 2 * (r % 2) + 2].reshape(256, 256)
        log_prob = dot(mine_ref[...], rows, NT) * STUDENT_INV - norm[:, at]
        prob_ref[:, at] = jnp.exp(log_prob) * coef[:, at]
        here = slice(256 * (r % 2), 256 * (r % 2) + 256)
        w_ref[:, at] = (et_ref[:, here].astype(f32) * log_prob).astype(bf16)


def grad_kernel(
    recv_ref, stat_ref, col_ref, own_ref, other_ref, prob_ref, sown_ref, sother_ref, pout_hbm, scale_ref, pout_ref, sems
):
    sums = jnp.sum(recv_ref[...].astype(f32), axis=0)
    entropy = sums[8:16]
    row = stat_ref[0] / sums[0:8]
    weight = stat_ref[1]
    loss = -jnp.sum(jnp.sum(weight * row * entropy, axis=1, keepdims=True), axis=0, keepdims=True) / IMAGES
    hi = loss.astype(bf16).astype(f32)
    mid = (loss - hi).astype(bf16).astype(f32)
    lo = loss - hi - mid
    which = lax.broadcasted_iota(jnp.int32, (8, 128), 0)
    tail = jnp.where(which == 0, hi, jnp.where(which == 1, mid, jnp.where(which == 2, lo, 0.0))).astype(bf16)
    coef = weight * GRAD_FACTOR
    scale_ref[0] = coef
    scale_ref[1] = coef * row
    scale_rows = jnp.concatenate(halves(coef * row), axis=1)
    sown, sother = sown_ref[...].reshape(512, 256), sother_ref[...].reshape(512, 256)
    copies = []
    for j in range(2):
        at = slice(512 * j, 512 * (j + 1))
        col = [jnp.broadcast_to(col_ref[i : i + 1, :], (128, 128)).T for i in range(4 * j, 4 * j + 4)]
        col = jnp.concatenate([jnp.concatenate(col, axis=0)] * 8, axis=1)
        teach = jnp.concatenate([own_ref[at, :], other_ref[at, :]], axis=1).astype(f32)
        grad = (prob_ref[at, :] - teach * col * scale_rows).astype(bf16)
        part = (dot(grad[:, :512], sown, NN) + dot(grad[:, 512:], sother, NN)).astype(bf16)
        for i in range(4):
            pout_ref[4 * j + i, 0:128, :] = part[128 * i : 128 * (i + 1), 0:128]
            pout_ref[4 * j + i, 128:256, :] = part[128 * i : 128 * (i + 1), 128:256]
            pout_ref[4 * j + i, 256:264, :] = tail
        at = pl.ds(4 * j, 4)
        copies.append(pltpu.make_async_copy(pout_ref.at[at], pout_hbm.at[at], sems.at[j]))
        copies[-1].start()
    for copy in copies:
        copy.wait()


def column(row, wide):
    return jnp.concatenate([jnp.broadcast_to(row, (128, 128)).T] * (wide // 128), axis=1)


def own_image():
    return pl.ds(lax.axis_index("x") * 2 + lax.axis_index("c"), 1)


def own_kernel(recv_ref, scale_ref, stat_ref, norm_ref, rows_hbm, proto_hbm, out_ref, rows_ref, proto_ref, sems):
    chunks = 2
    tall = proto_ref.shape[0] // chunks
    rows_copy = pltpu.make_async_copy(rows_hbm, rows_ref, sems.at[chunks])
    copies = [
        pltpu.make_async_copy(proto_hbm.at[pl.ds(i * tall, tall)], proto_ref.at[pl.ds(i * tall, tall)], sems.at[i])
        for i in range(chunks)
    ]
    for copy in [rows_copy] + copies:
        copy.start()
    y = lax.axis_index("y")
    peak = column(stat_ref[2, own_image(), :], 1024)
    norm = column(norm_ref[own_image(), :], 1024)
    coef = column(scale_ref[0, own_image(), :], 1024)
    scale = column(scale_ref[1, own_image(), :], 1024)
    cols = [recv_ref[(x * 4 + y) * 2 + c].astype(f32)[16:24] for x in range(4) for c in range(2)]
    rows_copy.wait()
    rows = rows_ref[...].reshape(2 * LIVE, 256)
    total = jnp.zeros((LIVE, 256), f32)
    for i in range(8):
        if i % 4 == 0:
            copies[i // 4].wait()
        col = jnp.concatenate([v[i : i + 1, :] for v in cols], axis=1)
        block = proto_ref[1024 * i : 1024 * (i + 1), :]
        logits = dot(rows, block, NT)
        teach = jnp.exp(logits[0:LIVE] * TEACHER_INV - peak).astype(bf16).astype(f32)
        prob = jnp.exp(logits[LIVE:] * STUDENT_INV - norm)
        grad = (prob * coef - teach * (col * scale)).astype(bf16)
        total += dot(grad, block, NN)
    out_ref[...] = total.astype(bf16)


def place_kernel(mask_ref, a_ref, b_ref, c_ref, d_ref, student_ref):
    pick = selection(mask_ref[...]).astype(bf16)
    parts = [ref[...].astype(f32) for ref in (a_ref, b_ref, c_ref, d_ref)]
    rows = (parts[0] + parts[2]) + (parts[1] + parts[3])
    student_ref[...] = sum(dot(pick, part.astype(bf16), TN) for part in thirds(rows))


def end_kernel(recv_ref, proto_ref, loss_ref):
    total = jnp.sum(recv_ref[...].astype(f32), axis=0)
    proto_ref[:, 0:128] = total[0:128]
    proto_ref[:, 128:256] = total[128:256]
    loss_ref[...] = total[256:257] + total[257:258] + total[258:259]


VM = pl.BlockSpec(memory_space=pltpu.VMEM)


def call(kernel, out, *args, scratch=(), limit=8, cost=None):
    out = [jax.ShapeDtypeStruct(s, d) for s, d in out]
    return pl.pallas_call(
        kernel,
        out_shape=out,
        in_specs=[VM] * len(args),
        out_specs=[VM] * len(out),
        scratch_shapes=list(scratch),
        compiler_params=pltpu.CompilerParams(vmem_limit_bytes=limit << 20),
        cost_estimate=cost and pl.CostEstimate(flops=cost, bytes_accessed=1 << 20, transcendentals=1 << 20),
    )(*args)


def in_hbm(v):
    return pltpu.with_memory_space_constraint(v, pltpu.HBM)


def a2a(v, axes):
    return lax.all_to_all(v, axes, 0, 0, tiled=True)


def shift(v, axis, n, k):
    return lax.ppermute(v, axis, [(i, (i + k) % n) for i in range(n)])


PLANE = ("x", "y", "c")
HBM = pl.BlockSpec(memory_space=pl.ANY)


def local(teacher_feats, student_feats, prototypes, patch_mask):
    own, peak_pay, mine = pl.pallas_call(
        head_kernel,
        out_shape=[
            jax.ShapeDtypeStruct((2, LIVE, 256), bf16),
            jax.ShapeDtypeStruct((32, 8, 128), bf16),
            jax.ShapeDtypeStruct((1024, 256), bf16),
        ],
        in_specs=[HBM] * 4,
        out_specs=[VM] * 3,
        scratch_shapes=[
            pltpu.VMEM((1, 256), jnp.int32),
            pltpu.VMEM((1, 256, 256), bf16),
            pltpu.VMEM((1, 256, 256), bf16),
            pltpu.VMEM((8192, 256), bf16),
            pltpu.SemaphoreType.DMA((5,)),
        ],
        compiler_params=pltpu.CompilerParams(vmem_limit_bytes=32 << 20),
    )(*(in_hbm(v) for v in (patch_mask, teacher_feats, student_feats, prototypes)))

    parts = [own] + [shift(own, "x", 4, k) for k in (1, 2, 3)]
    peak_recv = a2a(peak_pay, PLANE)
    teach_own, student_own = call(order_kernel, [((4, LIVE, 256), bf16)] * 2, peak_recv, *parts)
    teach_other, student_other = shift(teach_own, "c", 2, 1), shift(student_own, "c", 2, 1)
    et_own, stat, sums = call(
        expo_own_kernel,
        [((1024, 512), bf16), ((3, 8, 128), f32), ((16, 1024), f32)],
        peak_recv, teach_own, mine, limit=16, cost=1 << 28,
    )
    et_other, pay = call(
        expo_other_kernel, [((1024, 512), bf16), ((8, 8, 128), bf16)], stat, sums, teach_other, mine, limit=16
    )
    et = (et_own, et_other)

    recv = a2a(pay, "z")
    (pay,) = call(col_kernel, [((32, 8, 128), bf16)], recv, *et)
    recv = a2a(pay, PLANE)
    recv, stat2 = lax.optimization_barrier((recv, stat))
    prob, w, norm = call(
        student_prob_kernel, [((1024, 1024), f32), ((1024, 1024), bf16), ((8, 128), f32)],
        peak_recv, stat2, student_own, student_other, mine, *et, limit=24,
    )
    (pay,) = call(row_kernel, [((8, 8, 128), bf16)], recv, stat, *et)
    pay, prob, w, norm = lax.optimization_barrier((pay, prob, w, norm))
    for _ in range(BALANCING_PASSES - 2):
        recv = a2a(pay, "z")
        (pay,) = call(col_kernel, [((32, 8, 128), bf16)], recv, *et)
        recv = a2a(pay, PLANE)
        (pay,) = call(row_kernel, [((8, 8, 128), bf16)], recv, stat, *et)
    recv = a2a(pay, "z")
    pay, col = call(last_col_kernel, [((32, 24, 128), bf16), ((8, 128), f32)], recv, *et, w)
    recv = a2a(pay, PLANE)

    proto_part, scale = pl.pallas_call(
        grad_kernel,
        out_shape=[pltpu.HBM((8, 264, 128), bf16), jax.ShapeDtypeStruct((2, 8, 128), f32)],
        in_specs=[VM] * 8,
        out_specs=[pl.BlockSpec(memory_space=pltpu.HBM), VM],
        scratch_shapes=[pltpu.VMEM((8, 264, 128), bf16), pltpu.SemaphoreType.DMA((2,))],
        compiler_params=pltpu.CompilerParams(vmem_limit_bytes=24 << 20),
    )(recv, stat, col, *et, prob, student_own, student_other)
    proto_recv = a2a(proto_part, "z")
    student_rows = pl.pallas_call(
        own_kernel,
        out_shape=jax.ShapeDtypeStruct((LIVE, 256), bf16),
        in_specs=[VM] * 4 + [HBM] * 2,
        out_specs=VM,
        scratch_shapes=[
            pltpu.VMEM((2, LIVE, 256), bf16),
            pltpu.VMEM((8192, 256), bf16),
            pltpu.SemaphoreType.DMA((3,)),
        ],
        compiler_params=pltpu.CompilerParams(vmem_limit_bytes=24 << 20),
        cost_estimate=pl.CostEstimate(flops=1 << 31, bytes_accessed=4 << 20, transcendentals=2 << 20),
    )(recv, scale, stat, norm, in_hbm(own), in_hbm(prototypes))
    student_rows = [student_rows] + [shift(student_rows, "y", 4, k) for k in (1, 2, 3)]
    (student,) = call(place_kernel, [((256, 256), f32)], patch_mask, *student_rows, limit=16)
    proto, loss = call(end_kernel, [((128, 256), f32), ((1, 128), f32)], proto_recv, limit=16)
    return loss[0, 0], student[None], proto[None]


def solution(mesh):
    fine = Mesh(mesh.devices.reshape(8, 4, 2, 4), ("z", "x", "c", "y"))
    dp = ("z", "x", "c")
    return jax.shard_map(
        local,
        mesh=fine,
        in_specs=(P(dp, None, None), P(dp, None, None), P("y", None), P(dp, None)),
        out_specs=(P(), P(dp, None, None), P("y", dp, None)),
        check_vma=False,
    )
```
